32 devices in a mesh: blk: 8 (over z, x), grp: 4 (over y, core).
Axes of the slice: x: 2, y: 2, z: 4, core: 2. Of those that a mesh axis runs over, the one named last changes fastest.
Arguments:
- amplitudes: bfloat16 [1920, 1920], P('blk'), may hold values from -6 to 6
- hole_panel: bfloat16 [1920, 8, 1920], P(None, 'blk', 'grp'), may hold values from -0.375 to 0.375
- virt_fock: bfloat16 [1920, 1920], replicated, may hold values from -0.125 to 0.125
- irrep_sizes: int32 [8], replicated, may hold values from 1 to 480, 1920 in all
- pair_irreps: int32 [8], P('blk'), may hold values from 0 to 7
Outputs:
- dressed: bfloat16 [1920, 8, 1920], P('grp', 'blk')
The draws below stay inside these ranges and needn't reach their ends.
Inputs may be any that keep to these rules, and one draw needn't show every extreme that they name: `irrep_sizes`: the 8 entries sum to 1920.
All inputs are finite; a program needn't handle non-finite values.
Results may differ from the reference program's by a relative error of at most 0.0049.
Values may be sent and summed in bfloat16 or wider, within the bound.
No kernel may reach another device: no remote copies, remote signals or barrier semaphores. Data moves between devices by JAX's collectives and lax.ppermute only.
A program may use at most 128 MiB of HBM per device.

```python
import math
import jax
import jax.numpy as jnp
import numpy as np
from jax import lax

NVIR = 1920
NIRREP = 8
OCC_SLAB = 8


def with_ends(values, key, least, top_value):
    longest = values.shape.index(max(values.shape))
    spots = []
    for shift in (0, 1):
        where = [jax.random.randint(jax.random.fold_in(key, axis), (), 0, length) for axis, length in enumerate(values.shape)]
        where[longest] = (where[longest] + shift) % values.shape[longest]
        spots.append(tuple(where))
    return values.at[spots[0]].set(least).at[spots[1]].set(top_value)


def block_scale(rng, dims, pieces, low, largest):
    loudness, own = 1.0, jax.random.fold_in(rng, 6)
    for position, shards_of in pieces:
        steps = jnp.exp(jax.random.uniform(jax.random.fold_in(own, position), (shards_of,), jnp.float32, low / len(pieces), largest / len(pieces)))
        loudness = loudness * jnp.repeat(steps, dims[position] // shards_of).reshape([-1 if axis == position else 1 for axis in range(len(dims))])
    return loudness


def length_profile(number_of, total, limit, lean):
    weights = [(1 << 20) // math.isqrt(rank ** lean) + 1 for rank in range(2, number_of + 1)]
    spare, counts = total - limit - (number_of - 1), [1] * (number_of - 1)
    while spare > 0:
        candidates = [i for i in range(number_of - 1) if counts[i] < limit]
        mass, left = sum([weights[i] for i in candidates]), spare
        for i in candidates:
            more = min(limit - counts[i], max(1, left * weights[i] // mass), spare)
            counts[i] = counts[i] + more
            spare = spare - more
    return np.array([limit] + counts)


def ragged_sizes(stream_key, count, total, bound, skew):
    if count == 2:
        one = jax.random.randint(stream_key, (), max(1, total - bound), min(bound, total - 1) + 1)
        return jnp.stack([one, total - one])
    tallies = jnp.asarray(length_profile(count, total, bound, skew), jnp.int32)
    pairs = (count - 1) // 2
    source_of, taker = tallies[1:1 + 2 * pairs:2], tallies[2:2 + 2 * pairs:2]
    slack = jnp.minimum(source_of - 1, bound - taker)
    shifted = jax.random.randint(jax.random.fold_in(stream_key, 1), (pairs,), 0, 1 << 20) % (slack + 1)
    tallies = tallies.at[1:1 + 2 * pairs:2].set(source_of - shifted).at[2:2 + 2 * pairs:2].set(taker + shifted)
    return tallies[jax.random.permutation(jax.random.fold_in(stream_key, 2), count)]


def normal_values(key, dims, scale, bound, cuts=(), kind=jnp.bfloat16):
    factor_of = block_scale(key, dims, cuts, -0.22, 0.18) if cuts else 1.0
    result = jax.random.normal(key, dims, jnp.float32) * scale * factor_of
    return jnp.minimum(jnp.maximum(result, -bound), bound).astype(kind)


def setup_inputs(seed: int = 0) -> dict:
    arg_keys = jax.random.split(jax.random.key(seed), 6)
    amplitudes = normal_values(arg_keys[0], (NVIR, NVIR), 1.0, 6.0, ((0, 8),))
    hole_panel = normal_values(arg_keys[1], (NVIR, OCC_SLAB, NVIR), (NVIR // 8) ** -0.5, 0.375, ((1, 8), (2, 4)))
    virt_fock = normal_values(arg_keys[2], (NVIR, NVIR), NVIR ** -0.5, 0.125)
    irrep_sizes = ragged_sizes(arg_keys[3], NIRREP, NVIR, NVIR // 4, 1).astype(jnp.int32)
    pair_irreps = with_ends(jax.random.randint(arg_keys[4], (OCC_SLAB,), 0, 8), jax.random.fold_in(arg_keys[4], 1), 0, 7).astype(jnp.int32)
    return {"amplitudes": amplitudes, "hole_panel": hole_panel, "virt_fock": virt_fock, "irrep_sizes": irrep_sizes, "pair_irreps": pair_irreps}


def irrep_of(positions, block_sizes):
    bounds = jnp.cumsum(block_sizes)[:-1]
    return jnp.sum((positions[:, None] >= bounds[None, :]).astype(jnp.int32), axis=1)


def reference(amplitudes, hole_panel, virt_fock, irrep_sizes, pair_irreps):
    positions = jnp.arange(NVIR, dtype=jnp.int32)
    labels = irrep_of(positions, irrep_sizes)
    pair_xor = jnp.bitwise_xor(labels[:, None], labels[None, :])

    def one_pair(pair_item):
        pair_panel, target = pair_item
        masked = jnp.where(pair_xor == target, pair_panel, jnp.zeros((), pair_panel.dtype))
        coupled = jnp.dot(amplitudes, masked, preferred_element_type=jnp.float32).astype(jnp.bfloat16)
        return jnp.dot(coupled, virt_fock, preferred_element_type=jnp.float32).astype(jnp.bfloat16)

    stacked = lax.map(one_pair, (jnp.moveaxis(hole_panel, 1, 0), pair_irreps))
    return jnp.moveaxis(stacked, 0, 1)
```

```python
import jax
import jax.numpy as jnp
from jax import lax
from jax.sharding import PartitionSpec as P

LANES = 128


def irrep_of(positions, block_sizes):
    bounds = jnp.cumsum(block_sizes)[:-1]
    return jnp.sum((positions[:, None] >= bounds[None, :]).astype(jnp.int32), axis=1)


def swapped_bits(position, count):
    half = count // 2
    return (position % 2) * half + position // 2 if count % 2 == 0 else position


def make_local(blocks, groups):
    members = blocks // groups

    def device(hi, lo, grp):
        return (hi * members + lo) * groups + grp

    first = [
        (device(grp, lo, swapped_bits(hi, groups)), device(hi, lo, grp))
        for hi in range(groups)
        for lo in range(members)
        for grp in range(groups)
    ]

    def shifted(by):
        return [
            (device(hi, (lo + by) % members, grp), device(hi, lo, grp))
            for hi in range(groups)
            for lo in range(members)
            for grp in range(groups)
        ]

    def local(amplitudes, hole_panel, virt_fock, irrep_sizes, pair_irreps):
        rows, virtuals = amplitudes.shape
        quarter = hole_panel.shape[2]
        fold = -(-(virtuals // 4) // LANES) * LANES
        copies = -(-virtuals // fold)
        axes = ("blk", "grp")
        group = lax.axis_index("grp")
        member = lax.axis_index("blk") % members

        pieces = 2
        step = rows // pieces
        held = [
            lax.ppermute(amplitudes[k * step:(k + 1) * step], axes, first) for k in range(pieces)
        ]
        arrived = [held]
        for by in range(1, members):
            arrived.append([lax.ppermute(piece, axes, shifted(by)) for piece in held])

        labels = irrep_of(jnp.arange(virtuals, dtype=jnp.int32), irrep_sizes)
        wanted = jnp.bitwise_xor(labels, pair_irreps[0])
        own_wanted = lax.dynamic_slice_in_dim(wanted, group * quarter, quarter, 0)
        panel = jnp.swapaxes(hole_panel[:, 0, :], 0, 1)
        masked = jnp.where(own_wanted[:, None] == labels[None, :], panel, jnp.zeros((), panel.dtype))
        padded = jnp.pad(masked, ((0, 0), (0, copies * fold - virtuals)))
        folded = sum(padded[:, k * fold:(k + 1) * fold] for k in range(copies))

        grid = lambda step_of: [(p * groups + step_of(g), p * groups + g) for p in range(blocks) for g in range(groups)]
        if groups == 4:
            across = lax.ppermute(folded, axes, grid(lambda g: g ^ 2))
            beside = lax.ppermute(folded, axes, grid(lambda g: g ^ 1))
            both = lax.ppermute(across, axes, grid(lambda g: g ^ 1))
            stack = jnp.stack([folded, beside, across, both])
            full = jnp.concatenate([stack[group ^ k] for k in range(groups)])
        else:
            full = lax.all_gather(folded, "grp", axis=0, tiled=True)
        spread = jnp.concatenate([full] * copies, axis=1)[:, :virtuals]
        dense = jnp.where(wanted[:, None] == labels[None, :], spread, jnp.zeros((), full.dtype))

        parts = []
        for pieces_in in arrived:
            mine = jnp.concatenate(pieces_in)
            coupled = lax.dot_general(
                mine, dense, (((1,), (1,)), ((), ())), preferred_element_type=jnp.float32
            ).astype(jnp.bfloat16)
            parts.append(
                jnp.dot(coupled, virt_fock, preferred_element_type=jnp.float32).astype(jnp.bfloat16)
            )
        result = jnp.zeros((members * rows, virtuals), jnp.bfloat16)
        for by, part in enumerate(parts):
            place = (member + by) % members * rows
            result = lax.dynamic_update_slice_in_dim(result, part, place, 0)
        return result[:, None, :]

    return local


def solution(mesh):
    in_specs = (P("blk", None), P(None, "blk", "grp"), P(), P(), P("blk"))
    out_specs = P("grp", "blk", None)
    local = make_local(mesh.shape["blk"], mesh.shape["grp"])
    return jax.shard_map(local, mesh=mesh, in_specs=in_specs, out_specs=out_specs, check_vma=False)
```

```python
import functools

import jax
import jax.numpy as jnp
from jax import lax
from jax.experimental import pallas as pl
from jax.experimental.pallas import tpu as pltpu
from jax.sharding import PartitionSpec as P

LANES = 128
SUBLANES = 16
MIB = 1 << 20


def rounded(value, unit):
    return -(-value // unit) * unit


def fill_bounds(sizes, bounds):
    total = jnp.int32(0)
    for r in range(sizes.shape[0]):
        bounds[r] = total
        total = total + sizes[r]
    bounds[sizes.shape[0]] = total


def wanted_range(b, pair, bounds, irreps):
    low, high = jnp.zeros_like(b), jnp.zeros_like(b)
    for r in range(irreps):
        partner = jnp.bitwise_xor(pair[0], r)
        inside = (b >= bounds[r]) & (b < bounds[r + 1])
        low = jnp.where(inside, bounds[partner], low)
        high = jnp.where(inside, bounds[partner + 1], high)
    return low, high


def fold_kernel(sizes, pair, panel, folded, bounds):
    quarter, virtuals = panel.shape
    fold = folded.shape[1]
    fill_bounds(sizes, bounds)
    start = lax.axis_index("grp") * quarter
    step = 32 if quarter % 32 == 0 else SUBLANES

    @pl.loop(0, quarter // step)
    def _(i):
        first = pl.multiple_of(i * step, step)
        here = pl.ds(first, step)
        b = start + first + lax.broadcasted_iota(jnp.int32, (step, LANES), 0)
        low, high = wanted_range(b, pair, bounds, sizes.shape[0])
        lane = lax.broadcasted_iota(jnp.int32, (step, LANES), 1)
        low, high = low - lane, high - lane
        for place in range(0, fold, LANES):
            total = jnp.zeros((step, LANES), jnp.float32)
            for c in range(place, virtuals, fold):
                value = panel[here, c:c + LANES].astype(jnp.float32)
                total = jnp.where((low <= c) & (high > c), value, total)
            folded[here, place:place + LANES] = total.astype(folded.dtype)


def fold_panel(panel, sizes, pair, fold):
    quarter, virtuals = panel.shape
    return pl.pallas_call(
        fold_kernel,
        out_shape=jax.ShapeDtypeStruct((quarter, fold), panel.dtype),
        in_specs=[
            pl.BlockSpec(memory_space=pltpu.SMEM),
            pl.BlockSpec(memory_space=pltpu.SMEM),
            pl.BlockSpec(memory_space=pltpu.VMEM),
        ],
        out_specs=pl.BlockSpec(memory_space=pltpu.VMEM),
        scratch_shapes=[pltpu.SMEM((sizes.shape[0] + 1,), jnp.int32)],
        compiler_params=pltpu.CompilerParams(vmem_limit_bytes=8 * MIB),
        cost_estimate=pl.CostEstimate(
            flops=0, bytes_accessed=2 * quarter * (virtuals + fold), transcendentals=0
        ),
        name="fold_panel",
    )(sizes, pair, panel)


def spread_kernel(slots, sizes, pair, fock, *refs):
    count = len(slots)
    folded, (dense, fock_out, bounds, turned, sems) = refs[:count], refs[count:]
    quarter, fold = folded[0].shape
    virtuals = dense.shape[1]
    width = dense.shape[2]
    group = lax.axis_index("grp")
    copies = []
    for k, slot in enumerate(slots):
        first = pl.multiple_of(jnp.bitwise_xor(group, slot) * quarter, SUBLANES)
        copies.append(pltpu.make_async_copy(
            fock.at[pl.ds(first, quarter)], fock_out.at[k, pl.ds(0, quarter)], sems.at[k]
        ))
        copies[-1].start()
    fill_bounds(sizes, bounds)
    step = 32
    for k, slot in enumerate(slots):
        if width > quarter:
            fock_out[k, quarter:width, :] = jnp.zeros((width - quarter, virtuals), fock_out.dtype)
        values = folded[k][...].astype(jnp.float32)
        if width > quarter:
            values = jnp.concatenate([values, jnp.zeros((width - quarter, fold), jnp.float32)])
        turned[...] = values.T
        start = jnp.bitwise_xor(group, slot) * quarter
        b = start + lax.broadcasted_iota(jnp.int32, (8, width), 1)
        low, high = wanted_range(b, pair, bounds, sizes.shape[0])
        low = jnp.concatenate([low] * (step // 8))
        high = jnp.concatenate([high] * (step // 8))

        @pl.loop(0, virtuals // step)
        def _(i):
            first = pl.multiple_of(i * step, step)
            source = pl.multiple_of(lax.rem(first, fold), step)
            c = first + lax.broadcasted_iota(jnp.int32, (step, width), 0)
            kept = jnp.where((c >= low) & (c < high), turned[pl.ds(source, step), :], 0.0)
            dense[k, pl.ds(first, step), :] = kept.astype(dense.dtype)

    for copy in copies:
        copy.wait()


def spread(slots, folded, fock, sizes, pair):
    quarter, fold = folded[0].shape
    virtuals = fock.shape[0]
    width = rounded(quarter, LANES)
    count = len(slots)
    smem = pl.BlockSpec(memory_space=pltpu.SMEM)
    vmem = pl.BlockSpec(memory_space=pltpu.VMEM)
    return pl.pallas_call(
        functools.partial(spread_kernel, slots),
        out_shape=(
            pltpu.VMEM((count, virtuals, width), fock.dtype),
            pltpu.VMEM((count, width, virtuals), fock.dtype),
        ),
        in_specs=[smem, smem, pl.BlockSpec(memory_space=pl.ANY)] + [vmem] * count,
        out_specs=(vmem, vmem),
        scratch_shapes=[
            pltpu.SMEM((sizes.shape[0] + 1,), jnp.int32),
            pltpu.VMEM((fold, width), jnp.float32),
            pltpu.SemaphoreType.DMA((count,)),
        ],
        compiler_params=pltpu.CompilerParams(vmem_limit_bytes=16 * MIB),
        cost_estimate=pl.CostEstimate(
            flops=0, bytes_accessed=6 * count * quarter * virtuals, transcendentals=0
        ),
        name="spread_panel",
    )(sizes, pair, fock, *folded)


def column_tiles(total, tile):
    return [(first, min(tile, total - first)) for first in range(0, total, tile)]


def dress_kernel(by, offset, rows, members, sets, has_base, *refs):
    amplitudes, refs = refs[0], refs[1:]
    dense, focks, refs = refs[:sets], refs[sets:2 * sets], refs[2 * sets:]
    if has_base:
        refs = refs[1:]
    result, coupled, dressed, sems = refs
    height = amplitudes.shape[0]
    virtuals = amplitudes.shape[1]
    width = dense[0].shape[2]
    slots = [(part, k) for part in range(sets) for k in range(dense[part].shape[0])]
    member = lax.rem(lax.axis_index("blk") + by, members)
    place = pl.multiple_of(member * rows + offset, SUBLANES)
    for s, (part, k) in enumerate(slots):
        for first, tile in column_tiles(width, 256):
            coupled[:, s * width + first:s * width + first + tile] = jnp.dot(
                amplitudes[...], dense[part][k, :, first:first + tile],
                preferred_element_type=jnp.float32,
            ).astype(coupled.dtype)
    copies = []
    for t, (first, tile) in enumerate(column_tiles(virtuals, 512)):
        total = jnp.zeros((height, tile), jnp.float32)
        for s, (part, k) in enumerate(slots):
            total = total + jnp.dot(
                coupled[:, s * width:(s + 1) * width], focks[part][k, :, first:first + tile],
                preferred_element_type=jnp.float32,
            )
        dressed[:, first:first + tile] = total.astype(dressed.dtype)
        copies.append(pltpu.make_async_copy(
            dressed.at[:, pl.ds(first, tile)],
            result.at[pl.ds(place, height), pl.ds(first, tile)],
            sems.at[t],
        ))
        copies[-1].start()
    for copy in copies:
        copy.wait()


def dress(amplitudes, dense, focks, base, by, offset, rows, members, out_rows):
    height, virtuals = amplitudes.shape
    width = dense[0].shape[2]
    slots = sum(d.shape[0] for d in dense)
    vmem = pl.BlockSpec(memory_space=pltpu.VMEM)
    anywhere = pl.BlockSpec(memory_space=pl.ANY)
    pinned = [pltpu.with_memory_space_constraint(x, pltpu.VMEM) for x in (*dense, *focks)]
    bases = [] if base is None else [base]
    return pl.pallas_call(
        functools.partial(dress_kernel, by, offset, rows, members, len(dense), base is not None),
        out_shape=jax.ShapeDtypeStruct((out_rows, virtuals), amplitudes.dtype),
        in_specs=[vmem] * (1 + len(pinned)) + [anywhere] * len(bases),
        out_specs=anywhere,
        input_output_aliases={} if base is None else {1 + len(pinned): 0},
        scratch_shapes=[
            pltpu.VMEM((height, slots * width), amplitudes.dtype),
            pltpu.VMEM((height, virtuals), amplitudes.dtype),
            pltpu.SemaphoreType.DMA((len(column_tiles(virtuals, 512)),)),
        ],
        compiler_params=pltpu.CompilerParams(vmem_limit_bytes=16 * MIB),
        cost_estimate=pl.CostEstimate(
            flops=4 * height * virtuals * virtuals,
            bytes_accessed=4 * height * virtuals,
            transcendentals=0,
        ),
        name="dress_rows",
    )(amplitudes, *pinned, *bases)


def make_local(blocks, groups):
    members = blocks // groups
    axes = ("blk", "grp")

    def device(hi, lo, grp):
        return (hi * members + lo) * groups + grp

    everyone = [(h, l, g) for h in range(groups) for l in range(members) for g in range(groups)]

    def source_copy(hi, grp):
        if groups != 4:
            return hi
        order = {0: (0, 2, 1, 3), 1: (3, 1, 2, 0), 2: (0, 3, 2, 1), 3: (2, 0, 1, 3)}
        return order[grp][hi]

    to_group = [(device(g, l, source_copy(h, g)), device(h, l, g)) for h, l, g in everyone]

    def to_member(by):
        return [(device(h, (l + by) % members, g), device(h, l, g)) for h, l, g in everyone]

    def to_slot(slot):
        return [(device(h, l, g ^ slot), device(h, l, g)) for h, l, g in everyone]

    def local(amplitudes, hole_panel, virt_fock, irrep_sizes, pair_irreps):
        rows, virtuals = amplitudes.shape
        out_rows = rows * members
        fold = rounded(virtuals // 4, LANES)
        panel = jnp.swapaxes(hole_panel[:, 0, :], 0, 1)

        if rows % SUBLANES == 0:
            half = rounded(rows // 2, SUBLANES)
            spans = [(0, half), (half, rows - half)]
        else:
            spans = [(0, rows)]
        held = [
            lax.ppermute(lax.slice_in_dim(amplitudes, first, first + size), axes, to_group)
            for first, size in spans
        ]
        arrived = {(0, k): piece for k, piece in enumerate(held)}
        for k, piece in enumerate(held):
            for by in range(1, members):
                arrived[by, k] = lax.ppermute(piece, axes, to_member(by))

        own = fold_panel(panel, irrep_sizes, pair_irreps, fold)
        across = lax.ppermute(own, axes, to_slot(2))
        beside = lax.ppermute(own, axes, to_slot(1))
        near_dense, near_fock = spread((0, 1), (own, beside), virt_fock, irrep_sizes, pair_irreps)
        both = lax.ppermute(across, axes, to_slot(1))
        far_dense, far_fock = spread((2, 3), (across, both), virt_fock, irrep_sizes, pair_irreps)
        dense, focks = (near_dense, far_dense), (near_fock, far_fock)

        if rows % SUBLANES == 0:
            pieces = [(jnp.concatenate(held), 0, 0)]
            pieces += [
                (arrived[by, k], by, spans[k][0]) for by in range(1, members) for k in range(len(spans))
            ]
            result = None
            for piece, by, offset in pieces:
                result = dress(piece, dense, focks, result, by, offset, rows, members, out_rows)
        else:
            member = lax.axis_index("blk") % members
            stacked = jnp.stack([arrived[by, 0] for by in range(members)])
            ordered = jnp.roll(stacked, member, axis=0).reshape(out_rows, virtuals)
            result = dress(ordered, dense, focks, None, 0, 0, 0, members, out_rows)
        return result[:, None, :]

    return local


def solution(mesh):
    in_specs = (P("blk", None), P(None, "blk", "grp"), P(), P(), P("blk"))
    out_specs = P("grp", "blk", None)
    local = make_local(mesh.shape["blk"], mesh.shape["grp"])
    return jax.shard_map(local, mesh=mesh, in_specs=in_specs, out_specs=out_specs, check_vma=False)
```

```python
import functools

import jax
import jax.numpy as jnp
from jax import lax
from jax.experimental import pallas as pl
from jax.experimental.pallas import tpu as pltpu
from jax.sharding import PartitionSpec as P

LANES = 128
SUBLANES = 16
MIB = 1 << 20


def rounded(value, unit):
    return -(-value // unit) * unit


def fill_bounds(sizes, bounds):
    total = jnp.int32(0)
    for r in range(sizes.shape[0]):
        bounds[r] = total
        total = total + sizes[r]
    bounds[sizes.shape[0]] = total


def wanted_range(b, pair, bounds, irreps):
    low, high = jnp.zeros_like(b), jnp.zeros_like(b)
    for r in range(irreps):
        partner = jnp.bitwise_xor(pair[0], r)
        inside = (b >= bounds[r]) & (b < bounds[r + 1])
        low = jnp.where(inside, bounds[partner], low)
        high = jnp.where(inside, bounds[partner + 1], high)
    return low, high


def fold_kernel(sizes, pair, panel, folded, bounds):
    quarter, virtuals = panel.shape
    fold = folded.shape[1]
    fill_bounds(sizes, bounds)
    start = lax.axis_index("grp") * quarter
    step = 32 if quarter % 32 == 0 else SUBLANES

    @pl.loop(0, quarter // step)
    def _(i):
        first = pl.multiple_of(i * step, step)
        here = pl.ds(first, step)
        b = start + first + lax.broadcasted_iota(jnp.int32, (step, LANES), 0)
        low, high = wanted_range(b, pair, bounds, sizes.shape[0])
        lane = lax.broadcasted_iota(jnp.int32, (step, LANES), 1)
        low, high = low - lane, high - lane
        for place in range(0, fold, LANES):
            total = jnp.zeros((step, LANES), jnp.float32)
            for c in range(place, virtuals, fold):
                value = panel[here, c:c + LANES].astype(jnp.float32)
                total = jnp.where((low <= c) & (high > c), value, total)
            folded[here, place:place + LANES] = total.astype(folded.dtype)


def fold_panel(panel, sizes, pair, fold):
    quarter, virtuals = panel.shape
    return pl.pallas_call(
        fold_kernel,
        out_shape=jax.ShapeDtypeStruct((quarter, fold), panel.dtype),
        in_specs=[
            pl.BlockSpec(memory_space=pltpu.SMEM),
            pl.BlockSpec(memory_space=pltpu.SMEM),
            pl.BlockSpec(memory_space=pltpu.VMEM),
        ],
        out_specs=pl.BlockSpec(memory_space=pltpu.VMEM),
        scratch_shapes=[pltpu.SMEM((sizes.shape[0] + 1,), jnp.int32)],
        compiler_params=pltpu.CompilerParams(vmem_limit_bytes=8 * MIB),
        cost_estimate=pl.CostEstimate(
            flops=0, bytes_accessed=2 * quarter * (virtuals + fold), transcendentals=0
        ),
        name="fold_panel",
    )(sizes, pair, panel)


def spread_kernel(slots, sizes, pair, fock, *refs):
    count = len(slots)
    folded, (dense, fock_out, bounds, turned, sems) = refs[:count], refs[count:]
    quarter, fold = folded[0].shape
    virtuals = dense.shape[1]
    width = dense.shape[2]
    group = lax.axis_index("grp")
    copies = []
    for k, slot in enumerate(slots):
        first = pl.multiple_of(jnp.bitwise_xor(group, slot) * quarter, SUBLANES)
        copies.append(pltpu.make_async_copy(
            fock.at[pl.ds(first, quarter)], fock_out.at[k, pl.ds(0, quarter)], sems.at[k]
        ))
        copies[-1].start()
    fill_bounds(sizes, bounds)
    step = 32
    for k, slot in enumerate(slots):
        if width > quarter:
            fock_out[k, quarter:width, :] = jnp.zeros((width - quarter, virtuals), fock_out.dtype)
        values = folded[k][...].astype(jnp.float32)
        if width > quarter:
            values = jnp.concatenate([values, jnp.zeros((width - quarter, fold), jnp.float32)])
        turned[...] = values.T
        start = jnp.bitwise_xor(group, slot) * quarter
        b = start + lax.broadcasted_iota(jnp.int32, (8, width), 1)
        low, high = wanted_range(b, pair, bounds, sizes.shape[0])
        low = jnp.concatenate([low] * (step // 8))
        high = jnp.concatenate([high] * (step // 8))

        @pl.loop(0, virtuals // step)
        def _(i):
            first = pl.multiple_of(i * step, step)
            source = pl.multiple_of(lax.rem(first, fold), step)
            c = first + lax.broadcasted_iota(jnp.int32, (step, width), 0)
            kept = jnp.where((c >= low) & (c < high), turned[pl.ds(source, step), :], 0.0)
            dense[k, pl.ds(first, step), :] = kept.astype(dense.dtype)

    for copy in copies:
        copy.wait()


def spread(slots, folded, fock, sizes, pair):
    quarter, fold = folded[0].shape
    virtuals = fock.shape[0]
    width = rounded(quarter, LANES)
    count = len(slots)
    smem = pl.BlockSpec(memory_space=pltpu.SMEM)
    vmem = pl.BlockSpec(memory_space=pltpu.VMEM)
    return pl.pallas_call(
        functools.partial(spread_kernel, slots),
        out_shape=(
            pltpu.VMEM((count, virtuals, width), fock.dtype),
            pltpu.VMEM((count, width, virtuals), fock.dtype),
        ),
        in_specs=[smem, smem, pl.BlockSpec(memory_space=pl.ANY)] + [vmem] * count,
        out_specs=(vmem, vmem),
        scratch_shapes=[
            pltpu.SMEM((sizes.shape[0] + 1,), jnp.int32),
            pltpu.VMEM((fold, width), jnp.float32),
            pltpu.SemaphoreType.DMA((count,)),
        ],
        compiler_params=pltpu.CompilerParams(vmem_limit_bytes=16 * MIB),
        cost_estimate=pl.CostEstimate(
            flops=0, bytes_accessed=count * quarter * fold, transcendentals=0
        ),
        name="spread_panel",
    )(sizes, pair, fock, *folded)


def after(array, *others):
    anywhere = pl.BlockSpec(memory_space=pl.ANY)
    return pl.pallas_call(
        lambda *refs: None,
        out_shape=jax.ShapeDtypeStruct(array.shape, array.dtype),
        in_specs=[anywhere] * (1 + len(others)),
        out_specs=anywhere,
        input_output_aliases={0: 0},
        compiler_params=pltpu.CompilerParams(vmem_limit_bytes=MIB),
        cost_estimate=pl.CostEstimate(flops=0, bytes_accessed=0, transcendentals=0),
        name="after",
    )(array, *others)


def column_tiles(total, tile):
    return [(first, min(tile, total - first)) for first in range(0, total, tile)]


def dress_kernel(by, offset, rows, members, sets, has_base, *refs):
    amplitudes, refs = refs[0], refs[1:]
    dense, focks, refs = refs[:sets], refs[sets:2 * sets], refs[2 * sets:]
    if has_base:
        refs = refs[1:]
    result, coupled, dressed, sems = refs
    height = amplitudes.shape[0]
    virtuals = amplitudes.shape[1]
    width = dense[0].shape[2]
    slots = [(part, k) for part in range(sets) for k in range(dense[part].shape[0])]
    member = lax.rem(lax.axis_index("blk") + by, members)
    place = pl.multiple_of(member * rows + offset, SUBLANES)
    for s, (part, k) in enumerate(slots):
        for first, tile in column_tiles(width, 256):
            coupled[:, s * width + first:s * width + first + tile] = jnp.dot(
                amplitudes[...], dense[part][k, :, first:first + tile],
                preferred_element_type=jnp.float32,
            ).astype(coupled.dtype)
    copies = []
    for t, (first, tile) in enumerate(column_tiles(virtuals, 512)):
        total = jnp.zeros((height, tile), jnp.float32)
        for s, (part, k) in enumerate(slots):
            total = total + jnp.dot(
                coupled[:, s * width:(s + 1) * width], focks[part][k, :, first:first + tile],
                preferred_element_type=jnp.float32,
            )
        dressed[:, first:first + tile] = total.astype(dressed.dtype)
        copies.append(pltpu.make_async_copy(
            dressed.at[:, pl.ds(first, tile)],
            result.at[pl.ds(place, height), pl.ds(first, tile)],
            sems.at[t],
        ))
        copies[-1].start()
    for copy in copies:
        copy.wait()


def dress(amplitudes, dense, focks, base, by, offset, rows, members, out_rows):
    height, virtuals = amplitudes.shape
    width = dense[0].shape[2]
    slots = sum(d.shape[0] for d in dense)
    vmem = pl.BlockSpec(memory_space=pltpu.VMEM)
    anywhere = pl.BlockSpec(memory_space=pl.ANY)
    pinned = [pltpu.with_memory_space_constraint(x, pltpu.VMEM) for x in (*dense, *focks)]
    bases = [] if base is None else [base]
    return pl.pallas_call(
        functools.partial(dress_kernel, by, offset, rows, members, len(dense), base is not None),
        out_shape=jax.ShapeDtypeStruct((out_rows, virtuals), amplitudes.dtype),
        in_specs=[vmem] * (1 + len(pinned)) + [anywhere] * len(bases),
        out_specs=anywhere,
        input_output_aliases={} if base is None else {1 + len(pinned): 0},
        scratch_shapes=[
            pltpu.VMEM((height, slots * width), amplitudes.dtype),
            pltpu.VMEM((height, virtuals), amplitudes.dtype),
            pltpu.SemaphoreType.DMA((len(column_tiles(virtuals, 512)),)),
        ],
        compiler_params=pltpu.CompilerParams(vmem_limit_bytes=16 * MIB),
        cost_estimate=pl.CostEstimate(
            flops=4 * height * virtuals * virtuals,
            bytes_accessed=4 * height * virtuals,
            transcendentals=0,
        ),
        name="dress_rows",
    )(amplitudes, *pinned, *bases)


def make_local(blocks, groups):
    members = blocks // groups
    axes = ("blk", "grp")

    def device(hi, lo, grp):
        return (hi * members + lo) * groups + grp

    everyone = [(h, l, g) for h in range(groups) for l in range(members) for g in range(groups)]

    def source_copy(hi, grp):
        if groups != 4:
            return hi
        order = {0: (0, 2, 1, 3), 1: (3, 1, 2, 0), 2: (0, 3, 2, 1), 3: (2, 0, 1, 3)}
        return order[grp][hi]

    to_group = [(device(g, l, source_copy(h, g)), device(h, l, g)) for h, l, g in everyone]

    def to_member(by):
        return [(device(h, (l + by) % members, g), device(h, l, g)) for h, l, g in everyone]

    def to_slot(slot):
        return [(device(h, l, g ^ slot), device(h, l, g)) for h, l, g in everyone]

    def local(amplitudes, hole_panel, virt_fock, irrep_sizes, pair_irreps):
        rows, virtuals = amplitudes.shape
        out_rows = rows * members
        fold = rounded(virtuals // 4, LANES)
        panel = jnp.swapaxes(hole_panel[:, 0, :], 0, 1)

        if rows % SUBLANES == 0:
            half = rounded(rows // 2, SUBLANES)
            spans = [(0, half), (half, rows - half)]
        else:
            spans = [(0, rows)]
        held = [
            lax.ppermute(lax.slice_in_dim(amplitudes, first, first + size), axes, to_group)
            for first, size in spans
        ]

        own = fold_panel(panel, irrep_sizes, pair_irreps, fold)
        across = lax.ppermute(own, axes, to_slot(2))
        beside = lax.ppermute(own, axes, to_slot(1))
        fock = pltpu.with_memory_space_constraint(virt_fock, pltpu.HBM)
        near_dense, near_fock = spread((0, 1), (own, beside), fock, irrep_sizes, pair_irreps)
        across = after(across, near_dense)
        both = lax.ppermute(across, axes, to_slot(1))

        held[0] = after(held[0], near_dense)
        for k in range(1, len(held)):
            held[k] = after(held[k], held[k - 1])
        arrived = {(0, k): piece for k, piece in enumerate(held)}
        for k, piece in enumerate(held):
            for by in range(1, members):
                arrived[by, k] = lax.ppermute(piece, axes, to_member(by))

        far_dense, far_fock = spread((2, 3), (across, both), fock, irrep_sizes, pair_irreps)
        dense, focks = (near_dense, far_dense), (near_fock, far_fock)

        if rows % SUBLANES == 0:
            pieces = [(jnp.concatenate(held), 0, 0)]
            pieces += [
                (arrived[by, k], by, spans[k][0]) for by in range(1, members) for k in range(len(spans))
            ]
            result = None
            for piece, by, offset in pieces:
                result = dress(piece, dense, focks, result, by, offset, rows, members, out_rows)
        else:
            member = lax.axis_index("blk") % members
            stacked = jnp.stack([arrived[by, 0] for by in range(members)])
            ordered = jnp.roll(stacked, member, axis=0).reshape(out_rows, virtuals)
            result = dress(ordered, dense, focks, None, 0, 0, 0, members, out_rows)
        return result[:, None, :]

    return local


def solution(mesh):
    in_specs = (P("blk", None), P(None, "blk", "grp"), P(), P(), P("blk"))
    out_specs = P("grp", "blk", None)
    local = make_local(mesh.shape["blk"], mesh.shape["grp"])
    return jax.shard_map(local, mesh=mesh, in_specs=in_specs, out_specs=out_specs, check_vma=False)
```

```python
import functools

import jax
import jax.numpy as jnp
from jax import lax
from jax.experimental import pallas as pl
from jax.experimental.pallas import tpu as pltpu
from jax.sharding import PartitionSpec as P

LANES = 128
SUBLANES = 16
MIB = 1 << 20
NOTHING = pl.CostEstimate(flops=0, bytes_accessed=0, transcendentals=0)


def rounded(value, unit):
    return -(-value // unit) * unit


def fill_bounds(sizes, bounds):
    total = jnp.int32(0)
    for r in range(sizes.shape[0]):
        bounds[r] = total
        total = total + sizes[r]
    bounds[sizes.shape[0]] = total


def wanted_range(b, pair, bounds, irreps):
    low, high = jnp.zeros_like(b), jnp.zeros_like(b)
    for r in range(irreps):
        partner = jnp.bitwise_xor(pair[0], r)
        inside = (b >= bounds[r]) & (b < bounds[r + 1])
        low = jnp.where(inside, bounds[partner], low)
        high = jnp.where(inside, bounds[partner + 1], high)
    return low, high


def fold_kernel(sizes, pair, panel, folded, bounds):
    quarter, virtuals = panel.shape
    fold = folded.shape[1]
    fill_bounds(sizes, bounds)
    start = lax.axis_index("grp") * quarter
    step = 32 if quarter % 32 == 0 else SUBLANES

    @pl.loop(0, quarter // step)
    def _(i):
        first = pl.multiple_of(i * step, step)
        here = pl.ds(first, step)
        b = start + first + lax.broadcasted_iota(jnp.int32, (step, LANES), 0)
        low, high = wanted_range(b, pair, bounds, sizes.shape[0])
        lane = lax.broadcasted_iota(jnp.int32, (step, LANES), 1)
        low, high = low - lane, high - lane
        for place in range(0, fold, LANES):
            total = jnp.zeros((step, LANES), jnp.float32)
            for c in range(place, virtuals, fold):
                value = panel[here, c:c + LANES].astype(jnp.float32)
                total = jnp.where((low <= c) & (high > c), value, total)
            folded[here, place:place + LANES] = total.astype(folded.dtype)


def fold_panel(panel, sizes, pair, fold):
    quarter, virtuals = panel.shape
    return pl.pallas_call(
        fold_kernel,
        out_shape=jax.ShapeDtypeStruct((quarter, fold), panel.dtype),
        in_specs=[
            pl.BlockSpec(memory_space=pltpu.SMEM),
            pl.BlockSpec(memory_space=pltpu.SMEM),
            pl.BlockSpec(memory_space=pltpu.VMEM),
        ],
        out_specs=pl.BlockSpec(memory_space=pltpu.VMEM),
        scratch_shapes=[pltpu.SMEM((sizes.shape[0] + 1,), jnp.int32)],
        compiler_params=pltpu.CompilerParams(vmem_limit_bytes=8 * MIB),
        cost_estimate=NOTHING,
        name="fold_panel",
    )(sizes, pair, panel)


def spread_kernel(slots, sizes, pair, fock, *refs):
    count = len(slots)
    folded, (dense, fock_out, bounds, turned, sems) = refs[:count], refs[count:]
    quarter, fold = folded[0].shape
    virtuals = dense.shape[1]
    width = dense.shape[2]
    group = lax.axis_index("grp")
    copies = []
    for k, slot in enumerate(slots):
        first = pl.multiple_of(jnp.bitwise_xor(group, slot) * quarter, SUBLANES)
        copies.append(pltpu.make_async_copy(
            fock.at[pl.ds(first, quarter)], fock_out.at[k, pl.ds(0, quarter)], sems.at[k]
        ))
        copies[-1].start()
    fill_bounds(sizes, bounds)
    step = 32
    for k, slot in enumerate(slots):
        if width > quarter:
            fock_out[k, quarter:width, :] = jnp.zeros((width - quarter, virtuals), fock_out.dtype)
        values = folded[k][...].astype(jnp.float32)
        if width > quarter:
            values = jnp.concatenate([values, jnp.zeros((width - quarter, fold), jnp.float32)])
        turned[...] = values.T
        start = jnp.bitwise_xor(group, slot) * quarter
        b = start + lax.broadcasted_iota(jnp.int32, (8, width), 1)
        low, high = wanted_range(b, pair, bounds, sizes.shape[0])
        low = jnp.concatenate([low] * (step // 8))
        high = jnp.concatenate([high] * (step // 8))

        @pl.loop(0, virtuals // step)
        def _(i):
            first = pl.multiple_of(i * step, step)
            source = pl.multiple_of(lax.rem(first, fold), step)
            c = first + lax.broadcasted_iota(jnp.int32, (step, width), 0)
            kept = jnp.where((c >= low) & (c < high), turned[pl.ds(source, step), :], 0.0)
            dense[k, pl.ds(first, step), :] = kept.astype(dense.dtype)

    for copy in copies:
        copy.wait()


def spread(slots, folded, fock, sizes, pair):
    quarter, fold = folded[0].shape
    virtuals = fock.shape[0]
    width = rounded(quarter, LANES)
    count = len(slots)
    smem = pl.BlockSpec(memory_space=pltpu.SMEM)
    vmem = pl.BlockSpec(memory_space=pltpu.VMEM)
    return pl.pallas_call(
        functools.partial(spread_kernel, slots),
        out_shape=(
            pltpu.VMEM((count, virtuals, width), fock.dtype),
            pltpu.VMEM((count, width, virtuals), fock.dtype),
        ),
        in_specs=[smem, smem, pl.BlockSpec(memory_space=pl.ANY)] + [vmem] * count,
        out_specs=(vmem, vmem),
        scratch_shapes=[
            pltpu.SMEM((sizes.shape[0] + 1,), jnp.int32),
            pltpu.VMEM((fold, width), jnp.float32),
            pltpu.SemaphoreType.DMA((count,)),
        ],
        compiler_params=pltpu.CompilerParams(vmem_limit_bytes=16 * MIB),
        cost_estimate=NOTHING,
        name="spread_panel",
    )(sizes, pair, fock, *folded)


def after(array, *others):
    anywhere = pl.BlockSpec(memory_space=pl.ANY)
    return pl.pallas_call(
        lambda *refs: None,
        out_shape=jax.ShapeDtypeStruct(array.shape, array.dtype),
        in_specs=[anywhere] * (1 + len(others)),
        out_specs=anywhere,
        input_output_aliases={0: 0},
        compiler_params=pltpu.CompilerParams(vmem_limit_bytes=MIB),
        cost_estimate=NOTHING,
        name="after",
    )(array, *others)


def column_tiles(total, tile):
    return [(first, min(tile, total - first)) for first in range(0, total, tile)]


def dress_kernel(spans, rows, members, sets, has_base, *refs):
    amplitudes, refs = refs[0], refs[1:]
    dense, focks, refs = refs[:sets], refs[sets:2 * sets], refs[2 * sets:]
    if has_base:
        refs = refs[1:]
    result, token, coupled, dressed, sems = refs
    token[...] = jnp.zeros_like(token)
    height = amplitudes.shape[0]
    virtuals = amplitudes.shape[1]
    width = dense[0].shape[2]
    slots = [(part, k) for part in range(sets) for k in range(dense[part].shape[0])]
    block = lax.axis_index("blk")
    places = [
        pl.multiple_of(lax.rem(block + by, members) * rows + offset, SUBLANES)
        for by, offset, _ in spans
    ]
    for s, (part, k) in enumerate(slots):
        for first, tile in column_tiles(width, 256):
            coupled[:, s * width + first:s * width + first + tile] = jnp.dot(
                amplitudes[...], dense[part][k, :, first:first + tile],
                preferred_element_type=jnp.float32,
            ).astype(coupled.dtype)
    copies = []
    for t, (first, tile) in enumerate(column_tiles(virtuals, 512)):
        total = jnp.zeros((height, tile), jnp.float32)
        for s, (part, k) in enumerate(slots):
            total = total + jnp.dot(
                coupled[:, s * width:(s + 1) * width], focks[part][k, :, first:first + tile],
                preferred_element_type=jnp.float32,
            )
        dressed[:, first:first + tile] = total.astype(dressed.dtype)
        begin = 0
        for p, (_, _, size) in enumerate(spans):
            copies.append(pltpu.make_async_copy(
                dressed.at[pl.ds(begin, size), pl.ds(first, tile)],
                result.at[pl.ds(places[p], size), pl.ds(first, tile)],
                sems.at[p, t],
            ))
            copies[-1].start()
            begin += size
    for copy in copies:
        copy.wait()


def dress(amplitudes, spans, dense, focks, base, rows, members, out_rows):
    height, virtuals = amplitudes.shape
    width = dense[0].shape[2]
    slots = sum(d.shape[0] for d in dense)
    vmem = pl.BlockSpec(memory_space=pltpu.VMEM)
    anywhere = pl.BlockSpec(memory_space=pl.ANY)
    pinned = [pltpu.with_memory_space_constraint(x, pltpu.VMEM) for x in (*dense, *focks)]
    bases = [] if base is None else [base]
    return pl.pallas_call(
        functools.partial(dress_kernel, spans, rows, members, len(dense), base is not None),
        out_shape=(
            jax.ShapeDtypeStruct((out_rows, virtuals), amplitudes.dtype),
            pltpu.VMEM((8, LANES), jnp.int32),
        ),
        in_specs=[vmem] * (1 + len(pinned)) + [anywhere] * len(bases),
        out_specs=(anywhere, vmem),
        input_output_aliases={} if base is None else {1 + len(pinned): 0},
        scratch_shapes=[
            pltpu.VMEM((height, slots * width), amplitudes.dtype),
            pltpu.VMEM((height, virtuals), amplitudes.dtype),
            pltpu.SemaphoreType.DMA((len(spans), len(column_tiles(virtuals, 512)))),
        ],
        compiler_params=pltpu.CompilerParams(vmem_limit_bytes=16 * MIB),
        cost_estimate=NOTHING,
        name="dress_rows",
    )(amplitudes, *pinned, *bases)


def make_local(blocks, groups):
    members = blocks // groups
    axes = ("blk", "grp")

    def device(hi, lo, grp):
        return (hi * members + lo) * groups + grp

    everyone = [(h, l, g) for h in range(groups) for l in range(members) for g in range(groups)]

    def source_copy(hi, grp):
        if groups != 4:
            return hi
        order = {0: (0, 2, 1, 3), 1: (3, 1, 2, 0), 2: (0, 3, 2, 1), 3: (2, 0, 1, 3)}
        return order[grp][hi]

    to_group = [(device(g, l, source_copy(h, g)), device(h, l, g)) for h, l, g in everyone]

    def to_member(by):
        return [(device(h, (l + by) % members, g), device(h, l, g)) for h, l, g in everyone]

    def to_slot(slot):
        return [(device(h, l, g ^ slot), device(h, l, g)) for h, l, g in everyone]

    def local(amplitudes, hole_panel, virt_fock, irrep_sizes, pair_irreps):
        rows, virtuals = amplitudes.shape
        out_rows = rows * members
        fold = rounded(virtuals // 4, LANES)
        panel = jnp.swapaxes(hole_panel[:, 0, :], 0, 1)

        own = fold_panel(panel, irrep_sizes, pair_irreps, fold)
        across = lax.ppermute(own, axes, to_slot(2))
        beside = lax.ppermute(own, axes, to_slot(1))

        early = rounded(rows * 3 // 5, SUBLANES) if rows % SUBLANES == 0 else rows
        top = lax.ppermute(amplitudes[:early], axes, to_group)
        tops = [top] + [lax.ppermute(top, axes, to_member(by)) for by in range(1, members)]
        if early < rows:
            low = amplitudes[early:]
            lows = [low] + [lax.ppermute(low, axes, to_member(by)) for by in range(1, members)]
            lows = lax.ppermute(after(jnp.concatenate(lows), top), axes, to_group)

        fock = pltpu.with_memory_space_constraint(virt_fock, pltpu.HBM)
        near_dense, near_fock = spread((0, 1), (own, beside), fock, irrep_sizes, pair_irreps)
        across = after(across, near_dense, top)
        both = lax.ppermute(across, axes, to_slot(1))
        far_dense, far_fock = spread((2, 3), (across, both), fock, irrep_sizes, pair_irreps)
        dense, focks = (near_dense, far_dense), (near_fock, far_fock)

        if early < rows:
            result = None
            for by, piece in enumerate(tops):
                spans = [(by, 0, early)]
                result, token = dress(piece, spans, dense, focks, result, rows, members, out_rows)
            spans = [(by, early, rows - early) for by in range(members)]
            lows = after(lows, token)
            result, _ = dress(lows, spans, dense, focks, result, rows, members, out_rows)
        else:
            member = lax.axis_index("blk") % members
            ordered = jnp.roll(jnp.stack(tops), member, axis=0).reshape(out_rows, virtuals)
            spans = [(0, 0, out_rows)]
            result, _ = dress(ordered, spans, dense, focks, None, 0, members, out_rows)
        return result[:, None, :]

    return local


def solution(mesh):
    in_specs = (P("blk", None), P(None, "blk", "grp"), P(), P(), P("blk"))
    out_specs = P("grp", "blk", None)
    local = make_local(mesh.shape["blk"], mesh.shape["grp"])
    return jax.shard_map(local, mesh=mesh, in_specs=in_specs, out_specs=out_specs, check_vma=False)
```

```python
import functools

import jax
import jax.numpy as jnp
from jax import lax
from jax.experimental import pallas as pl
from jax.experimental.pallas import tpu as pltpu
from jax.sharding import PartitionSpec as P

LANES = 128
SUBLANES = 16
MIB = 1 << 20
NOTHING = pl.CostEstimate(flops=0, bytes_accessed=0, transcendentals=0)


def rounded(value, unit):
    return -(-value // unit) * unit


def fill_bounds(sizes, bounds):
    total = jnp.int32(0)
    for r in range(sizes.shape[0]):
        bounds[r] = total
        total = total + sizes[r]
    bounds[sizes.shape[0]] = total


def wanted_range(b, pair, bounds, irreps):
    low, high = jnp.zeros_like(b), jnp.zeros_like(b)
    for r in range(irreps):
        partner = jnp.bitwise_xor(pair[0], r)
        inside = (b >= bounds[r]) & (b < bounds[r + 1])
        low = jnp.where(inside, bounds[partner], low)
        high = jnp.where(inside, bounds[partner + 1], high)
    return low, high


def cut_kernel(whole, *refs):
    pieces, sems = refs[:-1], refs[-1]
    copies, first = [], 0
    for k, piece in enumerate(pieces):
        size = piece.shape[0]
        copies.append(pltpu.make_async_copy(whole.at[pl.ds(first, size)], piece, sems.at[k]))
        copies[-1].start()
        first += size
    for copy in copies:
        copy.wait()


def cut(whole, sizes):
    vmem = pl.BlockSpec(memory_space=pltpu.VMEM)
    return pl.pallas_call(
        cut_kernel,
        out_shape=[pltpu.VMEM((size, whole.shape[1]), whole.dtype) for size in sizes],
        in_specs=[pl.BlockSpec(memory_space=pl.ANY)],
        out_specs=[vmem] * len(sizes),
        scratch_shapes=[pltpu.SemaphoreType.DMA((len(sizes),))],
        compiler_params=pltpu.CompilerParams(vmem_limit_bytes=4 * MIB),
        cost_estimate=NOTHING,
        name="cut_rows",
    )(pltpu.with_memory_space_constraint(whole, pltpu.HBM))


def fold_kernel(sizes, pair, panel, folded, bounds):
    quarter, virtuals = panel.shape
    fold = folded.shape[1]
    fill_bounds(sizes, bounds)
    start = (lax.axis_index("grp") * pl.num_programs(0) + pl.program_id(0)) * quarter
    step = 32 if quarter % 32 == 0 else SUBLANES

    @pl.loop(0, quarter // step)
    def _(i):
        first = pl.multiple_of(i * step, step)
        here = pl.ds(first, step)
        b = start + first + lax.broadcasted_iota(jnp.int32, (step, LANES), 0)
        low, high = wanted_range(b, pair, bounds, sizes.shape[0])
        lane = lax.broadcasted_iota(jnp.int32, (step, LANES), 1)
        low, high = low - lane, high - lane
        for place in range(0, fold, LANES):
            total = jnp.zeros((step, LANES), jnp.float32)
            for c in range(place, virtuals, fold):
                value = panel[here, c:c + LANES].astype(jnp.float32)
                total = jnp.where((low <= c) & (high > c), value, total)
            folded[here, place:place + LANES] = total.astype(folded.dtype)


def fold_panel(panel, sizes, pair, fold):
    quarter, virtuals = panel.shape
    chunk = quarter // 5 if quarter % (5 * SUBLANES) == 0 else quarter
    return pl.pallas_call(
        fold_kernel,
        grid=(quarter // chunk,),
        out_shape=jax.ShapeDtypeStruct((quarter, fold), panel.dtype),
        in_specs=[
            pl.BlockSpec(memory_space=pltpu.SMEM),
            pl.BlockSpec(memory_space=pltpu.SMEM),
            pl.BlockSpec((chunk, virtuals), lambda i: (i, 0)),
        ],
        out_specs=pl.BlockSpec((chunk, fold), lambda i: (i, 0)),
        scratch_shapes=[pltpu.SMEM((sizes.shape[0] + 1,), jnp.int32)],
        compiler_params=pltpu.CompilerParams(vmem_limit_bytes=8 * MIB),
        cost_estimate=NOTHING,
        name="fold_panel",
    )(sizes, pair, pltpu.with_memory_space_constraint(panel, pltpu.HBM))


def spread_kernel(slots, sizes, pair, fock, *refs):
    count = len(slots)
    folded, (dense, fock_out, bounds, turned, sems) = refs[:count], refs[count:]
    quarter, fold = folded[0].shape
    virtuals = dense.shape[1]
    width = dense.shape[2]
    group = lax.axis_index("grp")
    copies = []
    for k, slot in enumerate(slots):
        first = pl.multiple_of(jnp.bitwise_xor(group, slot) * quarter, SUBLANES)
        copies.append(pltpu.make_async_copy(
            fock.at[pl.ds(first, quarter)], fock_out.at[k, pl.ds(0, quarter)], sems.at[k]
        ))
        copies[-1].start()
    fill_bounds(sizes, bounds)
    step = 32
    for k, slot in enumerate(slots):
        if width > quarter:
            fock_out[k, quarter:width, :] = jnp.zeros((width - quarter, virtuals), fock_out.dtype)
        values = folded[k][...].astype(jnp.float32)
        if width > quarter:
            values = jnp.concatenate([values, jnp.zeros((width - quarter, fold), jnp.float32)])
        turned[...] = values.T
        start = jnp.bitwise_xor(group, slot) * quarter
        b = start + lax.broadcasted_iota(jnp.int32, (8, width), 1)
        low, high = wanted_range(b, pair, bounds, sizes.shape[0])
        low = jnp.concatenate([low] * (step // 8))
        high = jnp.concatenate([high] * (step // 8))

        @pl.loop(0, virtuals // step)
        def _(i):
            first = pl.multiple_of(i * step, step)
            source = pl.multiple_of(lax.rem(first, fold), step)
            c = first + lax.broadcasted_iota(jnp.int32, (step, width), 0)
            kept = jnp.where((c >= low) & (c < high), turned[pl.ds(source, step), :], 0.0)
            dense[k, pl.ds(first, step), :] = kept.astype(dense.dtype)

    for copy in copies:
        copy.wait()


def spread(slots, folded, fock, sizes, pair):
    quarter, fold = folded[0].shape
    virtuals = fock.shape[0]
    width = rounded(quarter, LANES)
    count = len(slots)
    smem = pl.BlockSpec(memory_space=pltpu.SMEM)
    vmem = pl.BlockSpec(memory_space=pltpu.VMEM)
    return pl.pallas_call(
        functools.partial(spread_kernel, slots),
        out_shape=(
            pltpu.VMEM((count, virtuals, width), fock.dtype),
            pltpu.VMEM((count, width, virtuals), fock.dtype),
        ),
        in_specs=[smem, smem, pl.BlockSpec(memory_space=pl.ANY)] + [vmem] * count,
        out_specs=(vmem, vmem),
        scratch_shapes=[
            pltpu.SMEM((sizes.shape[0] + 1,), jnp.int32),
            pltpu.VMEM((fold, width), jnp.float32),
            pltpu.SemaphoreType.DMA((count,)),
        ],
        compiler_params=pltpu.CompilerParams(vmem_limit_bytes=16 * MIB),
        cost_estimate=NOTHING,
        name="spread_panel",
    )(sizes, pair, fock, *folded)


def after(array, *others):
    anywhere = pl.BlockSpec(memory_space=pl.ANY)
    return pl.pallas_call(
        lambda *refs: None,
        out_shape=jax.ShapeDtypeStruct(array.shape, array.dtype),
        in_specs=[anywhere] * (1 + len(others)),
        out_specs=anywhere,
        input_output_aliases={0: 0},
        compiler_params=pltpu.CompilerParams(vmem_limit_bytes=MIB),
        cost_estimate=NOTHING,
        name="after",
    )(array, *others)


def column_tiles(total, tile):
    return [(first, min(tile, total - first)) for first in range(0, total, tile)]


def dress_kernel(spans, rows, members, sets, has_base, *refs):
    amplitudes, refs = refs[0], refs[1:]
    dense, focks, refs = refs[:sets], refs[sets:2 * sets], refs[2 * sets:]
    if has_base:
        refs = refs[1:]
    result, token, coupled, dressed, sems = refs
    token[...] = jnp.zeros_like(token)
    height = amplitudes.shape[0]
    virtuals = amplitudes.shape[1]
    width = dense[0].shape[2]
    slots = [(part, k) for part in range(sets) for k in range(dense[part].shape[0])]
    block = lax.axis_index("blk")
    places = [
        pl.multiple_of(lax.rem(block + by, members) * rows + offset, SUBLANES)
        for by, offset, _ in spans
    ]
    for s, (part, k) in enumerate(slots):
        for first, tile in column_tiles(width, 256):
            coupled[:, s * width + first:s * width + first + tile] = jnp.dot(
                amplitudes[...], dense[part][k, :, first:first + tile],
                preferred_element_type=jnp.float32,
            ).astype(coupled.dtype)
    copies = []
    for t, (first, tile) in enumerate(column_tiles(virtuals, 512)):
        total = jnp.zeros((height, tile), jnp.float32)
        for s, (part, k) in enumerate(slots):
            total = total + jnp.dot(
                coupled[:, s * width:(s + 1) * width], focks[part][k, :, first:first + tile],
                preferred_element_type=jnp.float32,
            )
        dressed[:, first:first + tile] = total.astype(dressed.dtype)
        begin = 0
        for p, (_, _, size) in enumerate(spans):
            copies.append(pltpu.make_async_copy(
                dressed.at[pl.ds(begin, size), pl.ds(first, tile)],
                result.at[pl.ds(places[p], size), pl.ds(first, tile)],
                sems.at[p, t],
            ))
            copies[-1].start()
            begin += size
    for copy in copies:
        copy.wait()


def dress(amplitudes, spans, dense, focks, base, rows, members, out_rows):
    height, virtuals = amplitudes.shape
    width = dense[0].shape[2]
    slots = sum(d.shape[0] for d in dense)
    vmem = pl.BlockSpec(memory_space=pltpu.VMEM)
    anywhere = pl.BlockSpec(memory_space=pl.ANY)
    pinned = [pltpu.with_memory_space_constraint(x, pltpu.VMEM) for x in (*dense, *focks)]
    bases = [] if base is None else [base]
    return pl.pallas_call(
        functools.partial(dress_kernel, spans, rows, members, len(dense), base is not None),
        out_shape=(
            jax.ShapeDtypeStruct((out_rows, virtuals), amplitudes.dtype),
            pltpu.VMEM((8, LANES), jnp.int32),
        ),
        in_specs=[vmem] * (1 + len(pinned)) + [anywhere] * len(bases),
        out_specs=(anywhere, vmem),
        input_output_aliases={} if base is None else {1 + len(pinned): 0},
        scratch_shapes=[
            pltpu.VMEM((height, slots * width), amplitudes.dtype),
            pltpu.VMEM((height, virtuals), amplitudes.dtype),
            pltpu.SemaphoreType.DMA((len(spans), len(column_tiles(virtuals, 512)))),
        ],
        compiler_params=pltpu.CompilerParams(vmem_limit_bytes=16 * MIB),
        cost_estimate=NOTHING,
        name="dress_rows",
    )(amplitudes, *pinned, *bases)


def make_local(blocks, groups):
    members = blocks // groups
    axes = ("blk", "grp")

    def device(hi, lo, grp):
        return (hi * members + lo) * groups + grp

    everyone = [(h, l, g) for h in range(groups) for l in range(members) for g in range(groups)]

    def source_copy(hi, grp):
        if groups != 4:
            return hi
        order = {0: (0, 2, 1, 3), 1: (3, 1, 2, 0), 2: (0, 3, 2, 1), 3: (2, 0, 1, 3)}
        return order[grp][hi]

    to_group = [(device(g, l, source_copy(h, g)), device(h, l, g)) for h, l, g in everyone]

    def to_member(by):
        return [(device(h, (l + by) % members, g), device(h, l, g)) for h, l, g in everyone]

    def to_slot(slot):
        return [(device(h, l, g ^ slot), device(h, l, g)) for h, l, g in everyone]

    def local(amplitudes, hole_panel, virt_fock, irrep_sizes, pair_irreps):
        rows, virtuals = amplitudes.shape
        out_rows = rows * members
        fold = rounded(virtuals // 4, LANES)
        panel = jnp.swapaxes(hole_panel[:, 0, :], 0, 1)
        irrep_sizes = pltpu.with_memory_space_constraint(irrep_sizes, pltpu.HBM)

        own = fold_panel(panel, irrep_sizes, pair_irreps, fold)
        across = lax.ppermute(own, axes, to_slot(2))
        beside = lax.ppermute(own, axes, to_slot(1))

        early = rounded(rows * 2 // 3, SUBLANES) if rows % SUBLANES == 0 else rows
        if early < rows:
            top, low = cut(amplitudes, (early, rows - early))
            top = lax.ppermute(top, axes, to_group)
            lows = [low] + [lax.ppermute(low, axes, to_member(by)) for by in range(1, members)]
        else:
            top = lax.ppermute(amplitudes, axes, to_group)

        fock = pltpu.with_memory_space_constraint(virt_fock, pltpu.HBM)
        near_dense, near_fock = spread((0, 1), (own, beside), fock, irrep_sizes, pair_irreps)
        top = after(top, near_dense)
        tops = [top] + [lax.ppermute(top, axes, to_member(by)) for by in range(1, members)]
        if early < rows:
            lows = lax.ppermute(after(jnp.concatenate(lows), top), axes, to_group)
        across = after(across, near_dense, top)
        both = lax.ppermute(across, axes, to_slot(1))
        far_dense, far_fock = spread((2,), (across,), fock, irrep_sizes, pair_irreps)
        both = after(both, far_dense)
        last_dense, last_fock = spread((3,), (both,), fock, irrep_sizes, pair_irreps)
        dense, focks = (near_dense, far_dense, last_dense), (near_fock, far_fock, last_fock)

        if early < rows:
            result = None
            for by, piece in enumerate(tops):
                spans = [(by, 0, early)]
                result, token = dress(piece, spans, dense, focks, result, rows, members, out_rows)
            spans = [(by, early, rows - early) for by in range(members)]
            lows = after(lows, token)
            result, _ = dress(lows, spans, dense, focks, result, rows, members, out_rows)
        else:
            member = lax.axis_index("blk") % members
            ordered = jnp.roll(jnp.stack(tops), member, axis=0).reshape(out_rows, virtuals)
            spans = [(0, 0, out_rows)]
            result, _ = dress(ordered, spans, dense, focks, None, 0, members, out_rows)
        return result[:, None, :]

    return local


def solution(mesh):
    in_specs = (P("blk", None), P(None, "blk", "grp"), P(), P(), P("blk"))
    out_specs = P("grp", "blk", None)
    local = make_local(mesh.shape["blk"], mesh.shape["grp"])
    return jax.shard_map(local, mesh=mesh, in_specs=in_specs, out_specs=out_specs, check_vma=False)
```

```python
import functools

import jax
import jax.numpy as jnp
from jax import lax
from jax.experimental import pallas as pl
from jax.experimental.pallas import tpu as pltpu
from jax.sharding import PartitionSpec as P

LANES = 128
SUBLANES = 16
MIB = 1 << 20
NOTHING = pl.CostEstimate(flops=0, bytes_accessed=0, transcendentals=0)


def rounded(value, unit):
    return -(-value // unit) * unit


def fill_bounds(sizes, bounds):
    total = jnp.int32(0)
    for r in range(sizes.shape[0]):
        bounds[r] = total
        total = total + sizes[r]
    bounds[sizes.shape[0]] = total


def wanted_range(b, pair, bounds, irreps):
    low, high = jnp.zeros_like(b), jnp.zeros_like(b)
    for r in range(irreps):
        partner = jnp.bitwise_xor(pair[0], r)
        inside = (b >= bounds[r]) & (b < bounds[r + 1])
        low = jnp.where(inside, bounds[partner], low)
        high = jnp.where(inside, bounds[partner + 1], high)
    return low, high


def cut_kernel(whole, *refs):
    pieces, sems = refs[:-1], refs[-1]
    copies, first = [], 0
    for k, piece in enumerate(pieces):
        size = piece.shape[0]
        copies.append(pltpu.make_async_copy(whole.at[pl.ds(first, size)], piece, sems.at[k]))
        copies[-1].start()
        first += size
    for copy in copies:
        copy.wait()


def cut(whole, sizes):
    vmem = pl.BlockSpec(memory_space=pltpu.VMEM)
    return pl.pallas_call(
        cut_kernel,
        out_shape=[pltpu.VMEM((size, whole.shape[1]), whole.dtype) for size in sizes],
        in_specs=[pl.BlockSpec(memory_space=pl.ANY)],
        out_specs=[vmem] * len(sizes),
        scratch_shapes=[pltpu.SemaphoreType.DMA((len(sizes),))],
        compiler_params=pltpu.CompilerParams(vmem_limit_bytes=4 * MIB),
        cost_estimate=NOTHING,
        name="cut_rows",
    )(pltpu.with_memory_space_constraint(whole, pltpu.HBM))


def fold_kernel(chunk, sizes, pair, source, folded, again, panel, bounds, sems):
    quarter, virtuals = panel.shape
    fold = folded.shape[1]
    copies = []
    for k in range(quarter // chunk):
        rows = pl.ds(k * chunk, chunk)
        copies.append(pltpu.make_async_copy(source.at[rows], panel.at[rows], sems.at[k]))
        copies[-1].start()
    fill_bounds(sizes, bounds)
    start = lax.axis_index("grp") * quarter
    step = 32 if chunk % 32 == 0 else SUBLANES
    for k, copy in enumerate(copies):
        copy.wait()

        @pl.loop(0, chunk // step)
        def _(i):
            first = pl.multiple_of(k * chunk + i * step, SUBLANES)
            here = pl.ds(first, step)
            b = start + first + lax.broadcasted_iota(jnp.int32, (step, LANES), 0)
            low, high = wanted_range(b, pair, bounds, sizes.shape[0])
            lane = lax.broadcasted_iota(jnp.int32, (step, LANES), 1)
            low, high = low - lane, high - lane
            for place in range(0, fold, LANES):
                total = jnp.zeros((step, LANES), jnp.float32)
                for c in range(place, virtuals, fold):
                    value = panel[here, c:c + LANES].astype(jnp.float32)
                    total = jnp.where((low <= c) & (high > c), value, total)
                total = total.astype(folded.dtype)
                folded[here, place:place + LANES] = total
                again[here, place:place + LANES] = total


def fold_panel(panel, sizes, pair, fold):
    quarter, virtuals = panel.shape
    chunk = quarter // 5 if quarter % (5 * SUBLANES) == 0 else quarter
    smem = pl.BlockSpec(memory_space=pltpu.SMEM)
    return pl.pallas_call(
        functools.partial(fold_kernel, chunk),
        out_shape=[pltpu.VMEM((quarter, fold), panel.dtype)] * 2,
        in_specs=[smem, smem, pl.BlockSpec(memory_space=pl.ANY)],
        out_specs=[pl.BlockSpec(memory_space=pltpu.VMEM)] * 2,
        scratch_shapes=[
            pltpu.VMEM((quarter, virtuals), panel.dtype),
            pltpu.SMEM((sizes.shape[0] + 1,), jnp.int32),
            pltpu.SemaphoreType.DMA((quarter // chunk,)),
        ],
        compiler_params=pltpu.CompilerParams(vmem_limit_bytes=8 * MIB),
        cost_estimate=NOTHING,
        name="fold_panel",
    )(sizes, pair, pltpu.with_memory_space_constraint(panel, pltpu.HBM))


def spread_kernel(slots, fock_slots, sizes, pair, *refs):
    count, loads = len(slots), len(fock_slots)
    folded, refs = refs[:count], refs[count:]
    if loads:
        (fock, dense, fock_out, bounds, turned, sems) = refs
    else:
        (dense, bounds, turned) = refs
    quarter, fold = folded[0].shape
    virtuals = dense.shape[1]
    width = dense.shape[2]
    group = lax.axis_index("grp")
    copies = []
    for k, slot in enumerate(fock_slots):
        first = pl.multiple_of(jnp.bitwise_xor(group, slot) * quarter, SUBLANES)
        copies.append(pltpu.make_async_copy(
            fock.at[pl.ds(first, quarter)], fock_out.at[k, pl.ds(0, quarter)], sems.at[k]
        ))
        copies[-1].start()
        if width > quarter:
            fock_out[k, quarter:width, :] = jnp.zeros((width - quarter, virtuals), fock_out.dtype)
    fill_bounds(sizes, bounds)
    step = 32
    for k, slot in enumerate(slots):
        values = folded[k][...].astype(jnp.float32)
        if width > quarter:
            values = jnp.concatenate([values, jnp.zeros((width - quarter, fold), jnp.float32)])
        turned[...] = values.T
        start = jnp.bitwise_xor(group, slot) * quarter
        b = start + lax.broadcasted_iota(jnp.int32, (8, width), 1)
        low, high = wanted_range(b, pair, bounds, sizes.shape[0])
        low = jnp.concatenate([low] * (step // 8))
        high = jnp.concatenate([high] * (step // 8))

        @pl.loop(0, virtuals // step)
        def _(i):
            first = pl.multiple_of(i * step, step)
            source = pl.multiple_of(lax.rem(first, fold), step)
            c = first + lax.broadcasted_iota(jnp.int32, (step, width), 0)
            kept = jnp.where((c >= low) & (c < high), turned[pl.ds(source, step), :], 0.0)
            dense[k, pl.ds(first, step), :] = kept.astype(dense.dtype)

    for copy in copies:
        copy.wait()


def spread(slots, folded, sizes, pair, virtuals, fock=None, fock_slots=()):
    quarter, fold = folded[0].shape
    width = rounded(quarter, LANES)
    count, loads = len(slots), len(fock_slots)
    smem = pl.BlockSpec(memory_space=pltpu.SMEM)
    vmem = pl.BlockSpec(memory_space=pltpu.VMEM)
    out_shape = [pltpu.VMEM((count, virtuals, width), folded[0].dtype)]
    scratch = [
        pltpu.SMEM((sizes.shape[0] + 1,), jnp.int32),
        pltpu.VMEM((fold, width), jnp.float32),
    ]
    extra = []
    if loads:
        out_shape.append(pltpu.VMEM((loads, width, virtuals), fock.dtype))
        scratch.append(pltpu.SemaphoreType.DMA((loads,)))
        extra.append(pltpu.with_memory_space_constraint(fock, pltpu.HBM))
    return pl.pallas_call(
        functools.partial(spread_kernel, slots, fock_slots),
        out_shape=out_shape,
        in_specs=[smem, smem] + [vmem] * count + [pl.BlockSpec(memory_space=pl.ANY)] * len(extra),
        out_specs=[vmem] * len(out_shape),
        scratch_shapes=scratch,
        compiler_params=pltpu.CompilerParams(vmem_limit_bytes=8 * MIB),
        cost_estimate=NOTHING,
        name="spread_panel",
    )(sizes, pair, *folded, *extra)


def after(array, *others):
    anywhere = pl.BlockSpec(memory_space=pl.ANY)
    return pl.pallas_call(
        lambda *refs: None,
        out_shape=jax.ShapeDtypeStruct(array.shape, array.dtype),
        in_specs=[anywhere] * (1 + len(others)),
        out_specs=anywhere,
        input_output_aliases={0: 0},
        compiler_params=pltpu.CompilerParams(vmem_limit_bytes=MIB),
        cost_estimate=NOTHING,
        name="after",
    )(array, *others)


def column_tiles(total, tile):
    return [(first, min(tile, total - first)) for first in range(0, total, tile)]


def dress_kernel(spans, rows, members, sets, has_base, *refs):
    amplitudes, fock, refs = refs[0], refs[1], refs[2:]
    dense, refs = refs[:sets], refs[sets:]
    if has_base:
        refs = refs[1:]
    result, token, coupled, dressed, sems = refs
    token[...] = jnp.zeros_like(token)
    height = amplitudes.shape[0]
    virtuals = amplitudes.shape[1]
    width = dense[0].shape[2]
    slots = [(part, k) for part in range(sets) for k in range(dense[part].shape[0])]
    block = lax.axis_index("blk")
    places = [
        pl.multiple_of(lax.rem(block + by, members) * rows + offset, SUBLANES)
        for by, offset, _ in spans
    ]
    for s, (part, k) in enumerate(slots):
        for first, tile in column_tiles(width, 256):
            coupled[:, s * width + first:s * width + first + tile] = jnp.dot(
                amplitudes[...], dense[part][k, :, first:first + tile],
                preferred_element_type=jnp.float32,
            ).astype(coupled.dtype)
    copies = []
    for t, (first, tile) in enumerate(column_tiles(virtuals, 512)):
        total = jnp.zeros((height, tile), jnp.float32)
        for s, (part, k) in enumerate(slots):
            total = total + jnp.dot(
                coupled[:, s * width:(s + 1) * width], fock[s, :, first:first + tile],
                preferred_element_type=jnp.float32,
            )
        dressed[:, first:first + tile] = total.astype(dressed.dtype)
        begin = 0
        for p, (_, _, size) in enumerate(spans):
            copies.append(pltpu.make_async_copy(
                dressed.at[pl.ds(begin, size), pl.ds(first, tile)],
                result.at[pl.ds(places[p], size), pl.ds(first, tile)],
                sems.at[p, t],
            ))
            copies[-1].start()
            begin += size
    for copy in copies:
        copy.wait()


def dress(amplitudes, spans, dense, fock, base, rows, members, out_rows):
    height, virtuals = amplitudes.shape
    width = dense[0].shape[2]
    slots = sum(d.shape[0] for d in dense)
    vmem = pl.BlockSpec(memory_space=pltpu.VMEM)
    anywhere = pl.BlockSpec(memory_space=pl.ANY)
    pinned = [pltpu.with_memory_space_constraint(x, pltpu.VMEM) for x in (fock, *dense)]
    bases = [] if base is None else [base]
    return pl.pallas_call(
        functools.partial(dress_kernel, spans, rows, members, len(dense), base is not None),
        out_shape=(
            jax.ShapeDtypeStruct((out_rows, virtuals), amplitudes.dtype),
            pltpu.VMEM((8, LANES), jnp.int32),
        ),
        in_specs=[vmem] * (1 + len(pinned)) + [anywhere] * len(bases),
        out_specs=(anywhere, vmem),
        input_output_aliases={} if base is None else {1 + len(pinned): 0},
        scratch_shapes=[
            pltpu.VMEM((height, slots * width), amplitudes.dtype),
            pltpu.VMEM((height, virtuals), amplitudes.dtype),
            pltpu.SemaphoreType.DMA((len(spans), len(column_tiles(virtuals, 512)))),
        ],
        compiler_params=pltpu.CompilerParams(vmem_limit_bytes=16 * MIB),
        cost_estimate=NOTHING,
        name="dress_rows",
    )(amplitudes, *pinned, *bases)


def make_local(blocks, groups):
    members = blocks // groups
    axes = ("blk", "grp")

    def device(hi, lo, grp):
        return (hi * members + lo) * groups + grp

    everyone = [(h, l, g) for h in range(groups) for l in range(members) for g in range(groups)]

    def source_copy(hi, grp):
        if groups != 4:
            return hi
        order = {0: (0, 2, 1, 3), 1: (3, 1, 2, 0), 2: (0, 3, 2, 1), 3: (2, 0, 1, 3)}
        return order[grp][hi]

    to_group = [(device(g, l, source_copy(h, g)), device(h, l, g)) for h, l, g in everyone]

    def to_member(by):
        return [(device(h, (l + by) % members, g), device(h, l, g)) for h, l, g in everyone]

    def to_slot(slot):
        return [(device(h, l, g ^ slot), device(h, l, g)) for h, l, g in everyone]

    def local(amplitudes, hole_panel, virt_fock, irrep_sizes, pair_irreps):
        rows, virtuals = amplitudes.shape
        out_rows = rows * members
        fold = rounded(virtuals // 4, LANES)
        panel = jnp.swapaxes(hole_panel[:, 0, :], 0, 1)
        irrep_sizes = pltpu.with_memory_space_constraint(irrep_sizes, pltpu.HBM)

        own, own_again = fold_panel(panel, irrep_sizes, pair_irreps, fold)
        across = lax.ppermute(own, axes, to_slot(2))

        early = rounded(rows * 3 // 5, SUBLANES) if rows % SUBLANES == 0 else rows
        if early < rows:
            top, low = cut(amplitudes, (early, rows - early))
            top = lax.ppermute(top, axes, to_group)
            lows = [low] + [lax.ppermute(low, axes, to_member(by)) for by in range(1, members)]
            lows = jnp.concatenate(lows)
        else:
            top = lax.ppermute(amplitudes, axes, to_group)

        spread_one = lambda slot, folded, *fock: spread(
            (slot,), (folded,), irrep_sizes, pair_irreps, virtuals, *fock
        )
        first, fock = spread_one(0, own, virt_fock, range(groups))
        if early < rows:
            top = after(top, first)
            lows = after(lows, top)
            lows = lax.ppermute(lows, axes, to_group)
        tops = [top] + [lax.ppermute(top, axes, to_member(by)) for by in range(1, members)]
        beside = lax.ppermute(after(own_again, across), axes, to_slot(1))
        both = lax.ppermute(across, axes, to_slot(1))
        third, = spread_one(2, across)
        second, = spread_one(1, after(beside, third))
        fourth, = spread_one(3, after(both, third))
        dense = (first, second, third, fourth)

        if early < rows:
            result = None
            for by, piece in enumerate(tops):
                spans = [(by, 0, early)]
                result, token = dress(piece, spans, dense, fock, result, rows, members, out_rows)
            spans = [(by, early, rows - early) for by in range(members)]
            lows = after(lows, token)
            result, _ = dress(lows, spans, dense, fock, result, rows, members, out_rows)
        else:
            member = lax.axis_index("blk") % members
            ordered = jnp.roll(jnp.stack(tops), member, axis=0).reshape(out_rows, virtuals)
            spans = [(0, 0, out_rows)]
            result, _ = dress(ordered, spans, dense, fock, None, 0, members, out_rows)
        return result[:, None, :]

    return local


def solution(mesh):
    in_specs = (P("blk", None), P(None, "blk", "grp"), P(), P(), P("blk"))
    out_specs = P("grp", "blk", None)
    local = make_local(mesh.shape["blk"], mesh.shape["grp"])
    return jax.shard_map(local, mesh=mesh, in_specs=in_specs, out_specs=out_specs, check_vma=False)
```

```python
import functools

import jax
import jax.numpy as jnp
from jax import lax
from jax.experimental import pallas as pl
from jax.experimental.pallas import tpu as pltpu
from jax.sharding import PartitionSpec as P

LANES = 128
SUBLANES = 16
MIB = 1 << 20
NOTHING = pl.CostEstimate(flops=0, bytes_accessed=0, transcendentals=0)


def rounded(value, unit):
    return -(-value // unit) * unit


def fill_bounds(sizes, bounds):
    total = jnp.int32(0)
    for r in range(sizes.shape[0]):
        bounds[r] = total
        total = total + sizes[r]
    bounds[sizes.shape[0]] = total


def wanted_range(b, pair, bounds, irreps):
    low, high = jnp.zeros_like(b), jnp.zeros_like(b)
    for r in range(irreps):
        partner = jnp.bitwise_xor(pair[0], r)
        inside = (b >= bounds[r]) & (b < bounds[r + 1])
        low = jnp.where(inside, bounds[partner], low)
        high = jnp.where(inside, bounds[partner + 1], high)
    return low, high


def cut_kernel(whole, *refs):
    pieces, sems = refs[:-1], refs[-1]
    copies, first = [], 0
    for k, piece in enumerate(pieces):
        size = piece.shape[0]
        copies.append(pltpu.make_async_copy(whole.at[pl.ds(first, size)], piece, sems.at[k]))
        copies[-1].start()
        first += size
    for copy in copies:
        copy.wait()


def cut(whole, sizes):
    vmem = pl.BlockSpec(memory_space=pltpu.VMEM)
    return pl.pallas_call(
        cut_kernel,
        out_shape=[pltpu.VMEM((size, whole.shape[1]), whole.dtype) for size in sizes],
        in_specs=[pl.BlockSpec(memory_space=pl.ANY)],
        out_specs=[vmem] * len(sizes),
        scratch_shapes=[pltpu.SemaphoreType.DMA((len(sizes),))],
        compiler_params=pltpu.CompilerParams(vmem_limit_bytes=4 * MIB),
        cost_estimate=NOTHING,
        name="cut_rows",
    )(pltpu.with_memory_space_constraint(whole, pltpu.HBM))


def fold_kernel(chunk, sizes, pair, source, folded, again, panel, bounds, sems):
    quarter, virtuals = panel.shape
    fold = folded.shape[1]
    copies = []
    for k in range(quarter // chunk):
        rows = pl.ds(k * chunk, chunk)
        copies.append(pltpu.make_async_copy(source.at[rows], panel.at[rows], sems.at[k]))
        copies[-1].start()
    fill_bounds(sizes, bounds)
    start = lax.axis_index("grp") * quarter
    step = 32 if chunk % 32 == 0 else SUBLANES
    for k, copy in enumerate(copies):
        copy.wait()

        @pl.loop(0, chunk // step, unroll=True)
        def _(i):
            first = pl.multiple_of(k * chunk + i * step, SUBLANES)
            here = pl.ds(first, step)
            b = start + first + lax.broadcasted_iota(jnp.int32, (step, LANES), 0)
            low, high = wanted_range(b, pair, bounds, sizes.shape[0])
            lane = lax.broadcasted_iota(jnp.int32, (step, LANES), 1)
            low, high = low - lane, high - lane
            for place in range(0, fold, LANES):
                total = jnp.zeros((step, LANES), jnp.float32)
                for c in range(place, virtuals, fold):
                    value = panel[here, c:c + LANES].astype(jnp.float32)
                    total = jnp.where((low <= c) & (high > c), value, total)
                total = total.astype(folded.dtype)
                folded[here, place:place + LANES] = total
                again[here, place:place + LANES] = total


def fold_panel(panel, sizes, pair, fold):
    quarter, virtuals = panel.shape
    chunk = quarter // 5 if quarter % (5 * SUBLANES) == 0 else quarter
    smem = pl.BlockSpec(memory_space=pltpu.SMEM)
    return pl.pallas_call(
        functools.partial(fold_kernel, chunk),
        out_shape=[pltpu.VMEM((quarter, fold), panel.dtype)] * 2,
        in_specs=[smem, smem, pl.BlockSpec(memory_space=pl.ANY)],
        out_specs=[pl.BlockSpec(memory_space=pltpu.VMEM)] * 2,
        scratch_shapes=[
            pltpu.VMEM((quarter, virtuals), panel.dtype),
            pltpu.SMEM((sizes.shape[0] + 1,), jnp.int32),
            pltpu.SemaphoreType.DMA((quarter // chunk,)),
        ],
        compiler_params=pltpu.CompilerParams(vmem_limit_bytes=8 * MIB),
        cost_estimate=NOTHING,
        name="fold_panel",
    )(sizes, pair, pltpu.with_memory_space_constraint(panel, pltpu.HBM))


def spread_kernel(slots, fock_slots, sizes, pair, *refs):
    count, loads = len(slots), len(fock_slots)
    folded, refs = refs[:count], refs[count:]
    if loads:
        (fock, dense, fock_out, bounds, turned, sems) = refs
    else:
        (dense, bounds, turned) = refs
    quarter, fold = folded[0].shape
    virtuals = dense.shape[1]
    width = dense.shape[2]
    group = lax.axis_index("grp")
    copies = []
    for k, slot in enumerate(fock_slots):
        first = pl.multiple_of(jnp.bitwise_xor(group, slot) * quarter, SUBLANES)
        copies.append(pltpu.make_async_copy(
            fock.at[pl.ds(first, quarter)], fock_out.at[k, pl.ds(0, quarter)], sems.at[k]
        ))
        copies[-1].start()
        if width > quarter:
            fock_out[k, quarter:width, :] = jnp.zeros((width - quarter, virtuals), fock_out.dtype)
    fill_bounds(sizes, bounds)
    step = 32
    for k, slot in enumerate(slots):
        values = folded[k][...].astype(jnp.float32)
        if width > quarter:
            values = jnp.concatenate([values, jnp.zeros((width - quarter, fold), jnp.float32)])
        turned[...] = values.T
        start = jnp.bitwise_xor(group, slot) * quarter
        b = start + lax.broadcasted_iota(jnp.int32, (8, width), 1)
        low, high = wanted_range(b, pair, bounds, sizes.shape[0])
        low = jnp.concatenate([low] * (step // 8))
        high = jnp.concatenate([high] * (step // 8))

        @pl.loop(0, virtuals // step, unroll=4)
        def _(i):
            first = pl.multiple_of(i * step, step)
            source = pl.multiple_of(lax.rem(first, fold), step)
            c = first + lax.broadcasted_iota(jnp.int32, (step, width), 0)
            kept = jnp.where((c >= low) & (c < high), turned[pl.ds(source, step), :], 0.0)
            dense[k, pl.ds(first, step), :] = kept.astype(dense.dtype)

    for copy in copies:
        copy.wait()


def spread(slots, folded, sizes, pair, virtuals, fock=None, fock_slots=()):
    quarter, fold = folded[0].shape
    width = rounded(quarter, LANES)
    count, loads = len(slots), len(fock_slots)
    smem = pl.BlockSpec(memory_space=pltpu.SMEM)
    vmem = pl.BlockSpec(memory_space=pltpu.VMEM)
    out_shape = [pltpu.VMEM((count, virtuals, width), folded[0].dtype)]
    scratch = [
        pltpu.SMEM((sizes.shape[0] + 1,), jnp.int32),
        pltpu.VMEM((fold, width), jnp.float32),
    ]
    extra = []
    if loads:
        out_shape.append(pltpu.VMEM((loads, width, virtuals), fock.dtype))
        scratch.append(pltpu.SemaphoreType.DMA((loads,)))
        extra.append(pltpu.with_memory_space_constraint(fock, pltpu.HBM))
    return pl.pallas_call(
        functools.partial(spread_kernel, slots, fock_slots),
        out_shape=out_shape,
        in_specs=[smem, smem] + [vmem] * count + [pl.BlockSpec(memory_space=pl.ANY)] * len(extra),
        out_specs=[vmem] * len(out_shape),
        scratch_shapes=scratch,
        compiler_params=pltpu.CompilerParams(vmem_limit_bytes=8 * MIB),
        cost_estimate=NOTHING,
        name="spread_panel",
    )(sizes, pair, *folded, *extra)


def after(array, *others):
    anywhere = pl.BlockSpec(memory_space=pl.ANY)
    return pl.pallas_call(
        lambda *refs: None,
        out_shape=jax.ShapeDtypeStruct(array.shape, array.dtype),
        in_specs=[anywhere] * (1 + len(others)),
        out_specs=anywhere,
        input_output_aliases={0: 0},
        compiler_params=pltpu.CompilerParams(vmem_limit_bytes=MIB),
        cost_estimate=NOTHING,
        name="after",
    )(array, *others)


def column_tiles(total, tile):
    return [(first, min(tile, total - first)) for first in range(0, total, tile)]


def dress_kernel(spans, rows, members, sets, has_base, *refs):
    amplitudes, fock, refs = refs[0], refs[1], refs[2:]
    dense, refs = refs[:sets], refs[sets:]
    if has_base:
        refs = refs[1:]
    result, token, coupled, dressed, sems = refs
    token[...] = jnp.zeros_like(token)
    height = amplitudes.shape[0]
    virtuals = amplitudes.shape[1]
    width = dense[0].shape[2]
    slots = [(part, k) for part in range(sets) for k in range(dense[part].shape[0])]
    block = lax.axis_index("blk")
    places = [
        pl.multiple_of(lax.rem(block + by, members) * rows + offset, SUBLANES)
        for by, offset, _ in spans
    ]
    for s, (part, k) in enumerate(slots):
        for first, tile in column_tiles(width, 256):
            coupled[:, s * width + first:s * width + first + tile] = jnp.dot(
                amplitudes[...], dense[part][k, :, first:first + tile],
                preferred_element_type=jnp.float32,
            ).astype(coupled.dtype)
    copies = []
    for t, (first, tile) in enumerate(column_tiles(virtuals, 512)):
        total = jnp.zeros((height, tile), jnp.float32)
        for s, (part, k) in enumerate(slots):
            total = total + jnp.dot(
                coupled[:, s * width:(s + 1) * width], fock[s, :, first:first + tile],
                preferred_element_type=jnp.float32,
            )
        dressed[:, first:first + tile] = total.astype(dressed.dtype)
        begin = 0
        for p, (_, _, size) in enumerate(spans):
            copies.append(pltpu.make_async_copy(
                dressed.at[pl.ds(begin, size), pl.ds(first, tile)],
                result.at[pl.ds(places[p], size), pl.ds(first, tile)],
                sems.at[p, t],
            ))
            copies[-1].start()
            begin += size
    for copy in copies:
        copy.wait()


def dress(amplitudes, spans, dense, fock, base, rows, members, out_rows):
    height, virtuals = amplitudes.shape
    width = dense[0].shape[2]
    slots = sum(d.shape[0] for d in dense)
    vmem = pl.BlockSpec(memory_space=pltpu.VMEM)
    anywhere = pl.BlockSpec(memory_space=pl.ANY)
    pinned = [pltpu.with_memory_space_constraint(x, pltpu.VMEM) for x in (fock, *dense)]
    bases = [] if base is None else [base]
    return pl.pallas_call(
        functools.partial(dress_kernel, spans, rows, members, len(dense), base is not None),
        out_shape=(
            jax.ShapeDtypeStruct((out_rows, virtuals), amplitudes.dtype),
            pltpu.VMEM((8, LANES), jnp.int32),
        ),
        in_specs=[vmem] * (1 + len(pinned)) + [anywhere] * len(bases),
        out_specs=(anywhere, vmem),
        input_output_aliases={} if base is None else {1 + len(pinned): 0},
        scratch_shapes=[
            pltpu.VMEM((height, slots * width), amplitudes.dtype),
            pltpu.VMEM((height, virtuals), amplitudes.dtype),
            pltpu.SemaphoreType.DMA((len(spans), len(column_tiles(virtuals, 512)))),
        ],
        compiler_params=pltpu.CompilerParams(vmem_limit_bytes=16 * MIB),
        cost_estimate=NOTHING,
        name="dress_rows",
    )(amplitudes, *pinned, *bases)


def make_local(blocks, groups):
    members = blocks // groups
    axes = ("blk", "grp")

    def device(hi, lo, grp):
        return (hi * members + lo) * groups + grp

    everyone = [(h, l, g) for h in range(groups) for l in range(members) for g in range(groups)]

    def source_copy(hi, grp):
        if groups != 4:
            return hi
        order = {0: (0, 2, 1, 3), 1: (3, 1, 2, 0), 2: (0, 3, 2, 1), 3: (2, 0, 1, 3)}
        return order[grp][hi]

    to_group = [(device(g, l, source_copy(h, g)), device(h, l, g)) for h, l, g in everyone]

    def to_member(by):
        return [(device(h, (l + by) % members, g), device(h, l, g)) for h, l, g in everyone]

    def to_slot(slot):
        return [(device(h, l, g ^ slot), device(h, l, g)) for h, l, g in everyone]

    def local(amplitudes, hole_panel, virt_fock, irrep_sizes, pair_irreps):
        rows, virtuals = amplitudes.shape
        out_rows = rows * members
        fold = rounded(virtuals // 4, LANES)
        panel = jnp.swapaxes(hole_panel[:, 0, :], 0, 1)
        irrep_sizes = pltpu.with_memory_space_constraint(irrep_sizes, pltpu.HBM)

        own, own_again = fold_panel(panel, irrep_sizes, pair_irreps, fold)
        across = lax.ppermute(own, axes, to_slot(2))

        early = rounded(rows * 2 // 3, SUBLANES) if rows % SUBLANES == 0 else rows
        if early < rows:
            top, low = cut(amplitudes, (early, rows - early))
            top = lax.ppermute(top, axes, to_group)
            lows = [low] + [lax.ppermute(low, axes, to_member(by)) for by in range(1, members)]
            lows = jnp.concatenate(lows)
        else:
            top = lax.ppermute(amplitudes, axes, to_group)

        spread_one = lambda slot, folded, *fock: spread(
            (slot,), (folded,), irrep_sizes, pair_irreps, virtuals, *fock
        )
        first, fock = spread_one(0, own, virt_fock, range(groups))
        if early < rows:
            top = after(top, first)
            lows = after(lows, top)
            lows = lax.ppermute(lows, axes, to_group)
        tops = [top] + [lax.ppermute(top, axes, to_member(by)) for by in range(1, members)]
        beside = lax.ppermute(own_again, axes, to_slot(1))
        second, = spread_one(1, beside)
        across = after(across, second)
        both = lax.ppermute(across, axes, to_slot(1))
        third, = spread_one(2, across)
        fourth, = spread_one(3, after(both, third))
        dense = (first, second, third, fourth)

        if early < rows:
            result = None
            for by, piece in enumerate(tops):
                spans = [(by, 0, early)]
                result, token = dress(piece, spans, dense, fock, result, rows, members, out_rows)
            spans = [(by, early, rows - early) for by in range(members)]
            lows = after(lows, token)
            result, _ = dress(lows, spans, dense, fock, result, rows, members, out_rows)
        else:
            member = lax.axis_index("blk") % members
            ordered = jnp.roll(jnp.stack(tops), member, axis=0).reshape(out_rows, virtuals)
            spans = [(0, 0, out_rows)]
            result, _ = dress(ordered, spans, dense, fock, None, 0, members, out_rows)
        return result[:, None, :]

    return local


def solution(mesh):
    in_specs = (P("blk", None), P(None, "blk", "grp"), P(), P(), P("blk"))
    out_specs = P("grp", "blk", None)
    local = make_local(mesh.shape["blk"], mesh.shape["grp"])
    return jax.shard_map(local, mesh=mesh, in_specs=in_specs, out_specs=out_specs, check_vma=False)
```

```python
import functools

import jax
import jax.numpy as jnp
from jax import lax
from jax.experimental import pallas as pl
from jax.experimental.pallas import tpu as pltpu
from jax.sharding import PartitionSpec as P

LANES = 128
SUBLANES = 16
MIB = 1 << 20
NOTHING = pl.CostEstimate(flops=0, bytes_accessed=0, transcendentals=0)


def rounded(value, unit):
    return -(-value // unit) * unit


def fill_bounds(sizes, bounds):
    total = jnp.int32(0)
    for r in range(sizes.shape[0]):
        bounds[r] = total
        total = total + sizes[r]
    bounds[sizes.shape[0]] = total


def wanted_range(b, pair, bounds, irreps):
    low, high = jnp.zeros_like(b), jnp.zeros_like(b)
    for r in range(irreps):
        partner = jnp.bitwise_xor(pair[0], r)
        inside = (b >= bounds[r]) & (b < bounds[r + 1])
        low = jnp.where(inside, bounds[partner], low)
        high = jnp.where(inside, bounds[partner + 1], high)
    return low, high


def cut_kernel(whole, *refs):
    pieces, sems = refs[:-1], refs[-1]
    copies, first = [], 0
    for k, piece in enumerate(pieces):
        size = piece.shape[0]
        copies.append(pltpu.make_async_copy(whole.at[pl.ds(first, size)], piece, sems.at[k]))
        copies[-1].start()
        first += size
    for copy in copies:
        copy.wait()


def cut(whole, sizes):
    vmem = pl.BlockSpec(memory_space=pltpu.VMEM)
    return pl.pallas_call(
        cut_kernel,
        out_shape=[pltpu.VMEM((size, whole.shape[1]), whole.dtype) for size in sizes],
        in_specs=[pl.BlockSpec(memory_space=pl.ANY)],
        out_specs=[vmem] * len(sizes),
        scratch_shapes=[pltpu.SemaphoreType.DMA((len(sizes),))],
        compiler_params=pltpu.CompilerParams(vmem_limit_bytes=4 * MIB),
        cost_estimate=NOTHING,
        name="cut_rows",
    )(pltpu.with_memory_space_constraint(whole, pltpu.HBM))


def fold_kernel(chunk, sizes, pair, source, folded, again, panel, bounds, sems):
    quarter, virtuals = panel.shape
    fold = folded.shape[1]
    copies = []
    for k in range(quarter // chunk):
        rows = pl.ds(k * chunk, chunk)
        copies.append(pltpu.make_async_copy(source.at[rows], panel.at[rows], sems.at[k]))
        copies[-1].start()
    fill_bounds(sizes, bounds)
    start = lax.axis_index("grp") * quarter
    step = 32 if chunk % 32 == 0 else SUBLANES
    for k, copy in enumerate(copies):
        copy.wait()

        @pl.loop(0, chunk // step, unroll=True)
        def _(i):
            first = pl.multiple_of(k * chunk + i * step, SUBLANES)
            here = pl.ds(first, step)
            b = start + first + lax.broadcasted_iota(jnp.int32, (step, LANES), 0)
            low, high = wanted_range(b, pair, bounds, sizes.shape[0])
            lane = lax.broadcasted_iota(jnp.int32, (step, LANES), 1)
            low, high = low - lane, high - lane
            for place in range(0, fold, LANES):
                total = jnp.zeros((step, LANES), jnp.float32)
                for c in range(place, virtuals, fold):
                    value = panel[here, c:c + LANES].astype(jnp.float32)
                    total = jnp.where((low <= c) & (high > c), value, total)
                total = total.astype(folded.dtype)
                folded[here, place:place + LANES] = total
                again[here, place:place + LANES] = total


def fold_panel(panel, sizes, pair, fold):
    quarter, virtuals = panel.shape
    chunk = quarter // 5 if quarter % (5 * SUBLANES) == 0 else quarter
    smem = pl.BlockSpec(memory_space=pltpu.SMEM)
    return pl.pallas_call(
        functools.partial(fold_kernel, chunk),
        out_shape=[pltpu.VMEM((quarter, fold), panel.dtype)] * 2,
        in_specs=[smem, smem, pl.BlockSpec(memory_space=pl.ANY)],
        out_specs=[pl.BlockSpec(memory_space=pltpu.VMEM)] * 2,
        scratch_shapes=[
            pltpu.VMEM((quarter, virtuals), panel.dtype),
            pltpu.SMEM((sizes.shape[0] + 1,), jnp.int32),
            pltpu.SemaphoreType.DMA((quarter // chunk,)),
        ],
        compiler_params=pltpu.CompilerParams(vmem_limit_bytes=8 * MIB),
        cost_estimate=NOTHING,
        name="fold_panel",
    )(sizes, pair, pltpu.with_memory_space_constraint(panel, pltpu.HBM))


def spread_kernel(slot, groups, first, sizes, pair, folded, other, *refs):
    if first:
        dense, fock_out, bounds, turned, sems = refs
    else:
        dense, bounds, turned = refs
    quarter, fold = folded.shape
    virtuals, total = dense.shape
    width = total // groups
    group = lax.axis_index("grp")
    copies = []
    if first:
        for k in range(groups):
            start = pl.multiple_of(jnp.bitwise_xor(group, k) * quarter, SUBLANES)
            copies.append(pltpu.make_async_copy(
                other.at[pl.ds(start, quarter)], fock_out.at[pl.ds(k * width, quarter)], sems.at[k]
            ))
            copies[-1].start()
            if width > quarter:
                fock_out[k * width + quarter:(k + 1) * width, :] = jnp.zeros(
                    (width - quarter, virtuals), fock_out.dtype
                )
    fill_bounds(sizes, bounds)
    step = 32
    values = folded[...].astype(jnp.float32)
    if width > quarter:
        values = jnp.concatenate([values, jnp.zeros((width - quarter, fold), jnp.float32)])
    turned[...] = values.T
    start = jnp.bitwise_xor(group, slot) * quarter
    b = start + lax.broadcasted_iota(jnp.int32, (8, width), 1)
    low, high = wanted_range(b, pair, bounds, sizes.shape[0])
    low = jnp.concatenate([low] * (step // 8))
    high = jnp.concatenate([high] * (step // 8))

    @pl.loop(0, virtuals // step, unroll=4)
    def _(i):
        row = pl.multiple_of(i * step, step)
        source = pl.multiple_of(lax.rem(row, fold), step)
        c = row + lax.broadcasted_iota(jnp.int32, (step, width), 0)
        kept = jnp.where((c >= low) & (c < high), turned[pl.ds(source, step), :], 0.0)
        dense[pl.ds(row, step), slot * width:(slot + 1) * width] = kept.astype(dense.dtype)

    for copy in copies:
        copy.wait()


def spread(slot, groups, folded, sizes, pair, *, fock=None, dense=None):
    quarter, fold = folded.shape
    first = dense is None
    virtuals = fock.shape[0] if first else dense.shape[0]
    width = rounded(quarter, LANES)
    smem = pl.BlockSpec(memory_space=pltpu.SMEM)
    vmem = pl.BlockSpec(memory_space=pltpu.VMEM)
    out_shape = [pltpu.VMEM((virtuals, groups * width), folded.dtype)]
    scratch = [
        pltpu.SMEM((sizes.shape[0] + 1,), jnp.int32),
        pltpu.VMEM((fold, width), jnp.float32),
    ]
    if first:
        out_shape.append(pltpu.VMEM((groups * width, virtuals), fock.dtype))
        scratch.append(pltpu.SemaphoreType.DMA((groups,)))
        other = pltpu.with_memory_space_constraint(fock, pltpu.HBM)
    else:
        other = pltpu.with_memory_space_constraint(dense, pltpu.VMEM)
    return pl.pallas_call(
        functools.partial(spread_kernel, slot, groups, first),
        out_shape=out_shape,
        in_specs=[smem, smem, vmem, pl.BlockSpec(memory_space=pl.ANY)],
        out_specs=[vmem] * len(out_shape),
        input_output_aliases={} if first else {3: 0},
        scratch_shapes=scratch,
        compiler_params=pltpu.CompilerParams(vmem_limit_bytes=8 * MIB),
        cost_estimate=NOTHING,
        name="spread_panel",
    )(sizes, pair, folded, other)


def after(array, *others):
    anywhere = pl.BlockSpec(memory_space=pl.ANY)
    return pl.pallas_call(
        lambda *refs: None,
        out_shape=jax.ShapeDtypeStruct(array.shape, array.dtype),
        in_specs=[anywhere] * (1 + len(others)),
        out_specs=anywhere,
        input_output_aliases={0: 0},
        compiler_params=pltpu.CompilerParams(vmem_limit_bytes=MIB),
        cost_estimate=NOTHING,
        name="after",
    )(array, *others)


def column_tiles(total, tile):
    return [(first, min(tile, total - first)) for first in range(0, total, tile)]


def dress_kernel(spans, rows, members, has_base, amplitudes, dense, fock, *refs):
    if has_base:
        refs = refs[1:]
    result, token, coupled, dressed, sems = refs
    token[...] = jnp.zeros_like(token)
    virtuals, total = dense.shape
    block = lax.axis_index("blk")
    places = [
        pl.multiple_of(lax.rem(block + by, members) * rows + offset, SUBLANES)
        for by, offset, _ in spans
    ]
    for first, tile in column_tiles(total, 512):
        coupled[:, first:first + tile] = jnp.dot(
            amplitudes[...], dense[:, first:first + tile], preferred_element_type=jnp.float32
        ).astype(coupled.dtype)
    copies = []
    for t, (first, tile) in enumerate(column_tiles(virtuals, 512)):
        dressed[:, first:first + tile] = jnp.dot(
            coupled[...], fock[:, first:first + tile], preferred_element_type=jnp.float32
        ).astype(dressed.dtype)
        begin = 0
        for p, (_, _, size) in enumerate(spans):
            copies.append(pltpu.make_async_copy(
                dressed.at[pl.ds(begin, size), pl.ds(first, tile)],
                result.at[pl.ds(places[p], size), pl.ds(first, tile)],
                sems.at[p, t],
            ))
            copies[-1].start()
            begin += size
    for copy in copies:
        copy.wait()


def dress(amplitudes, spans, dense, fock, base, rows, members, out_rows):
    height, virtuals = amplitudes.shape
    vmem = pl.BlockSpec(memory_space=pltpu.VMEM)
    anywhere = pl.BlockSpec(memory_space=pl.ANY)
    pinned = [pltpu.with_memory_space_constraint(x, pltpu.VMEM) for x in (dense, fock)]
    bases = [] if base is None else [base]
    return pl.pallas_call(
        functools.partial(dress_kernel, spans, rows, members, base is not None),
        out_shape=(
            jax.ShapeDtypeStruct((out_rows, virtuals), amplitudes.dtype),
            pltpu.VMEM((8, LANES), jnp.int32),
        ),
        in_specs=[vmem] * 3 + [anywhere] * len(bases),
        out_specs=(anywhere, vmem),
        input_output_aliases={} if base is None else {3: 0},
        scratch_shapes=[
            pltpu.VMEM((height, dense.shape[1]), amplitudes.dtype),
            pltpu.VMEM((height, virtuals), amplitudes.dtype),
            pltpu.SemaphoreType.DMA((len(spans), len(column_tiles(virtuals, 512)))),
        ],
        compiler_params=pltpu.CompilerParams(vmem_limit_bytes=16 * MIB),
        cost_estimate=NOTHING,
        name="dress_rows",
    )(amplitudes, *pinned, *bases)


def make_local(blocks, groups):
    members = blocks // groups
    axes = ("blk", "grp")

    def device(hi, lo, grp):
        return (hi * members + lo) * groups + grp

    everyone = [(h, l, g) for h in range(groups) for l in range(members) for g in range(groups)]

    if groups == 4:
        copies = ((None, 1, 0, 3), (0, None, 2, 1), (0, 2, None, 3), (2, 0, 3, None))
    else:
        copies = [[None if h == g else h for h in range(groups)] for g in range(groups)]
    to_group = [
        (device(g, l, copies[g][h]), device(h, l, g)) for h, l, g in everyone if h != g
    ]

    def to_member(by):
        return [(device(h, (l + by) % members, g), device(h, l, g)) for h, l, g in everyone]

    def to_slot(slot):
        return [(device(h, l, g ^ slot), device(h, l, g)) for h, l, g in everyone]

    def local(amplitudes, hole_panel, virt_fock, irrep_sizes, pair_irreps):
        rows, virtuals = amplitudes.shape
        out_rows = rows * members
        fold = rounded(virtuals // 4, LANES)
        panel = jnp.swapaxes(hole_panel[:, 0, :], 0, 1)
        irrep_sizes = pltpu.with_memory_space_constraint(irrep_sizes, pltpu.HBM)

        own, own_again = fold_panel(panel, irrep_sizes, pair_irreps, fold)
        across = lax.ppermute(own, axes, to_slot(2))
        beside = lax.ppermute(own_again, axes, to_slot(1))

        owner = lax.axis_index("blk") // members == lax.axis_index("grp")

        def arrived(piece, kept):
            return jnp.where(owner, kept, piece)

        early = rounded(rows * 2 // 3, SUBLANES) if rows % SUBLANES == 0 else rows
        if early < rows:
            top, low = cut(amplitudes, (early, rows - early))
            lows = [low] + [lax.ppermute(low, axes, to_member(by)) for by in range(1, members)]
            lows = jnp.concatenate(lows)
        else:
            top = amplitudes
        top = arrived(lax.ppermute(top, axes, to_group), top)

        spread_one = functools.partial(spread, sizes=irrep_sizes, pair=pair_irreps)
        dense, fock = spread_one(0, groups, own, fock=virt_fock)
        top = after(top, fock)
        if early < rows:
            lows = after(lows, top)
            late = lax.ppermute(lows, axes, to_group)
        tops = [top] + [lax.ppermute(top, axes, to_member(by)) for by in range(1, members)]
        dense, = spread_one(1, groups, beside, dense=dense)
        across = after(across, dense)
        both = lax.ppermute(across, axes, to_slot(1))
        dense, = spread_one(2, groups, across, dense=dense)
        dense, = spread_one(3, groups, both, dense=dense)

        if early < rows:
            result = None
            for by, piece in enumerate(tops):
                spans = [(by, 0, early)]
                result, token = dress(piece, spans, dense, fock, result, rows, members, out_rows)
            spans = [(by, early, rows - early) for by in range(members)]
            lows = arrived(after(late, token), lows)
            result, _ = dress(lows, spans, dense, fock, result, rows, members, out_rows)
        else:
            member = lax.axis_index("blk") % members
            ordered = jnp.roll(jnp.stack(tops), member, axis=0).reshape(out_rows, virtuals)
            spans = [(0, 0, out_rows)]
            result, _ = dress(ordered, spans, dense, fock, None, 0, members, out_rows)
        return result[:, None, :]

    return local


def solution(mesh):
    in_specs = (P("blk", None), P(None, "blk", "grp"), P(), P(), P("blk"))
    out_specs = P("grp", "blk", None)
    local = make_local(mesh.shape["blk"], mesh.shape["grp"])
    return jax.shard_map(local, mesh=mesh, in_specs=in_specs, out_specs=out_specs, check_vma=False)
```

```python
import functools

import jax
import jax.numpy as jnp
from jax import lax
from jax.experimental import pallas as pl
from jax.experimental.pallas import tpu as pltpu
from jax.sharding import PartitionSpec as P

LANES = 128
SUBLANES = 16
MIB = 1 << 20
NOTHING = pl.CostEstimate(flops=0, bytes_accessed=0, transcendentals=0)


def rounded(value, unit):
    return -(-value // unit) * unit


def fill_bounds(sizes, bounds):
    total = jnp.int32(0)
    for r in range(sizes.shape[0]):
        bounds[r] = total
        total = total + sizes[r]
    bounds[sizes.shape[0]] = total


def wanted_range(b, pair, bounds, irreps):
    low, high = jnp.zeros_like(b), jnp.zeros_like(b)
    for r in range(irreps):
        partner = jnp.bitwise_xor(pair[0], r)
        inside = (b >= bounds[r]) & (b < bounds[r + 1])
        low = jnp.where(inside, bounds[partner], low)
        high = jnp.where(inside, bounds[partner + 1], high)
    return low, high


def cut_kernel(whole, *refs):
    pieces, sems = refs[:-1], refs[-1]
    copies, first = [], 0
    for k, piece in enumerate(pieces):
        size = piece.shape[0]
        copies.append(pltpu.make_async_copy(whole.at[pl.ds(first, size)], piece, sems.at[k]))
        copies[-1].start()
        first += size
    for copy in copies:
        copy.wait()


def cut(whole, sizes):
    vmem = pl.BlockSpec(memory_space=pltpu.VMEM)
    return pl.pallas_call(
        cut_kernel,
        out_shape=[pltpu.VMEM((size, whole.shape[1]), whole.dtype) for size in sizes],
        in_specs=[pl.BlockSpec(memory_space=pl.ANY)],
        out_specs=[vmem] * len(sizes),
        scratch_shapes=[pltpu.SemaphoreType.DMA((len(sizes),))],
        compiler_params=pltpu.CompilerParams(vmem_limit_bytes=4 * MIB),
        cost_estimate=NOTHING,
        name="cut_rows",
    )(pltpu.with_memory_space_constraint(whole, pltpu.HBM))


def fold_kernel(chunk, sizes, pair, source, folded, again, panel, bounds, sems):
    quarter, virtuals = panel.shape
    fold = folded.shape[1]
    copies = []
    for k in range(quarter // chunk):
        rows = pl.ds(k * chunk, chunk)
        copies.append(pltpu.make_async_copy(source.at[rows], panel.at[rows], sems.at[k]))
        copies[-1].start()
    fill_bounds(sizes, bounds)
    start = lax.axis_index("grp") * quarter
    step = 32 if chunk % 32 == 0 else SUBLANES
    for k, copy in enumerate(copies):
        copy.wait()

        @pl.loop(0, chunk // step, unroll=True)
        def _(i):
            first = pl.multiple_of(k * chunk + i * step, SUBLANES)
            here = pl.ds(first, step)
            b = start + first + lax.broadcasted_iota(jnp.int32, (step, LANES), 0)
            low, high = wanted_range(b, pair, bounds, sizes.shape[0])
            lane = lax.broadcasted_iota(jnp.int32, (step, LANES), 1)
            low, high = low - lane, high - lane
            for place in range(0, fold, LANES):
                total = jnp.zeros((step, LANES), jnp.float32)
                for c in range(place, virtuals, fold):
                    value = panel[here, c:c + LANES].astype(jnp.float32)
                    total = jnp.where((low <= c) & (high > c), value, total)
                total = total.astype(folded.dtype)
                folded[here, place:place + LANES] = total
                again[here, place:place + LANES] = total


def fold_panel(panel, sizes, pair, fold):
    quarter, virtuals = panel.shape
    chunk = quarter // 5 if quarter % (5 * SUBLANES) == 0 else quarter
    smem = pl.BlockSpec(memory_space=pltpu.SMEM)
    return pl.pallas_call(
        functools.partial(fold_kernel, chunk),
        out_shape=[pltpu.VMEM((quarter, fold), panel.dtype)] * 2,
        in_specs=[smem, smem, pl.BlockSpec(memory_space=pl.ANY)],
        out_specs=[pl.BlockSpec(memory_space=pltpu.VMEM)] * 2,
        scratch_shapes=[
            pltpu.VMEM((quarter, virtuals), panel.dtype),
            pltpu.SMEM((sizes.shape[0] + 1,), jnp.int32),
            pltpu.SemaphoreType.DMA((quarter // chunk,)),
        ],
        compiler_params=pltpu.CompilerParams(vmem_limit_bytes=8 * MIB),
        cost_estimate=NOTHING,
        name="fold_panel",
    )(sizes, pair, pltpu.with_memory_space_constraint(panel, pltpu.HBM))


def spread_kernel(slot, groups, first, sizes, pair, folded, other, *refs):
    if first:
        dense, token, fock_out, bounds, turned, sems = refs
    else:
        dense, token, bounds, turned = refs
    token[...] = jnp.zeros_like(token)
    quarter, fold = folded.shape
    virtuals, total = dense.shape
    width = total // groups
    group = lax.axis_index("grp")
    copies = []
    if first:
        for k in range(groups):
            start = pl.multiple_of(jnp.bitwise_xor(group, k) * quarter, SUBLANES)
            copies.append(pltpu.make_async_copy(
                other.at[pl.ds(start, quarter)], fock_out.at[pl.ds(k * width, quarter)], sems.at[k]
            ))
            copies[-1].start()
            if width > quarter:
                fock_out[k * width + quarter:(k + 1) * width, :] = jnp.zeros(
                    (width - quarter, virtuals), fock_out.dtype
                )
    fill_bounds(sizes, bounds)
    step = 32
    values = folded[...].astype(jnp.float32)
    if width > quarter:
        values = jnp.concatenate([values, jnp.zeros((width - quarter, fold), jnp.float32)])
    turned[...] = values.T
    start = jnp.bitwise_xor(group, slot) * quarter
    b = start + lax.broadcasted_iota(jnp.int32, (8, width), 1)
    low, high = wanted_range(b, pair, bounds, sizes.shape[0])
    low = jnp.concatenate([low] * (step // 8))
    high = jnp.concatenate([high] * (step // 8))

    @pl.loop(0, virtuals // step, unroll=4)
    def _(i):
        row = pl.multiple_of(i * step, step)
        source = pl.multiple_of(lax.rem(row, fold), step)
        c = row + lax.broadcasted_iota(jnp.int32, (step, width), 0)
        kept = jnp.where((c >= low) & (c < high), turned[pl.ds(source, step), :], 0.0)
        dense[pl.ds(row, step), slot * width:(slot + 1) * width] = kept.astype(dense.dtype)

    for copy in copies:
        copy.wait()


def spread(slot, groups, folded, sizes, pair, *, fock=None, dense=None):
    quarter, fold = folded.shape
    first = dense is None
    virtuals = fock.shape[0] if first else dense.shape[0]
    width = rounded(quarter, LANES)
    smem = pl.BlockSpec(memory_space=pltpu.SMEM)
    vmem = pl.BlockSpec(memory_space=pltpu.VMEM)
    out_shape = [
        pltpu.VMEM((virtuals, groups * width), folded.dtype), pltpu.VMEM((8, LANES), jnp.int32)
    ]
    scratch = [
        pltpu.SMEM((sizes.shape[0] + 1,), jnp.int32),
        pltpu.VMEM((fold, width), jnp.float32),
    ]
    if first:
        out_shape.append(pltpu.VMEM((groups * width, virtuals), fock.dtype))
        scratch.append(pltpu.SemaphoreType.DMA((groups,)))
        other = pltpu.with_memory_space_constraint(fock, pltpu.HBM)
    else:
        other = pltpu.with_memory_space_constraint(dense, pltpu.VMEM)
    return pl.pallas_call(
        functools.partial(spread_kernel, slot, groups, first),
        out_shape=out_shape,
        in_specs=[smem, smem, vmem, pl.BlockSpec(memory_space=pl.ANY)],
        out_specs=[vmem] * len(out_shape),
        input_output_aliases={} if first else {3: 0},
        scratch_shapes=scratch,
        compiler_params=pltpu.CompilerParams(vmem_limit_bytes=8 * MIB),
        cost_estimate=NOTHING,
        name="spread_panel",
    )(sizes, pair, folded, other)


def after(array, *others):
    anywhere = pl.BlockSpec(memory_space=pl.ANY)
    return pl.pallas_call(
        lambda *refs: None,
        out_shape=jax.ShapeDtypeStruct(array.shape, array.dtype),
        in_specs=[anywhere] * (1 + len(others)),
        out_specs=anywhere,
        input_output_aliases={0: 0},
        compiler_params=pltpu.CompilerParams(vmem_limit_bytes=MIB),
        cost_estimate=NOTHING,
        name="after",
    )(array, *others)


def column_tiles(total, tile):
    return [(first, min(tile, total - first)) for first in range(0, total, tile)]


def dress_kernel(spans, rows, members, has_base, amplitudes, dense, fock, *refs):
    if has_base:
        refs = refs[1:]
    result, token, coupled, dressed, sems = refs
    token[...] = jnp.zeros_like(token)
    virtuals, total = dense.shape
    block = lax.axis_index("blk")
    places = [
        pl.multiple_of(lax.rem(block + by, members) * rows + offset, SUBLANES)
        for by, offset, _ in spans
    ]
    for first, tile in column_tiles(total, 512):
        coupled[:, first:first + tile] = jnp.dot(
            amplitudes[...], dense[:, first:first + tile], preferred_element_type=jnp.float32
        ).astype(coupled.dtype)
    copies = []
    for t, (first, tile) in enumerate(column_tiles(virtuals, 512)):
        dressed[:, first:first + tile] = jnp.dot(
            coupled[...], fock[:, first:first + tile], preferred_element_type=jnp.float32
        ).astype(dressed.dtype)
        begin = 0
        for p, (_, _, size) in enumerate(spans):
            copies.append(pltpu.make_async_copy(
                dressed.at[pl.ds(begin, size), pl.ds(first, tile)],
                result.at[pl.ds(places[p], size), pl.ds(first, tile)],
                sems.at[p, t],
            ))
            copies[-1].start()
            begin += size
    for copy in copies:
        copy.wait()


def dress(amplitudes, spans, dense, fock, base, rows, members, out_rows):
    height, virtuals = amplitudes.shape
    vmem = pl.BlockSpec(memory_space=pltpu.VMEM)
    anywhere = pl.BlockSpec(memory_space=pl.ANY)
    pinned = [pltpu.with_memory_space_constraint(x, pltpu.VMEM) for x in (dense, fock)]
    bases = [] if base is None else [base]
    return pl.pallas_call(
        functools.partial(dress_kernel, spans, rows, members, base is not None),
        out_shape=(
            jax.ShapeDtypeStruct((out_rows, virtuals), amplitudes.dtype),
            pltpu.VMEM((8, LANES), jnp.int32),
        ),
        in_specs=[vmem] * 3 + [anywhere] * len(bases),
        out_specs=(anywhere, vmem),
        input_output_aliases={} if base is None else {3: 0},
        scratch_shapes=[
            pltpu.VMEM((height, dense.shape[1]), amplitudes.dtype),
            pltpu.VMEM((height, virtuals), amplitudes.dtype),
            pltpu.SemaphoreType.DMA((len(spans), len(column_tiles(virtuals, 512)))),
        ],
        compiler_params=pltpu.CompilerParams(vmem_limit_bytes=16 * MIB),
        cost_estimate=NOTHING,
        name="dress_rows",
    )(amplitudes, *pinned, *bases)


def make_local(blocks, groups):
    members = blocks // groups
    axes = ("blk", "grp")

    def device(hi, lo, grp):
        return (hi * members + lo) * groups + grp

    everyone = [(h, l, g) for h in range(groups) for l in range(members) for g in range(groups)]

    if groups == 4:
        copies = ((None, 1, 0, 3), (0, None, 2, 1), (0, 2, None, 3), (2, 0, 3, None))
    else:
        copies = [[None if h == g else h for h in range(groups)] for g in range(groups)]
    to_group = [
        (device(g, l, copies[g][h]), device(h, l, g)) for h, l, g in everyone if h != g
    ]

    def to_member(by):
        return [(device(h, (l + by) % members, g), device(h, l, g)) for h, l, g in everyone]

    def to_slot(slot):
        return [(device(h, l, g ^ slot), device(h, l, g)) for h, l, g in everyone]

    def local(amplitudes, hole_panel, virt_fock, irrep_sizes, pair_irreps):
        rows, virtuals = amplitudes.shape
        out_rows = rows * members
        fold = rounded(virtuals // 4, LANES)
        panel = jnp.swapaxes(hole_panel[:, 0, :], 0, 1)
        irrep_sizes = pltpu.with_memory_space_constraint(irrep_sizes, pltpu.HBM)

        own, own_again = fold_panel(panel, irrep_sizes, pair_irreps, fold)
        across = lax.ppermute(own, axes, to_slot(2))
        beside = lax.ppermute(own_again, axes, to_slot(1))

        owner = lax.axis_index("blk") // members == lax.axis_index("grp")

        def arrived(piece, kept):
            return jnp.where(owner, kept, piece)

        early = rounded(rows * 2 // 3, SUBLANES) if rows % SUBLANES == 0 else rows
        if early < rows:
            top, low = cut(amplitudes, (early, rows - early))
            lows = [low] + [lax.ppermute(low, axes, to_member(by)) for by in range(1, members)]
            lows = jnp.concatenate(lows)
        else:
            top = amplitudes
        top = arrived(lax.ppermute(top, axes, to_group), top)

        spread_one = functools.partial(spread, sizes=irrep_sizes, pair=pair_irreps)
        dense, token, fock = spread_one(0, groups, own, fock=virt_fock)
        top = after(top, token)
        if early < rows:
            lows = after(lows, top)
            late = lax.ppermute(lows, axes, to_group)
        tops = [top] + [lax.ppermute(top, axes, to_member(by)) for by in range(1, members)]
        dense, token = spread_one(1, groups, beside, dense=dense)
        across = after(across, token)
        both = lax.ppermute(across, axes, to_slot(1))
        dense, _ = spread_one(2, groups, across, dense=dense)
        dense, _ = spread_one(3, groups, both, dense=dense)

        if early < rows:
            result = None
            for by, piece in enumerate(tops):
                spans = [(by, 0, early)]
                result, token = dress(piece, spans, dense, fock, result, rows, members, out_rows)
            spans = [(by, early, rows - early) for by in range(members)]
            lows = arrived(after(late, token), lows)
            result, _ = dress(lows, spans, dense, fock, result, rows, members, out_rows)
        else:
            member = lax.axis_index("blk") % members
            ordered = jnp.roll(jnp.stack(tops), member, axis=0).reshape(out_rows, virtuals)
            spans = [(0, 0, out_rows)]
            result, _ = dress(ordered, spans, dense, fock, None, 0, members, out_rows)
        return result[:, None, :]

    return local


def solution(mesh):
    in_specs = (P("blk", None), P(None, "blk", "grp"), P(), P(), P("blk"))
    out_specs = P("grp", "blk", None)
    local = make_local(mesh.shape["blk"], mesh.shape["grp"])
    return jax.shard_map(local, mesh=mesh, in_specs=in_specs, out_specs=out_specs, check_vma=False)
```

```python
import functools

import jax
import jax.numpy as jnp
from jax import lax
from jax.experimental import pallas as pl
from jax.experimental.pallas import tpu as pltpu
from jax.sharding import PartitionSpec as P

LANES = 128
SUBLANES = 16
MIB = 1 << 20
NOTHING = pl.CostEstimate(flops=0, bytes_accessed=0, transcendentals=0)


def rounded(value, unit):
    return -(-value // unit) * unit


def fill_bounds(sizes, bounds):
    total = jnp.int32(0)
    for r in range(sizes.shape[0]):
        bounds[r] = total
        total = total + sizes[r]
    bounds[sizes.shape[0]] = total


def wanted_range(b, pair, bounds, irreps):
    low, high = jnp.zeros_like(b), jnp.zeros_like(b)
    for r in range(irreps):
        partner = jnp.bitwise_xor(pair[0], r)
        inside = (b >= bounds[r]) & (b < bounds[r + 1])
        low = jnp.where(inside, bounds[partner], low)
        high = jnp.where(inside, bounds[partner + 1], high)
    return low, high


def cut_kernel(whole, *refs):
    pieces, sems = refs[:-1], refs[-1]
    copies, first = [], 0
    for k, piece in enumerate(pieces):
        size = piece.shape[0]
        copies.append(pltpu.make_async_copy(whole.at[pl.ds(first, size)], piece, sems.at[k]))
        copies[-1].start()
        first += size
    for copy in copies:
        copy.wait()


def cut(whole, sizes):
    vmem = pl.BlockSpec(memory_space=pltpu.VMEM)
    return pl.pallas_call(
        cut_kernel,
        out_shape=[pltpu.VMEM((size, whole.shape[1]), whole.dtype) for size in sizes],
        in_specs=[pl.BlockSpec(memory_space=pl.ANY)],
        out_specs=[vmem] * len(sizes),
        scratch_shapes=[pltpu.SemaphoreType.DMA((len(sizes),))],
        compiler_params=pltpu.CompilerParams(vmem_limit_bytes=4 * MIB),
        cost_estimate=NOTHING,
        name="cut_rows",
    )(pltpu.with_memory_space_constraint(whole, pltpu.HBM))


def fold_kernel(chunk, sizes, pair, source, folded, again, panel, bounds, sems):
    quarter, virtuals = panel.shape
    fold = folded.shape[1]
    copies = []
    for k in range(quarter // chunk):
        rows = pl.ds(k * chunk, chunk)
        copies.append(pltpu.make_async_copy(source.at[rows], panel.at[rows], sems.at[k]))
        copies[-1].start()
    fill_bounds(sizes, bounds)
    start = lax.axis_index("grp") * quarter
    step = 32 if chunk % 32 == 0 else SUBLANES
    for k, copy in enumerate(copies):
        copy.wait()

        @pl.loop(0, chunk // step, unroll=True)
        def _(i):
            first = pl.multiple_of(k * chunk + i * step, SUBLANES)
            here = pl.ds(first, step)
            b = start + first + lax.broadcasted_iota(jnp.int32, (step, LANES), 0)
            low, high = wanted_range(b, pair, bounds, sizes.shape[0])
            lane = lax.broadcasted_iota(jnp.int32, (step, LANES), 1)
            low, high = low - lane, high - lane
            for place in range(0, fold, LANES):
                total = jnp.zeros((step, LANES), jnp.float32)
                for c in range(place, virtuals, fold):
                    value = panel[here, c:c + LANES].astype(jnp.float32)
                    total = jnp.where((low <= c) & (high > c), value, total)
                total = total.astype(folded.dtype)
                folded[here, place:place + LANES] = total
                again[here, place:place + LANES] = total


def fold_panel(panel, sizes, pair, fold):
    quarter, virtuals = panel.shape
    chunk = quarter // 5 if quarter % (5 * SUBLANES) == 0 else quarter
    smem = pl.BlockSpec(memory_space=pltpu.SMEM)
    return pl.pallas_call(
        functools.partial(fold_kernel, chunk),
        out_shape=[pltpu.VMEM((quarter, fold), panel.dtype)] * 2,
        in_specs=[smem, smem, pl.BlockSpec(memory_space=pl.ANY)],
        out_specs=[pl.BlockSpec(memory_space=pltpu.VMEM)] * 2,
        scratch_shapes=[
            pltpu.VMEM((quarter, virtuals), panel.dtype),
            pltpu.SMEM((sizes.shape[0] + 1,), jnp.int32),
            pltpu.SemaphoreType.DMA((quarter // chunk,)),
        ],
        compiler_params=pltpu.CompilerParams(vmem_limit_bytes=8 * MIB),
        cost_estimate=NOTHING,
        name="fold_panel",
    )(sizes, pair, pltpu.with_memory_space_constraint(panel, pltpu.HBM))


def spread_kernel(slot, groups, first, sizes, pair, folded, other, *refs):
    if first:
        dense, token, fock_out, bounds, turned, sems = refs
    else:
        dense, token, bounds, turned = refs
    token[...] = jnp.zeros_like(token)
    quarter, fold = folded.shape
    virtuals, total = dense.shape
    width = total // groups
    group = lax.axis_index("grp")
    copies = []
    if first:
        for k in range(groups):
            start = pl.multiple_of(jnp.bitwise_xor(group, k) * quarter, SUBLANES)
            copies.append(pltpu.make_async_copy(
                other.at[pl.ds(start, quarter)], fock_out.at[pl.ds(k * width, quarter)], sems.at[k]
            ))
            copies[-1].start()
            if width > quarter:
                fock_out[k * width + quarter:(k + 1) * width, :] = jnp.zeros(
                    (width - quarter, virtuals), fock_out.dtype
                )
    fill_bounds(sizes, bounds)
    step = 32
    values = folded[...].astype(jnp.float32)
    if width > quarter:
        values = jnp.concatenate([values, jnp.zeros((width - quarter, fold), jnp.float32)])
    turned[...] = values.T
    start = jnp.bitwise_xor(group, slot) * quarter
    b = start + lax.broadcasted_iota(jnp.int32, (8, width), 1)
    low, high = wanted_range(b, pair, bounds, sizes.shape[0])
    low = jnp.concatenate([low] * (step // 8))
    high = jnp.concatenate([high] * (step // 8))

    @pl.loop(0, virtuals // step, unroll=4)
    def _(i):
        row = pl.multiple_of(i * step, step)
        source = pl.multiple_of(lax.rem(row, fold), step)
        c = row + lax.broadcasted_iota(jnp.int32, (step, width), 0)
        kept = jnp.where((c >= low) & (c < high), turned[pl.ds(source, step), :], 0.0)
        dense[pl.ds(row, step), slot * width:(slot + 1) * width] = kept.astype(dense.dtype)

    for copy in copies:
        copy.wait()


def spread(slot, groups, folded, sizes, pair, *, fock=None, dense=None):
    quarter, fold = folded.shape
    first = dense is None
    virtuals = fock.shape[0] if first else dense.shape[0]
    width = rounded(quarter, LANES)
    smem = pl.BlockSpec(memory_space=pltpu.SMEM)
    vmem = pl.BlockSpec(memory_space=pltpu.VMEM)
    out_shape = [
        pltpu.VMEM((virtuals, groups * width), folded.dtype), pltpu.VMEM((8, LANES), jnp.int32)
    ]
    scratch = [
        pltpu.SMEM((sizes.shape[0] + 1,), jnp.int32),
        pltpu.VMEM((fold, width), jnp.float32),
    ]
    if first:
        out_shape.append(pltpu.VMEM((groups * width, virtuals), fock.dtype))
        scratch.append(pltpu.SemaphoreType.DMA((groups,)))
        other = pltpu.with_memory_space_constraint(fock, pltpu.HBM)
    else:
        other = pltpu.with_memory_space_constraint(dense, pltpu.VMEM)
    return pl.pallas_call(
        functools.partial(spread_kernel, slot, groups, first),
        out_shape=out_shape,
        in_specs=[smem, smem, vmem, pl.BlockSpec(memory_space=pl.ANY)],
        out_specs=[vmem] * len(out_shape),
        input_output_aliases={} if first else {3: 0},
        scratch_shapes=scratch,
        compiler_params=pltpu.CompilerParams(vmem_limit_bytes=8 * MIB),
        cost_estimate=NOTHING,
        name="spread_panel",
    )(sizes, pair, folded, other)


def after(array, *others):
    anywhere = pl.BlockSpec(memory_space=pl.ANY)
    return pl.pallas_call(
        lambda *refs: None,
        out_shape=jax.ShapeDtypeStruct(array.shape, array.dtype),
        in_specs=[anywhere] * (1 + len(others)),
        out_specs=anywhere,
        input_output_aliases={0: 0},
        compiler_params=pltpu.CompilerParams(vmem_limit_bytes=MIB),
        cost_estimate=NOTHING,
        name="after",
    )(array, *others)


def owned_kernel(members, received, kept, *refs):
    out, sem = refs[-2:]

    @pl.when(lax.div(lax.axis_index("blk"), members) == lax.axis_index("grp"))
    def _():
        copy = pltpu.make_async_copy(kept, out, sem)
        copy.start()
        copy.wait()


def owned(received, kept, members, *others):
    anywhere = pl.BlockSpec(memory_space=pl.ANY)
    return pl.pallas_call(
        functools.partial(owned_kernel, members),
        out_shape=jax.ShapeDtypeStruct(received.shape, received.dtype),
        in_specs=[anywhere] * (2 + len(others)),
        out_specs=anywhere,
        input_output_aliases={0: 0},
        scratch_shapes=[pltpu.SemaphoreType.DMA],
        compiler_params=pltpu.CompilerParams(vmem_limit_bytes=MIB),
        cost_estimate=NOTHING,
        name="owned_rows",
    )(received, kept, *others)


def column_tiles(total, tile):
    return [(first, min(tile, total - first)) for first in range(0, total, tile)]


def dress_kernel(spans, rows, members, has_base, amplitudes, dense, fock, *refs):
    if has_base:
        refs = refs[1:]
    result, token, coupled, dressed, sems = refs
    token[...] = jnp.zeros_like(token)
    virtuals, total = dense.shape
    block = lax.axis_index("blk")
    places = [
        pl.multiple_of(lax.rem(block + by, members) * rows + offset, SUBLANES)
        for by, offset, _ in spans
    ]
    for first, tile in column_tiles(total, 512):
        coupled[:, first:first + tile] = jnp.dot(
            amplitudes[...], dense[:, first:first + tile], preferred_element_type=jnp.float32
        ).astype(coupled.dtype)
    copies = []
    for t, (first, tile) in enumerate(column_tiles(virtuals, 512)):
        dressed[:, first:first + tile] = jnp.dot(
            coupled[...], fock[:, first:first + tile], preferred_element_type=jnp.float32
        ).astype(dressed.dtype)
        begin = 0
        for p, (_, _, size) in enumerate(spans):
            copies.append(pltpu.make_async_copy(
                dressed.at[pl.ds(begin, size), pl.ds(first, tile)],
                result.at[pl.ds(places[p], size), pl.ds(first, tile)],
                sems.at[p, t],
            ))
            copies[-1].start()
            begin += size
    for copy in copies:
        copy.wait()


def dress(amplitudes, spans, dense, fock, base, rows, members, out_rows):
    height, virtuals = amplitudes.shape
    vmem = pl.BlockSpec(memory_space=pltpu.VMEM)
    anywhere = pl.BlockSpec(memory_space=pl.ANY)
    pinned = [pltpu.with_memory_space_constraint(x, pltpu.VMEM) for x in (dense, fock)]
    bases = [] if base is None else [base]
    return pl.pallas_call(
        functools.partial(dress_kernel, spans, rows, members, base is not None),
        out_shape=(
            jax.ShapeDtypeStruct((out_rows, virtuals), amplitudes.dtype),
            pltpu.VMEM((8, LANES), jnp.int32),
        ),
        in_specs=[vmem] * 3 + [anywhere] * len(bases),
        out_specs=(anywhere, vmem),
        input_output_aliases={} if base is None else {3: 0},
        scratch_shapes=[
            pltpu.VMEM((height, dense.shape[1]), amplitudes.dtype),
            pltpu.VMEM((height, virtuals), amplitudes.dtype),
            pltpu.SemaphoreType.DMA((len(spans), len(column_tiles(virtuals, 512)))),
        ],
        compiler_params=pltpu.CompilerParams(vmem_limit_bytes=16 * MIB),
        cost_estimate=NOTHING,
        name="dress_rows",
    )(amplitudes, *pinned, *bases)


def make_local(blocks, groups):
    members = blocks // groups
    axes = ("blk", "grp")

    def device(hi, lo, grp):
        return (hi * members + lo) * groups + grp

    everyone = [(h, l, g) for h in range(groups) for l in range(members) for g in range(groups)]

    if groups == 4:
        copies = ((None, 1, 0, 3), (0, None, 2, 1), (0, 2, None, 3), (2, 0, 3, None))
    else:
        copies = [[None if h == g else h for h in range(groups)] for g in range(groups)]
    to_group = [
        (device(g, l, copies[g][h]), device(h, l, g)) for h, l, g in everyone if h != g
    ]

    def to_member(by):
        return [(device(h, (l + by) % members, g), device(h, l, g)) for h, l, g in everyone]

    def to_slot(slot):
        return [(device(h, l, g ^ slot), device(h, l, g)) for h, l, g in everyone]

    def local(amplitudes, hole_panel, virt_fock, irrep_sizes, pair_irreps):
        rows, virtuals = amplitudes.shape
        out_rows = rows * members
        fold = rounded(virtuals // 4, LANES)
        panel = jnp.swapaxes(hole_panel[:, 0, :], 0, 1)
        irrep_sizes = pltpu.with_memory_space_constraint(irrep_sizes, pltpu.HBM)

        own, own_again = fold_panel(panel, irrep_sizes, pair_irreps, fold)
        across = lax.ppermute(own, axes, to_slot(2))
        beside = lax.ppermute(own_again, axes, to_slot(1))

        early = rounded(rows * 2 // 3, SUBLANES) if rows % SUBLANES == 0 else rows
        if early < rows:
            top, low = cut(amplitudes, (early, rows - early))
            lows = [low] + [lax.ppermute(low, axes, to_member(by)) for by in range(1, members)]
            lows = jnp.concatenate(lows)
        else:
            top = amplitudes

        spread_one = functools.partial(spread, sizes=irrep_sizes, pair=pair_irreps)
        dense, token, fock = spread_one(0, groups, own, fock=virt_fock)
        top = owned(lax.ppermute(top, axes, to_group), top, members, token)
        if early < rows:
            lows = after(lows, top)
            late = lax.ppermute(lows, axes, to_group)
        tops = [top] + [lax.ppermute(top, axes, to_member(by)) for by in range(1, members)]
        dense, token = spread_one(1, groups, beside, dense=dense)
        across = after(across, token)
        both = lax.ppermute(across, axes, to_slot(1))
        dense, _ = spread_one(2, groups, across, dense=dense)
        dense, _ = spread_one(3, groups, both, dense=dense)

        if early < rows:
            result = None
            for by, piece in enumerate(tops):
                spans = [(by, 0, early)]
                result, token = dress(piece, spans, dense, fock, result, rows, members, out_rows)
            spans = [(by, early, rows - early) for by in range(members)]
            lows = owned(late, lows, members, token)
            result, _ = dress(lows, spans, dense, fock, result, rows, members, out_rows)
        else:
            member = lax.axis_index("blk") % members
            ordered = jnp.roll(jnp.stack(tops), member, axis=0).reshape(out_rows, virtuals)
            spans = [(0, 0, out_rows)]
            result, _ = dress(ordered, spans, dense, fock, None, 0, members, out_rows)
        return result[:, None, :]

    return local


def solution(mesh):
    in_specs = (P("blk", None), P(None, "blk", "grp"), P(), P(), P("blk"))
    out_specs = P("grp", "blk", None)
    local = make_local(mesh.shape["blk"], mesh.shape["grp"])
    return jax.shard_map(local, mesh=mesh, in_specs=in_specs, out_specs=out_specs, check_vma=False)
```

```python
import functools

import jax
import jax.numpy as jnp
from jax import lax
from jax.experimental import pallas as pl
from jax.experimental.pallas import tpu as pltpu
from jax.sharding import PartitionSpec as P

LANES = 128
SUBLANES = 16
MIB = 1 << 20
TOKEN = pltpu.VMEM((8, LANES), jnp.int32)
NOTHING = pl.CostEstimate(flops=0, bytes_accessed=0, transcendentals=0)


def rounded(value, unit):
    return -(-value // unit) * unit


def fill_bounds(sizes, bounds):
    total = jnp.int32(0)
    for r in range(sizes.shape[0]):
        bounds[r] = total
        total = total + sizes[r]
    bounds[sizes.shape[0]] = total


def wanted_range(b, pair, bounds, irreps):
    low, high = jnp.zeros_like(b), jnp.zeros_like(b)
    for r in range(irreps):
        partner = jnp.bitwise_xor(pair[0], r)
        inside = (b >= bounds[r]) & (b < bounds[r + 1])
        low = jnp.where(inside, bounds[partner], low)
        high = jnp.where(inside, bounds[partner + 1], high)
    return low, high


def cut_kernel(whole, *refs):
    pieces, sems = refs[:-1], refs[-1]
    copies, first = [], 0
    for k, piece in enumerate(pieces):
        size = piece.shape[0]
        copies.append(pltpu.make_async_copy(whole.at[pl.ds(first, size)], piece, sems.at[k]))
        copies[-1].start()
        first += size
    for copy in copies:
        copy.wait()


def cut(whole, sizes):
    vmem = pl.BlockSpec(memory_space=pltpu.VMEM)
    return pl.pallas_call(
        cut_kernel,
        out_shape=[pltpu.VMEM((size, whole.shape[1]), whole.dtype) for size in sizes],
        in_specs=[pl.BlockSpec(memory_space=pl.ANY)],
        out_specs=[vmem] * len(sizes),
        scratch_shapes=[pltpu.SemaphoreType.DMA((len(sizes),))],
        compiler_params=pltpu.CompilerParams(vmem_limit_bytes=4 * MIB),
        cost_estimate=NOTHING,
        name="cut_rows",
    )(pltpu.with_memory_space_constraint(whole, pltpu.HBM))


def fold_kernel(chunk, sizes, pair, source, folded, again, panel, bounds, sems):
    quarter, virtuals = panel.shape
    fold = folded.shape[1]
    copies = []
    for k in range(quarter // chunk):
        rows = pl.ds(k * chunk, chunk)
        copies.append(pltpu.make_async_copy(source.at[rows], panel.at[rows], sems.at[k]))
        copies[-1].start()
    fill_bounds(sizes, bounds)
    start = lax.axis_index("grp") * quarter
    step = 32 if chunk % 32 == 0 else SUBLANES
    for k, copy in enumerate(copies):
        copy.wait()

        @pl.loop(0, chunk // step, unroll=True)
        def _(i):
            first = pl.multiple_of(k * chunk + i * step, SUBLANES)
            here = pl.ds(first, step)
            b = start + first + lax.broadcasted_iota(jnp.int32, (step, LANES), 0)
            low, high = wanted_range(b, pair, bounds, sizes.shape[0])
            lane = lax.broadcasted_iota(jnp.int32, (step, LANES), 1)
            low, high = low - lane, high - lane
            for place in range(0, fold, LANES):
                total = jnp.zeros((step, LANES), jnp.float32)
                for c in range(place, virtuals, fold):
                    value = panel[here, c:c + LANES].astype(jnp.float32)
                    total = jnp.where((low <= c) & (high > c), value, total)
                total = total.astype(folded.dtype)
                folded[here, place:place + LANES] = total
                again[here, place:place + LANES] = total


def fold_panel(panel, sizes, pair, fold):
    quarter, virtuals = panel.shape
    chunk = quarter // 5 if quarter % (5 * SUBLANES) == 0 else quarter
    smem = pl.BlockSpec(memory_space=pltpu.SMEM)
    return pl.pallas_call(
        functools.partial(fold_kernel, chunk),
        out_shape=[pltpu.VMEM((quarter, fold), panel.dtype)] * 2,
        in_specs=[smem, smem, pl.BlockSpec(memory_space=pl.ANY)],
        out_specs=[pl.BlockSpec(memory_space=pltpu.VMEM)] * 2,
        scratch_shapes=[
            pltpu.VMEM((quarter, virtuals), panel.dtype),
            pltpu.SMEM((sizes.shape[0] + 1,), jnp.int32),
            pltpu.SemaphoreType.DMA((quarter // chunk,)),
        ],
        compiler_params=pltpu.CompilerParams(vmem_limit_bytes=8 * MIB),
        cost_estimate=NOTHING,
        name="fold_panel",
    )(sizes, pair, pltpu.with_memory_space_constraint(panel, pltpu.HBM))


def spread_kernel(slot, groups, first, signed, sizes, pair, folded, other, dense, *refs):
    if signed:
        refs[0][...] = jnp.zeros_like(refs[0])
        refs = refs[1:]
    if first:
        fock_out, bounds, turned, sems = refs
    else:
        bounds, turned = refs
    quarter, fold = folded.shape
    virtuals, total = dense.shape
    width = total // groups
    group = lax.axis_index("grp")
    copies = []
    if first:
        for k in range(groups):
            start = pl.multiple_of(jnp.bitwise_xor(group, k) * quarter, SUBLANES)
            copies.append(pltpu.make_async_copy(
                other.at[pl.ds(start, quarter)], fock_out.at[pl.ds(k * width, quarter)], sems.at[k]
            ))
            copies[-1].start()
            if width > quarter:
                fock_out[k * width + quarter:(k + 1) * width, :] = jnp.zeros(
                    (width - quarter, virtuals), fock_out.dtype
                )
    fill_bounds(sizes, bounds)
    step = 32
    values = folded[...].astype(jnp.float32)
    if width > quarter:
        values = jnp.concatenate([values, jnp.zeros((width - quarter, fold), jnp.float32)])
    turned[...] = values.T
    start = jnp.bitwise_xor(group, slot) * quarter
    b = start + lax.broadcasted_iota(jnp.int32, (8, width), 1)
    low, high = wanted_range(b, pair, bounds, sizes.shape[0])
    low = jnp.concatenate([low] * (step // 8))
    high = jnp.concatenate([high] * (step // 8))

    @pl.loop(0, virtuals // step, unroll=4)
    def _(i):
        row = pl.multiple_of(i * step, step)
        source = pl.multiple_of(lax.rem(row, fold), step)
        c = row + lax.broadcasted_iota(jnp.int32, (step, width), 0)
        kept = jnp.where((c >= low) & (c < high), turned[pl.ds(source, step), :], 0.0)
        dense[pl.ds(row, step), slot * width:(slot + 1) * width] = kept.astype(dense.dtype)

    for copy in copies:
        copy.wait()


def spread(slot, groups, folded, sizes, pair, *, fock=None, dense=None, signed=False):
    quarter, fold = folded.shape
    first = dense is None
    virtuals = fock.shape[0] if first else dense.shape[0]
    width = rounded(quarter, LANES)
    smem = pl.BlockSpec(memory_space=pltpu.SMEM)
    vmem = pl.BlockSpec(memory_space=pltpu.VMEM)
    out_shape = [pltpu.VMEM((virtuals, groups * width), folded.dtype)] + [TOKEN] * signed
    scratch = [
        pltpu.SMEM((sizes.shape[0] + 1,), jnp.int32),
        pltpu.VMEM((fold, width), jnp.float32),
    ]
    if first:
        out_shape.append(pltpu.VMEM((groups * width, virtuals), fock.dtype))
        scratch.append(pltpu.SemaphoreType.DMA((groups,)))
        other = pltpu.with_memory_space_constraint(fock, pltpu.HBM)
    else:
        other = pltpu.with_memory_space_constraint(dense, pltpu.VMEM)
    return pl.pallas_call(
        functools.partial(spread_kernel, slot, groups, first, signed),
        out_shape=out_shape,
        in_specs=[smem, smem, vmem, pl.BlockSpec(memory_space=pl.ANY)],
        out_specs=[vmem] * len(out_shape),
        input_output_aliases={} if first else {3: 0},
        scratch_shapes=scratch,
        compiler_params=pltpu.CompilerParams(vmem_limit_bytes=8 * MIB),
        cost_estimate=NOTHING,
        name="spread_panel",
    )(sizes, pair, folded, other)


def after(array, *others):
    anywhere = pl.BlockSpec(memory_space=pl.ANY)
    return pl.pallas_call(
        lambda *refs: None,
        out_shape=jax.ShapeDtypeStruct(array.shape, array.dtype),
        in_specs=[anywhere] * (1 + len(others)),
        out_specs=anywhere,
        input_output_aliases={0: 0},
        compiler_params=pltpu.CompilerParams(vmem_limit_bytes=MIB),
        cost_estimate=NOTHING,
        name="after",
    )(array, *others)


def owned_kernel(members, received, kept, *refs):
    out, sem = refs[-2:]

    @pl.when(lax.div(lax.axis_index("blk"), members) == lax.axis_index("grp"))
    def _():
        copy = pltpu.make_async_copy(kept, out, sem)
        copy.start()
        copy.wait()


def owned(received, kept, members, *others):
    anywhere = pl.BlockSpec(memory_space=pl.ANY)
    return pl.pallas_call(
        functools.partial(owned_kernel, members),
        out_shape=jax.ShapeDtypeStruct(received.shape, received.dtype),
        in_specs=[anywhere] * (2 + len(others)),
        out_specs=anywhere,
        input_output_aliases={0: 0},
        scratch_shapes=[pltpu.SemaphoreType.DMA],
        compiler_params=pltpu.CompilerParams(vmem_limit_bytes=MIB),
        cost_estimate=NOTHING,
        name="owned_rows",
    )(received, kept, *others)


def column_tiles(total, tile):
    return [(first, min(tile, total - first)) for first in range(0, total, tile)]


def dress_kernel(job, amplitudes, dense, fock, *refs):
    columns, spans, rows, members, has_sums, has_base, signed = job
    if has_sums:
        sums, refs = refs[0], refs[1:]
    refs = refs[has_base:]
    result, refs = refs[0], refs[1:]
    if signed:
        refs[0][...] = jnp.zeros_like(refs[0])
        refs = refs[1:]
    virtuals = dense.shape[0]
    begin, end = columns
    coupled = refs[0]
    for first, tile in column_tiles(end - begin, 512):
        coupled[:, first:first + tile] = jnp.dot(
            amplitudes[...], dense[:, begin + first:begin + first + tile],
            preferred_element_type=jnp.float32,
        ).astype(coupled.dtype)
    if spans:
        dressed, sems = refs[1:]
        block = lax.axis_index("blk")
        places = [
            pl.multiple_of(lax.rem(block + by, members) * rows + offset, SUBLANES)
            for by, offset, _ in spans
        ]
    copies = []
    for t, (first, tile) in enumerate(column_tiles(virtuals, 512)):
        here = slice(first, first + tile)
        total = jnp.dot(
            coupled[...], fock[begin:end, here], preferred_element_type=jnp.float32
        )
        if has_sums:
            total = total + sums[:, here]
        if not spans:
            result[:, here] = total
            continue
        dressed[:, here] = total.astype(dressed.dtype)
        top = 0
        for p, (_, _, size) in enumerate(spans):
            copies.append(pltpu.make_async_copy(
                dressed.at[pl.ds(top, size), pl.ds(first, tile)],
                result.at[pl.ds(places[p], size), pl.ds(first, tile)],
                sems.at[p, t],
            ))
            copies[-1].start()
            top += size
    for copy in copies:
        copy.wait()


def dress(amplitudes, dense, fock, *, columns=None, sums=None, spans=(), base=None, rows=0, members=1,
          out_rows=0, signed=False):
    height, virtuals = amplitudes.shape
    begin, end = columns or (0, dense.shape[1])
    vmem = pl.BlockSpec(memory_space=pltpu.VMEM)
    anywhere = pl.BlockSpec(memory_space=pl.ANY)
    pinned = [dense, fock] + ([] if sums is None else [sums])
    pinned = [pltpu.with_memory_space_constraint(x, pltpu.VMEM) for x in pinned]
    bases = [] if base is None else [base]
    scratch = [pltpu.VMEM((height, end - begin), amplitudes.dtype)]
    if spans:
        out_shape = [jax.ShapeDtypeStruct((out_rows, virtuals), amplitudes.dtype)]
        scratch += [
            pltpu.VMEM((height, virtuals), amplitudes.dtype),
            pltpu.SemaphoreType.DMA((len(spans), len(column_tiles(virtuals, 512)))),
        ]
    else:
        out_shape = [pltpu.VMEM((height, virtuals), jnp.float32)]
    job = ((begin, end), spans, rows, members, sums is not None, base is not None, signed)
    return pl.pallas_call(
        functools.partial(dress_kernel, job),
        out_shape=out_shape + [TOKEN] * signed,
        in_specs=[vmem] * (1 + len(pinned)) + [anywhere] * len(bases),
        out_specs=[anywhere if spans else vmem] + [vmem] * signed,
        input_output_aliases={} if base is None else {1 + len(pinned): 0},
        scratch_shapes=scratch,
        compiler_params=pltpu.CompilerParams(vmem_limit_bytes=16 * MIB),
        cost_estimate=NOTHING,
        name="dress_rows",
    )(amplitudes, *pinned, *bases)


def make_local(blocks, groups):
    members = blocks // groups
    axes = ("blk", "grp")

    def device(hi, lo, grp):
        return (hi * members + lo) * groups + grp

    everyone = [(h, l, g) for h in range(groups) for l in range(members) for g in range(groups)]

    if groups == 4:
        copies = ((None, 1, 0, 3), (0, None, 2, 1), (0, 2, None, 3), (2, 0, 3, None))
    else:
        copies = [[None if h == g else h for h in range(groups)] for g in range(groups)]
    to_group = [
        (device(g, l, copies[g][h]), device(h, l, g)) for h, l, g in everyone if h != g
    ]

    def to_member(by):
        return [(device(h, (l + by) % members, g), device(h, l, g)) for h, l, g in everyone]

    def to_slot(slot):
        return [(device(h, l, g ^ slot), device(h, l, g)) for h, l, g in everyone]

    def local(amplitudes, hole_panel, virt_fock, irrep_sizes, pair_irreps):
        rows, virtuals = amplitudes.shape
        out_rows = rows * members
        fold = rounded(virtuals // 4, LANES)
        panel = jnp.swapaxes(hole_panel[:, 0, :], 0, 1)
        irrep_sizes = pltpu.with_memory_space_constraint(irrep_sizes, pltpu.HBM)

        own, own_again = fold_panel(panel, irrep_sizes, pair_irreps, fold)
        across = lax.ppermute(own, axes, to_slot(2))
        beside = lax.ppermute(own_again, axes, to_slot(1))

        early = rounded(rows * 2 // 3, SUBLANES) if rows % SUBLANES == 0 else rows
        if early < rows:
            top, low = cut(amplitudes, (early, rows - early))
            lows = [low] + [lax.ppermute(low, axes, to_member(by)) for by in range(1, members)]
            lows = jnp.concatenate(lows)
        else:
            top = amplitudes

        spread_one = functools.partial(spread, sizes=irrep_sizes, pair=pair_irreps)
        dense, token, fock = spread_one(0, groups, own, fock=virt_fock, signed=True)
        top = owned(lax.ppermute(top, axes, to_group), top, members, token)
        if early < rows:
            lows = after(lows, top)
            late = lax.ppermute(lows, axes, to_group)
        tops = [top] + [lax.ppermute(top, axes, to_member(by)) for by in range(1, members)]
        dense, = spread_one(1, groups, beside, dense=dense)
        near = 2 * dense.shape[1] // groups
        if early < rows:
            sums, token = dress(top, dense, fock, columns=(0, near), signed=True)
            across = after(across, token)
        both = lax.ppermute(across, axes, to_slot(1))
        dense, = spread_one(2, groups, across, dense=dense)
        dense, = spread_one(3, groups, both, dense=dense)

        if early < rows:
            place = dict(rows=rows, members=members, out_rows=out_rows)
            result, = dress(
                top, dense, fock, columns=(near, dense.shape[1]), sums=sums, spans=((0, 0, early),),
                **place,
            )
            for by in range(1, members):
                result, *token = dress(
                    tops[by], dense, fock, spans=((by, 0, early),), base=result,
                    signed=by == members - 1, **place,
                )
            lows = owned(late, lows, members, *token)
            spans = tuple((by, early, rows - early) for by in range(members))
            result, = dress(lows, dense, fock, spans=spans, base=result, **place)
        else:
            member = lax.axis_index("blk") % members
            ordered = jnp.roll(jnp.stack(tops), member, axis=0).reshape(out_rows, virtuals)
            result, = dress(ordered, dense, fock, spans=((0, 0, out_rows),), out_rows=out_rows)
        return result[:, None, :]

    return local


def solution(mesh):
    in_specs = (P("blk", None), P(None, "blk", "grp"), P(), P(), P("blk"))
    out_specs = P("grp", "blk", None)
    local = make_local(mesh.shape["blk"], mesh.shape["grp"])
    return jax.shard_map(local, mesh=mesh, in_specs=in_specs, out_specs=out_specs, check_vma=False)
```

```python
import functools

import jax
import jax.numpy as jnp
from jax import lax
from jax.experimental import pallas as pl
from jax.experimental.pallas import tpu as pltpu
from jax.sharding import PartitionSpec as P

LANES = 128
SUBLANES = 16
MIB = 1 << 20
TOKEN = pltpu.VMEM((8, LANES), jnp.int32)
NOTHING = pl.CostEstimate(flops=0, bytes_accessed=0, transcendentals=0)


def rounded(value, unit):
    return -(-value // unit) * unit


def fill_bounds(sizes, bounds):
    total = jnp.int32(0)
    for r in range(sizes.shape[0]):
        bounds[r] = total
        total = total + sizes[r]
    bounds[sizes.shape[0]] = total


def wanted_range(b, pair, bounds, irreps):
    low, high = jnp.zeros_like(b), jnp.zeros_like(b)
    for r in range(irreps):
        partner = jnp.bitwise_xor(pair[0], r)
        inside = (b >= bounds[r]) & (b < bounds[r + 1])
        low = jnp.where(inside, bounds[partner], low)
        high = jnp.where(inside, bounds[partner + 1], high)
    return low, high


def cut_kernel(whole, *refs):
    pieces, sems = refs[:-1], refs[-1]
    copies, first = [], 0
    for k, piece in enumerate(pieces):
        size = piece.shape[0]
        copies.append(pltpu.make_async_copy(whole.at[pl.ds(first, size)], piece, sems.at[k]))
        copies[-1].start()
        first += size
    for copy in copies:
        copy.wait()


def cut(whole, sizes):
    vmem = pl.BlockSpec(memory_space=pltpu.VMEM)
    return pl.pallas_call(
        cut_kernel,
        out_shape=[pltpu.VMEM((size, whole.shape[1]), whole.dtype) for size in sizes],
        in_specs=[pl.BlockSpec(memory_space=pl.ANY)],
        out_specs=[vmem] * len(sizes),
        scratch_shapes=[pltpu.SemaphoreType.DMA((len(sizes),))],
        compiler_params=pltpu.CompilerParams(vmem_limit_bytes=4 * MIB),
        cost_estimate=NOTHING,
        name="cut_rows",
    )(pltpu.with_memory_space_constraint(whole, pltpu.HBM))


def fold_kernel(chunk, pair, sizes_in, source, folded, again, token, panel, sizes, bounds, sems):
    quarter, virtuals = panel.shape
    fold = folded.shape[1]
    small = pltpu.make_async_copy(sizes_in, sizes, sems.at[quarter // chunk])
    small.start()
    copies = []
    for k in range(quarter // chunk):
        rows = pl.ds(k * chunk, chunk)
        copies.append(pltpu.make_async_copy(source.at[rows], panel.at[rows], sems.at[k]))
        copies[-1].start()
    token[...] = jnp.zeros_like(token)
    small.wait()
    fill_bounds(sizes, bounds)
    start = lax.axis_index("grp") * quarter
    step = 32 if chunk % 32 == 0 else SUBLANES
    for k, copy in enumerate(copies):
        copy.wait()

        @pl.loop(0, chunk // step, unroll=True)
        def _(i):
            first = pl.multiple_of(k * chunk + i * step, SUBLANES)
            here = pl.ds(first, step)
            b = start + first + lax.broadcasted_iota(jnp.int32, (step, LANES), 0)
            low, high = wanted_range(b, pair, bounds, sizes.shape[0])
            lane = lax.broadcasted_iota(jnp.int32, (step, LANES), 1)
            low, high = low - lane, high - lane
            for place in range(0, fold, LANES):
                total = jnp.zeros((step, LANES), jnp.float32)
                for c in range(place, virtuals, fold):
                    value = panel[here, c:c + LANES].astype(jnp.float32)
                    total = jnp.where((low <= c) & (high > c), value, total)
                total = total.astype(folded.dtype)
                folded[here, place:place + LANES] = total
                again[here, place:place + LANES] = total


def fold_panel(panel, sizes, pair, fold):
    quarter, virtuals = panel.shape
    chunk = quarter // 5 if quarter % (5 * SUBLANES) == 0 else quarter
    return pl.pallas_call(
        functools.partial(fold_kernel, chunk),
        out_shape=[pltpu.VMEM((quarter, fold), panel.dtype)] * 2 + [TOKEN],
        in_specs=[pl.BlockSpec(memory_space=pltpu.SMEM)] + [pl.BlockSpec(memory_space=pl.ANY)] * 2,
        out_specs=[pl.BlockSpec(memory_space=pltpu.VMEM)] * 3,
        scratch_shapes=[
            pltpu.VMEM((quarter, virtuals), panel.dtype),
            pltpu.SMEM(sizes.shape, jnp.int32),
            pltpu.SMEM((sizes.shape[0] + 1,), jnp.int32),
            pltpu.SemaphoreType.DMA((quarter // chunk + 1,)),
        ],
        compiler_params=pltpu.CompilerParams(vmem_limit_bytes=8 * MIB),
        cost_estimate=NOTHING,
        name="fold_panel",
    )(pair, sizes, pltpu.with_memory_space_constraint(panel, pltpu.HBM))


def place_panel(slot, folded, ranges, dense, turned):
    quarter, fold = folded.shape
    virtuals = dense.shape[0]
    width = turned.shape[1]
    columns = slice(slot * width, (slot + 1) * width)
    step = 32
    values = folded[...].astype(jnp.float32)
    if width > quarter:
        values = jnp.concatenate([values, jnp.zeros((width - quarter, fold), jnp.float32)])
    turned[...] = values.T
    low = jnp.concatenate([ranges[0, :, columns]] * (step // 8))
    high = jnp.concatenate([ranges[1, :, columns]] * (step // 8))

    @pl.loop(0, virtuals // step, unroll=4)
    def _(i):
        row = pl.multiple_of(i * step, step)
        source = pl.multiple_of(lax.rem(row, fold), step)
        c = row + lax.broadcasted_iota(jnp.int32, (step, width), 0)
        kept = jnp.where((c >= low) & (c < high), turned[pl.ds(source, step), :], 0.0)
        dense[pl.ds(row, step), columns] = kept.astype(dense.dtype)


def first_spread_kernel(
    groups, sizes, pair, folded, fock, dense, fock_out, ranges, token, bounds, turned, sems
):
    quarter = folded.shape[0]
    virtuals = dense.shape[0]
    width = turned.shape[1]
    group = lax.axis_index("grp")
    copies = []
    for k in range(groups):
        start = pl.multiple_of(jnp.bitwise_xor(group, k) * quarter, SUBLANES)
        copies.append(pltpu.make_async_copy(
            fock.at[pl.ds(start, quarter)], fock_out.at[pl.ds(k * width, quarter)], sems.at[k]
        ))
        copies[-1].start()
        if width > quarter:
            fock_out[k * width + quarter:(k + 1) * width, :] = jnp.zeros(
                (width - quarter, virtuals), fock_out.dtype
            )
    token[...] = jnp.zeros_like(token)
    fill_bounds(sizes, bounds)
    for k in range(groups):
        start = jnp.bitwise_xor(group, k) * quarter
        b = start + lax.broadcasted_iota(jnp.int32, (8, width), 1)
        low, high = wanted_range(b, pair, bounds, sizes.shape[0])
        ranges[0, :, k * width:(k + 1) * width] = low
        ranges[1, :, k * width:(k + 1) * width] = high
    place_panel(0, folded, ranges, dense, turned)
    for copy in copies:
        copy.wait()


def first_spread(groups, folded, fock, sizes, pair):
    quarter, fold = folded.shape
    virtuals = fock.shape[0]
    width = rounded(quarter, LANES)
    smem = pl.BlockSpec(memory_space=pltpu.SMEM)
    vmem = pl.BlockSpec(memory_space=pltpu.VMEM)
    return pl.pallas_call(
        functools.partial(first_spread_kernel, groups),
        out_shape=[
            pltpu.VMEM((virtuals, groups * width), folded.dtype),
            pltpu.VMEM((groups * width, virtuals), fock.dtype),
            pltpu.VMEM((2, 8, groups * width), jnp.int32),
            TOKEN,
        ],
        in_specs=[smem, smem, vmem, pl.BlockSpec(memory_space=pl.ANY)],
        out_specs=[vmem] * 4,
        scratch_shapes=[
            pltpu.SMEM((sizes.shape[0] + 1,), jnp.int32),
            pltpu.VMEM((fold, width), jnp.float32),
            pltpu.SemaphoreType.DMA((groups,)),
        ],
        compiler_params=pltpu.CompilerParams(vmem_limit_bytes=8 * MIB),
        cost_estimate=NOTHING,
        name="first_spread",
    )(sizes, pair, folded, pltpu.with_memory_space_constraint(fock, pltpu.HBM))


def spread_kernel(slot, folded, ranges, before, dense, turned):
    place_panel(slot, folded, ranges, dense, turned)


def spread(slot, folded, ranges, dense):
    fold = folded.shape[1]
    width = rounded(folded.shape[0], LANES)
    vmem = pl.BlockSpec(memory_space=pltpu.VMEM)
    pinned = [pltpu.with_memory_space_constraint(x, pltpu.VMEM) for x in (ranges, dense)]
    return pl.pallas_call(
        functools.partial(spread_kernel, slot),
        out_shape=pltpu.VMEM(dense.shape, dense.dtype),
        in_specs=[vmem, vmem, pl.BlockSpec(memory_space=pl.ANY)],
        out_specs=vmem,
        input_output_aliases={2: 0},
        scratch_shapes=[pltpu.VMEM((fold, width), jnp.float32)],
        compiler_params=pltpu.CompilerParams(vmem_limit_bytes=8 * MIB),
        cost_estimate=NOTHING,
        name="spread_panel",
    )(folded, *pinned)


def after(array, *others):
    anywhere = pl.BlockSpec(memory_space=pl.ANY)
    return pl.pallas_call(
        lambda *refs: None,
        out_shape=jax.ShapeDtypeStruct(array.shape, array.dtype),
        in_specs=[anywhere] * (1 + len(others)),
        out_specs=anywhere,
        input_output_aliases={0: 0},
        compiler_params=pltpu.CompilerParams(vmem_limit_bytes=MIB),
        cost_estimate=NOTHING,
        name="after",
    )(array, *others)


def owned_kernel(members, received, kept, *refs):
    out, sem = refs[-2:]

    @pl.when(lax.div(lax.axis_index("blk"), members) == lax.axis_index("grp"))
    def _():
        copy = pltpu.make_async_copy(kept, out, sem)
        copy.start()
        copy.wait()


def owned(received, kept, members, *others):
    anywhere = pl.BlockSpec(memory_space=pl.ANY)
    return pl.pallas_call(
        functools.partial(owned_kernel, members),
        out_shape=jax.ShapeDtypeStruct(received.shape, received.dtype),
        in_specs=[anywhere] * (2 + len(others)),
        out_specs=anywhere,
        input_output_aliases={0: 0},
        scratch_shapes=[pltpu.SemaphoreType.DMA],
        compiler_params=pltpu.CompilerParams(vmem_limit_bytes=MIB),
        cost_estimate=NOTHING,
        name="owned_rows",
    )(received, kept, *others)


def column_tiles(total, tile):
    return [(first, min(tile, total - first)) for first in range(0, total, tile)]


def dress_kernel(job, amplitudes, dense, fock, *refs):
    columns, spans, rows, members, has_sums, has_base, signed = job
    if has_sums:
        sums, refs = refs[0], refs[1:]
    refs = refs[has_base:]
    result, refs = refs[0], refs[1:]
    if signed:
        refs[0][...] = jnp.zeros_like(refs[0])
        refs = refs[1:]
    virtuals = dense.shape[0]
    begin, end = columns
    coupled = refs[0]
    for first, tile in column_tiles(end - begin, 512):
        coupled[:, first:first + tile] = jnp.dot(
            amplitudes[...], dense[:, begin + first:begin + first + tile],
            preferred_element_type=jnp.float32,
        ).astype(coupled.dtype)
    if spans:
        dressed, sems = refs[1:]
        block = lax.axis_index("blk")
        places = [
            pl.multiple_of(lax.rem(block + by, members) * rows + offset, SUBLANES)
            for by, offset, _ in spans
        ]
    copies = []
    for t, (first, tile) in enumerate(column_tiles(virtuals, 512)):
        here = slice(first, first + tile)
        total = jnp.dot(
            coupled[...], fock[begin:end, here], preferred_element_type=jnp.float32
        )
        if has_sums:
            total = total + sums[:, here]
        if not spans:
            result[:, here] = total
            continue
        dressed[:, here] = total.astype(dressed.dtype)
        top = 0
        for p, (_, _, size) in enumerate(spans):
            copies.append(pltpu.make_async_copy(
                dressed.at[pl.ds(top, size), pl.ds(first, tile)],
                result.at[pl.ds(places[p], size), pl.ds(first, tile)],
                sems.at[p, t],
            ))
            copies[-1].start()
            top += size
    for copy in copies:
        copy.wait()


def dress(amplitudes, dense, fock, *, columns=None, sums=None, spans=(), base=None, rows=0, members=1,
          out_rows=0, signed=False):
    height, virtuals = amplitudes.shape
    begin, end = columns or (0, dense.shape[1])
    vmem = pl.BlockSpec(memory_space=pltpu.VMEM)
    anywhere = pl.BlockSpec(memory_space=pl.ANY)
    pinned = [dense, fock] + ([] if sums is None else [sums])
    pinned = [pltpu.with_memory_space_constraint(x, pltpu.VMEM) for x in pinned]
    bases = [] if base is None else [base]
    scratch = [pltpu.VMEM((height, end - begin), amplitudes.dtype)]
    if spans:
        out_shape = [jax.ShapeDtypeStruct((out_rows, virtuals), amplitudes.dtype)]
        scratch += [
            pltpu.VMEM((height, virtuals), amplitudes.dtype),
            pltpu.SemaphoreType.DMA((len(spans), len(column_tiles(virtuals, 512)))),
        ]
    else:
        out_shape = [pltpu.VMEM((height, virtuals), jnp.float32)]
    job = ((begin, end), spans, rows, members, sums is not None, base is not None, signed)
    return pl.pallas_call(
        functools.partial(dress_kernel, job),
        out_shape=out_shape + [TOKEN] * signed,
        in_specs=[vmem] * (1 + len(pinned)) + [anywhere] * len(bases),
        out_specs=[anywhere if spans else vmem] + [vmem] * signed,
        input_output_aliases={} if base is None else {1 + len(pinned): 0},
        scratch_shapes=scratch,
        compiler_params=pltpu.CompilerParams(vmem_limit_bytes=16 * MIB),
        cost_estimate=NOTHING,
        name="dress_rows",
    )(amplitudes, *pinned, *bases)


def make_local(blocks, groups):
    members = blocks // groups
    axes = ("blk", "grp")

    def device(hi, lo, grp):
        return (hi * members + lo) * groups + grp

    everyone = [(h, l, g) for h in range(groups) for l in range(members) for g in range(groups)]

    if groups == 4:
        copies = ((None, 1, 0, 3), (0, None, 2, 1), (0, 2, None, 3), (2, 0, 3, None))
    else:
        copies = [[None if h == g else h for h in range(groups)] for g in range(groups)]
    to_group = [
        (device(g, l, copies[g][h]), device(h, l, g)) for h, l, g in everyone if h != g
    ]

    def to_member(by):
        return [(device(h, (l + by) % members, g), device(h, l, g)) for h, l, g in everyone]

    def to_slot(slot):
        return [(device(h, l, g ^ slot), device(h, l, g)) for h, l, g in everyone]

    def local(amplitudes, hole_panel, virt_fock, irrep_sizes, pair_irreps):
        rows, virtuals = amplitudes.shape
        out_rows = rows * members
        fold = rounded(virtuals // 4, LANES)
        panel = jnp.swapaxes(hole_panel[:, 0, :], 0, 1)
        irrep_sizes = pltpu.with_memory_space_constraint(irrep_sizes, pltpu.HBM)

        own, own_again, token = fold_panel(panel, irrep_sizes, pair_irreps, fold)
        across = lax.ppermute(own, axes, to_slot(2))
        beside = lax.ppermute(own_again, axes, to_slot(1))

        early = rounded(rows * 2 // 3, SUBLANES) if rows % SUBLANES == 0 else rows
        if early < rows:
            top, low = cut(amplitudes, (early, rows - early))
            low = after(low, token)
            lows = [low] + [lax.ppermute(low, axes, to_member(by)) for by in range(1, members)]
            lows = jnp.concatenate(lows)
        else:
            top = amplitudes

        dense, fock, ranges, token = first_spread(groups, own, virt_fock, irrep_sizes, pair_irreps)
        top = owned(lax.ppermute(top, axes, to_group), top, members, token)
        if early < rows:
            lows = after(lows, top)
            late = lax.ppermute(lows, axes, to_group)
        tops = [top] + [lax.ppermute(top, axes, to_member(by)) for by in range(1, members)]
        dense = spread(1, beside, ranges, dense)
        near = 2 * dense.shape[1] // groups
        if early < rows:
            sums, token = dress(top, dense, fock, columns=(0, near), signed=True)
            across = after(across, token)
        both = lax.ppermute(across, axes, to_slot(1))
        dense = spread(2, across, ranges, dense)
        dense = spread(3, both, ranges, dense)

        if early < rows:
            place = dict(rows=rows, members=members, out_rows=out_rows)
            result, = dress(
                top, dense, fock, columns=(near, dense.shape[1]), sums=sums, spans=((0, 0, early),),
                **place,
            )
            for by in range(1, members):
                result, *token = dress(
                    tops[by], dense, fock, spans=((by, 0, early),), base=result,
                    signed=by == members - 1, **place,
                )
            lows = owned(late, lows, members, *token)
            spans = tuple((by, early, rows - early) for by in range(members))
            result, = dress(lows, dense, fock, spans=spans, base=result, **place)
        else:
            member = lax.axis_index("blk") % members
            ordered = jnp.roll(jnp.stack(tops), member, axis=0).reshape(out_rows, virtuals)
            result, = dress(ordered, dense, fock, spans=((0, 0, out_rows),), out_rows=out_rows)
        return result[:, None, :]

    return local


def solution(mesh):
    in_specs = (P("blk", None), P(None, "blk", "grp"), P(), P(), P("blk"))
    out_specs = P("grp", "blk", None)
    local = make_local(mesh.shape["blk"], mesh.shape["grp"])
    return jax.shard_map(local, mesh=mesh, in_specs=in_specs, out_specs=out_specs, check_vma=False)
```

```python
import functools

import jax
import jax.numpy as jnp
from jax import lax
from jax.experimental import pallas as pl
from jax.experimental.pallas import tpu as pltpu
from jax.sharding import PartitionSpec as P

LANES = 128
SUBLANES = 16
MIB = 1 << 20
TOKEN = pltpu.VMEM((8, LANES), jnp.int32)
NOTHING = pl.CostEstimate(flops=0, bytes_accessed=0, transcendentals=0)


def rounded(value, unit):
    return -(-value // unit) * unit


def fill_bounds(sizes, bounds):
    total = jnp.int32(0)
    for r in range(sizes.shape[0]):
        bounds[r] = total
        total = total + sizes[r]
    bounds[sizes.shape[0]] = total


def wanted_range(b, pair, bounds, irreps):
    low, high = jnp.zeros_like(b), jnp.zeros_like(b)
    for r in range(irreps):
        partner = jnp.bitwise_xor(pair[0], r)
        inside = (b >= bounds[r]) & (b < bounds[r + 1])
        low = jnp.where(inside, bounds[partner], low)
        high = jnp.where(inside, bounds[partner + 1], high)
    return low, high


def copies_of(source, first, target, sems):
    count = sems.shape[0]
    step = rounded(-(-target.shape[0] // count), SUBLANES)
    copies = []
    for k, begin in enumerate(range(0, target.shape[0], step)):
        size = min(step, target.shape[0] - begin)
        copies.append(pltpu.make_async_copy(
            source.at[pl.ds(first + begin, size)], target.at[pl.ds(begin, size)], sems.at[k]
        ))
        copies[-1].start()
    return copies


def cut_kernel(whole, piece, sems):
    for copy in copies_of(whole, 0, piece, sems):
        copy.wait()


def cut(whole, size):
    return pl.pallas_call(
        cut_kernel,
        out_shape=pltpu.VMEM((size, whole.shape[1]), whole.dtype),
        in_specs=[pl.BlockSpec(memory_space=pl.ANY)],
        out_specs=pl.BlockSpec(memory_space=pltpu.VMEM),
        scratch_shapes=[pltpu.SemaphoreType.DMA((5,))],
        compiler_params=pltpu.CompilerParams(vmem_limit_bytes=4 * MIB),
        cost_estimate=NOTHING,
        name="cut_rows",
    )(whole)


def fold_kernel(chunk, late, pair, sizes_in, source, *refs):
    if late:
        amplitudes, folded, again, low, panel, sizes, bounds, sems, low_sems = refs
    else:
        folded, again, panel, sizes, bounds, sems = refs
    quarter, virtuals = panel.shape
    fold = folded.shape[1]
    small = pltpu.make_async_copy(sizes_in, sizes, sems.at[quarter // chunk])
    small.start()
    copies = []
    for k in range(quarter // chunk):
        rows = pl.ds(k * chunk, chunk)
        copies.append(pltpu.make_async_copy(source.at[rows], panel.at[rows], sems.at[k]))
        copies[-1].start()
    lows = copies_of(amplitudes, late, low, low_sems) if late else []
    small.wait()
    fill_bounds(sizes, bounds)
    start = lax.axis_index("grp") * quarter
    step = 32 if chunk % 32 == 0 else SUBLANES
    for k, copy in enumerate(copies):
        copy.wait()

        @pl.loop(0, chunk // step, unroll=True)
        def _(i):
            first = pl.multiple_of(k * chunk + i * step, SUBLANES)
            here = pl.ds(first, step)
            b = start + first + lax.broadcasted_iota(jnp.int32, (step, LANES), 0)
            low, high = wanted_range(b, pair, bounds, sizes.shape[0])
            lane = lax.broadcasted_iota(jnp.int32, (step, LANES), 1)
            low, high = low - lane, high - lane
            for place in range(0, fold, LANES):
                total = jnp.zeros((step, LANES), jnp.float32)
                for c in range(place, virtuals, fold):
                    value = panel[here, c:c + LANES].astype(jnp.float32)
                    total = jnp.where((low <= c) & (high > c), value, total)
                total = total.astype(folded.dtype)
                folded[here, place:place + LANES] = total
                again[here, place:place + LANES] = total

    for copy in lows:
        copy.wait()


def fold_panel(panel, sizes, pair, fold, amplitudes, late):
    quarter, virtuals = panel.shape
    chunk = quarter // 5 if quarter % (5 * SUBLANES) == 0 else quarter
    vmem = pl.BlockSpec(memory_space=pltpu.VMEM)
    anywhere = pl.BlockSpec(memory_space=pl.ANY)
    out_shape = [pltpu.VMEM((quarter, fold), panel.dtype)] * 2
    scratch = [
        pltpu.VMEM((quarter, virtuals), panel.dtype),
        pltpu.SMEM(sizes.shape, jnp.int32),
        pltpu.SMEM((sizes.shape[0] + 1,), jnp.int32),
        pltpu.SemaphoreType.DMA((quarter // chunk + 1,)),
    ]
    extra = []
    if late:
        out_shape.append(pltpu.VMEM((amplitudes.shape[0] - late, virtuals), amplitudes.dtype))
        scratch.append(pltpu.SemaphoreType.DMA((2,)))
        extra.append(amplitudes)
    return pl.pallas_call(
        functools.partial(fold_kernel, chunk, late),
        out_shape=out_shape,
        in_specs=[pl.BlockSpec(memory_space=pltpu.SMEM)] + [anywhere] * (2 + len(extra)),
        out_specs=[vmem] * len(out_shape),
        scratch_shapes=scratch,
        compiler_params=pltpu.CompilerParams(vmem_limit_bytes=8 * MIB),
        cost_estimate=NOTHING,
        name="fold_panel",
    )(pair, sizes, pltpu.with_memory_space_constraint(panel, pltpu.HBM), *extra)


def place_panel(slot, folded, ranges, dense, turned):
    quarter, fold = folded.shape
    virtuals = dense.shape[0]
    width = turned.shape[1]
    columns = slice(slot * width, (slot + 1) * width)
    step = 32
    values = folded[...].astype(jnp.float32)
    if width > quarter:
        values = jnp.concatenate([values, jnp.zeros((width - quarter, fold), jnp.float32)])
    turned[...] = values.T
    low = jnp.concatenate([ranges[0, :, columns]] * (step // 8))
    high = jnp.concatenate([ranges[1, :, columns]] * (step // 8))

    @pl.loop(0, virtuals // step, unroll=4)
    def _(i):
        row = pl.multiple_of(i * step, step)
        source = pl.multiple_of(lax.rem(row, fold), step)
        c = row + lax.broadcasted_iota(jnp.int32, (step, width), 0)
        kept = jnp.where((c >= low) & (c < high), turned[pl.ds(source, step), :], 0.0)
        dense[pl.ds(row, step), columns] = kept.astype(dense.dtype)


def first_spread_kernel(
    groups, sizes, pair, folded, fock, dense, fock_out, ranges, token, bounds, turned, sems
):
    quarter = folded.shape[0]
    virtuals = dense.shape[0]
    width = turned.shape[1]
    group = lax.axis_index("grp")
    copies = []
    for k in range(groups):
        start = pl.multiple_of(jnp.bitwise_xor(group, k) * quarter, SUBLANES)
        copies.append(pltpu.make_async_copy(
            fock.at[pl.ds(start, quarter)], fock_out.at[pl.ds(k * width, quarter)], sems.at[k]
        ))
        copies[-1].start()
        if width > quarter:
            fock_out[k * width + quarter:(k + 1) * width, :] = jnp.zeros(
                (width - quarter, virtuals), fock_out.dtype
            )
    token[...] = jnp.zeros_like(token)
    fill_bounds(sizes, bounds)
    for k in range(groups):
        start = jnp.bitwise_xor(group, k) * quarter
        b = start + lax.broadcasted_iota(jnp.int32, (8, width), 1)
        low, high = wanted_range(b, pair, bounds, sizes.shape[0])
        ranges[0, :, k * width:(k + 1) * width] = low
        ranges[1, :, k * width:(k + 1) * width] = high
    place_panel(0, folded, ranges, dense, turned)
    for copy in copies:
        copy.wait()


def first_spread(groups, folded, fock, sizes, pair):
    quarter, fold = folded.shape
    virtuals = fock.shape[0]
    width = rounded(quarter, LANES)
    smem = pl.BlockSpec(memory_space=pltpu.SMEM)
    vmem = pl.BlockSpec(memory_space=pltpu.VMEM)
    return pl.pallas_call(
        functools.partial(first_spread_kernel, groups),
        out_shape=[
            pltpu.VMEM((virtuals, groups * width), folded.dtype),
            pltpu.VMEM((groups * width, virtuals), fock.dtype),
            pltpu.VMEM((2, 8, groups * width), jnp.int32),
            TOKEN,
        ],
        in_specs=[smem, smem, vmem, pl.BlockSpec(memory_space=pl.ANY)],
        out_specs=[vmem] * 4,
        scratch_shapes=[
            pltpu.SMEM((sizes.shape[0] + 1,), jnp.int32),
            pltpu.VMEM((fold, width), jnp.float32),
            pltpu.SemaphoreType.DMA((groups,)),
        ],
        compiler_params=pltpu.CompilerParams(vmem_limit_bytes=8 * MIB),
        cost_estimate=NOTHING,
        name="first_spread",
    )(sizes, pair, folded, pltpu.with_memory_space_constraint(fock, pltpu.HBM))


def spread_kernel(slot, folded, ranges, before, dense, turned):
    place_panel(slot, folded, ranges, dense, turned)


def spread(slot, folded, ranges, dense):
    fold = folded.shape[1]
    width = rounded(folded.shape[0], LANES)
    vmem = pl.BlockSpec(memory_space=pltpu.VMEM)
    pinned = [pltpu.with_memory_space_constraint(x, pltpu.VMEM) for x in (ranges, dense)]
    return pl.pallas_call(
        functools.partial(spread_kernel, slot),
        out_shape=pltpu.VMEM(dense.shape, dense.dtype),
        in_specs=[vmem, vmem, pl.BlockSpec(memory_space=pl.ANY)],
        out_specs=vmem,
        input_output_aliases={2: 0},
        scratch_shapes=[pltpu.VMEM((fold, width), jnp.float32)],
        compiler_params=pltpu.CompilerParams(vmem_limit_bytes=8 * MIB),
        cost_estimate=NOTHING,
        name="spread_panel",
    )(folded, *pinned)


def after(array, *others):
    anywhere = pl.BlockSpec(memory_space=pl.ANY)
    return pl.pallas_call(
        lambda *refs: None,
        out_shape=jax.ShapeDtypeStruct(array.shape, array.dtype),
        in_specs=[anywhere] * (1 + len(others)),
        out_specs=anywhere,
        input_output_aliases={0: 0},
        compiler_params=pltpu.CompilerParams(vmem_limit_bytes=MIB),
        cost_estimate=NOTHING,
        name="after",
    )(array, *others)


def owned_kernel(members, received, kept, *refs):
    out, sem = refs[-2:]

    @pl.when(lax.div(lax.axis_index("blk"), members) == lax.axis_index("grp"))
    def _():
        copy = pltpu.make_async_copy(kept, out, sem)
        copy.start()
        copy.wait()


def owned(received, kept, members, *others):
    anywhere = pl.BlockSpec(memory_space=pl.ANY)
    return pl.pallas_call(
        functools.partial(owned_kernel, members),
        out_shape=jax.ShapeDtypeStruct(received.shape, received.dtype),
        in_specs=[anywhere] * (2 + len(others)),
        out_specs=anywhere,
        input_output_aliases={0: 0},
        scratch_shapes=[pltpu.SemaphoreType.DMA],
        compiler_params=pltpu.CompilerParams(vmem_limit_bytes=MIB),
        cost_estimate=NOTHING,
        name="owned_rows",
    )(received, kept, *others)


def column_tiles(total, tile):
    return [(first, min(tile, total - first)) for first in range(0, total, tile)]


def dress_kernel(job, amplitudes, dense, fock, *refs):
    columns, spans, rows, members, has_sums, has_base, signed = job
    if has_sums:
        sums, refs = refs[0], refs[1:]
    refs = refs[has_base:]
    result, refs = refs[0], refs[1:]
    if signed:
        refs[0][...] = jnp.zeros_like(refs[0])
        refs = refs[1:]
    virtuals = dense.shape[0]
    begin, end = columns
    coupled = refs[0]
    for first, tile in column_tiles(end - begin, 512):
        coupled[:, first:first + tile] = jnp.dot(
            amplitudes[...], dense[:, begin + first:begin + first + tile],
            preferred_element_type=jnp.float32,
        ).astype(coupled.dtype)
    if spans:
        dressed, sems = refs[1:]
        block = lax.axis_index("blk")
        places = [
            pl.multiple_of(lax.rem(block + by, members) * rows + offset, SUBLANES)
            for by, offset, _ in spans
        ]
    copies = []
    for t, (first, tile) in enumerate(column_tiles(virtuals, 512)):
        here = slice(first, first + tile)
        total = jnp.dot(
            coupled[...], fock[begin:end, here], preferred_element_type=jnp.float32
        )
        if has_sums:
            total = total + sums[:, here]
        if not spans:
            result[:, here] = total
            continue
        dressed[:, here] = total.astype(dressed.dtype)
        top = 0
        for p, (_, _, size) in enumerate(spans):
            copies.append(pltpu.make_async_copy(
                dressed.at[pl.ds(top, size), pl.ds(first, tile)],
                result.at[pl.ds(places[p], size), pl.ds(first, tile)],
                sems.at[p, t],
            ))
            copies[-1].start()
            top += size
    for copy in copies:
        copy.wait()


def dress(amplitudes, dense, fock, *, columns=None, sums=None, spans=(), base=None, rows=0, members=1,
          out_rows=0, signed=False):
    height, virtuals = amplitudes.shape
    begin, end = columns or (0, dense.shape[1])
    vmem = pl.BlockSpec(memory_space=pltpu.VMEM)
    anywhere = pl.BlockSpec(memory_space=pl.ANY)
    pinned = [dense, fock] + ([] if sums is None else [sums])
    pinned = [pltpu.with_memory_space_constraint(x, pltpu.VMEM) for x in pinned]
    bases = [] if base is None else [base]
    scratch = [pltpu.VMEM((height, end - begin), amplitudes.dtype)]
    if spans:
        out_shape = [jax.ShapeDtypeStruct((out_rows, virtuals), amplitudes.dtype)]
        scratch += [
            pltpu.VMEM((height, virtuals), amplitudes.dtype),
            pltpu.SemaphoreType.DMA((len(spans), len(column_tiles(virtuals, 512)))),
        ]
    else:
        out_shape = [pltpu.VMEM((height, virtuals), jnp.float32)]
    job = ((begin, end), spans, rows, members, sums is not None, base is not None, signed)
    return pl.pallas_call(
        functools.partial(dress_kernel, job),
        out_shape=out_shape + [TOKEN] * signed,
        in_specs=[vmem] * (1 + len(pinned)) + [anywhere] * len(bases),
        out_specs=[anywhere if spans else vmem] + [vmem] * signed,
        input_output_aliases={} if base is None else {1 + len(pinned): 0},
        scratch_shapes=scratch,
        compiler_params=pltpu.CompilerParams(vmem_limit_bytes=16 * MIB),
        cost_estimate=NOTHING,
        name="dress_rows",
    )(amplitudes, *pinned, *bases)


def make_local(blocks, groups):
    members = blocks // groups
    axes = ("blk", "grp")

    def device(hi, lo, grp):
        return (hi * members + lo) * groups + grp

    everyone = [(h, l, g) for h in range(groups) for l in range(members) for g in range(groups)]

    if groups == 4:
        copies = ((None, 1, 0, 3), (0, None, 2, 1), (0, 2, None, 3), (2, 0, 3, None))
    else:
        copies = [[None if h == g else h for h in range(groups)] for g in range(groups)]
    to_group = [
        (device(g, l, copies[g][h]), device(h, l, g)) for h, l, g in everyone if h != g
    ]

    def to_member(by):
        return [(device(h, (l + by) % members, g), device(h, l, g)) for h, l, g in everyone]

    def to_slot(slot):
        return [(device(h, l, g ^ slot), device(h, l, g)) for h, l, g in everyone]

    def local(amplitudes, hole_panel, virt_fock, irrep_sizes, pair_irreps):
        rows, virtuals = amplitudes.shape
        out_rows = rows * members
        fold = rounded(virtuals // 4, LANES)
        panel = jnp.swapaxes(hole_panel[:, 0, :], 0, 1)
        irrep_sizes = pltpu.with_memory_space_constraint(irrep_sizes, pltpu.HBM)

        early = rounded(rows * 2 // 3, SUBLANES) if rows % SUBLANES == 0 else 0
        if early:
            amplitudes = pltpu.with_memory_space_constraint(amplitudes, pltpu.HBM)
            top = cut(amplitudes, early)
        else:
            top = amplitudes
        own, own_again, *low = fold_panel(panel, irrep_sizes, pair_irreps, fold, amplitudes, early)
        across = lax.ppermute(own, axes, to_slot(2))
        beside = lax.ppermute(own_again, axes, to_slot(1))
        if early:
            low = low[0]
            swapped = [lax.ppermute(low, axes, to_member(by)) for by in range(1, members)]

        dense, fock, ranges, token = first_spread(groups, own, virt_fock, irrep_sizes, pair_irreps)
        top = owned(lax.ppermute(top, axes, to_group), top, members, token)
        if early:
            lows = jnp.concatenate([after(piece, top) for piece in [low] + swapped])
            late = lax.ppermute(lows, axes, to_group)
        tops = [top] + [lax.ppermute(top, axes, to_member(by)) for by in range(1, members)]
        dense = spread(1, beside, ranges, dense)
        near = 2 * dense.shape[1] // groups
        if early:
            sums, token = dress(top, dense, fock, columns=(0, near), signed=True)
            across = after(across, token)
        both = lax.ppermute(across, axes, to_slot(1))
        dense = spread(2, across, ranges, dense)
        dense = spread(3, both, ranges, dense)

        if early:
            place = dict(rows=rows, members=members, out_rows=out_rows)
            result, = dress(
                top, dense, fock, columns=(near, dense.shape[1]), sums=sums, spans=((0, 0, early),),
                **place,
            )
            for by in range(1, members):
                result, *token = dress(
                    tops[by], dense, fock, spans=((by, 0, early),), base=result,
                    signed=by == members - 1, **place,
                )
            lows = owned(late, lows, members, *token)
            spans = tuple((by, early, rows - early) for by in range(members))
            result, = dress(lows, dense, fock, spans=spans, base=result, **place)
        else:
            member = lax.axis_index("blk") % members
            ordered = jnp.roll(jnp.stack(tops), member, axis=0).reshape(out_rows, virtuals)
            result, = dress(ordered, dense, fock, spans=((0, 0, out_rows),), out_rows=out_rows)
        return result[:, None, :]

    return local


def solution(mesh):
    in_specs = (P("blk", None), P(None, "blk", "grp"), P(), P(), P("blk"))
    out_specs = P("grp", "blk", None)
    local = make_local(mesh.shape["blk"], mesh.shape["grp"])
    return jax.shard_map(local, mesh=mesh, in_specs=in_specs, out_specs=out_specs, check_vma=False)
```

```python
import functools

import jax
import jax.numpy as jnp
from jax import lax
from jax.experimental import pallas as pl
from jax.experimental.pallas import tpu as pltpu
from jax.sharding import PartitionSpec as P

LANES = 128
SUBLANES = 16
MIB = 1 << 20
TOKEN = pltpu.VMEM((8, LANES), jnp.int32)
NOTHING = pl.CostEstimate(flops=0, bytes_accessed=0, transcendentals=0)


def rounded(value, unit):
    return -(-value // unit) * unit


def fill_bounds(sizes, bounds):
    total = jnp.int32(0)
    for r in range(sizes.shape[0]):
        bounds[r] = total
        total = total + sizes[r]
    bounds[sizes.shape[0]] = total


def wanted_range(b, pair, bounds, irreps):
    low, high = jnp.zeros_like(b), jnp.zeros_like(b)
    for r in range(irreps):
        partner = jnp.bitwise_xor(pair[0], r)
        inside = (b >= bounds[r]) & (b < bounds[r + 1])
        low = jnp.where(inside, bounds[partner], low)
        high = jnp.where(inside, bounds[partner + 1], high)
    return low, high


def copies_of(source, first, target, sems):
    count = sems.shape[0]
    step = rounded(-(-target.shape[0] // count), SUBLANES)
    copies = []
    for k, begin in enumerate(range(0, target.shape[0], step)):
        size = min(step, target.shape[0] - begin)
        copies.append(pltpu.make_async_copy(
            source.at[pl.ds(first + begin, size)], target.at[pl.ds(begin, size)], sems.at[k]
        ))
        copies[-1].start()
    return copies


def cut_kernel(whole, piece, sems):
    for copy in copies_of(whole, 0, piece, sems):
        copy.wait()


def cut(whole, size):
    return pl.pallas_call(
        cut_kernel,
        out_shape=pltpu.VMEM((size, whole.shape[1]), whole.dtype),
        in_specs=[pl.BlockSpec(memory_space=pl.ANY)],
        out_specs=pl.BlockSpec(memory_space=pltpu.VMEM),
        scratch_shapes=[pltpu.SemaphoreType.DMA((5,))],
        compiler_params=pltpu.CompilerParams(vmem_limit_bytes=4 * MIB),
        cost_estimate=NOTHING,
        name="cut_rows",
    )(whole)


def fold_kernel(chunk, late, pair, sizes_in, source, *refs):
    if late:
        amplitudes, folded, again, low, panel, sizes, bounds, sems, low_sems = refs
    else:
        folded, again, panel, sizes, bounds, sems = refs
    quarter, virtuals = panel.shape
    fold = folded.shape[1]
    small = pltpu.make_async_copy(sizes_in, sizes, sems.at[quarter // chunk])
    small.start()
    copies = []
    for k in range(quarter // chunk):
        rows = pl.ds(k * chunk, chunk)
        copies.append(pltpu.make_async_copy(source.at[rows], panel.at[rows], sems.at[k]))
        copies[-1].start()
    lows = copies_of(amplitudes, late, low, low_sems) if late else []
    small.wait()
    fill_bounds(sizes, bounds)
    start = lax.axis_index("grp") * quarter
    step = 32 if chunk % 32 == 0 else SUBLANES
    for k, copy in enumerate(copies):
        copy.wait()

        @pl.loop(0, chunk // step, unroll=True)
        def _(i):
            first = pl.multiple_of(k * chunk + i * step, SUBLANES)
            here = pl.ds(first, step)
            b = start + first + lax.broadcasted_iota(jnp.int32, (step, LANES), 0)
            low, high = wanted_range(b, pair, bounds, sizes.shape[0])
            lane = lax.broadcasted_iota(jnp.int32, (step, LANES), 1)
            low, high = low - lane, high - lane
            for place in range(0, fold, LANES):
                total = jnp.zeros((step, LANES), jnp.float32)
                for c in range(place, virtuals, fold):
                    value = panel[here, c:c + LANES].astype(jnp.float32)
                    total = jnp.where((low <= c) & (high > c), value, total)
                total = total.astype(folded.dtype)
                folded[here, place:place + LANES] = total
                again[here, place:place + LANES] = total

    for copy in lows:
        copy.wait()


def fold_panel(panel, sizes, pair, fold, amplitudes, late):
    quarter, virtuals = panel.shape
    chunk = quarter // 5 if quarter % (5 * SUBLANES) == 0 else quarter
    vmem = pl.BlockSpec(memory_space=pltpu.VMEM)
    anywhere = pl.BlockSpec(memory_space=pl.ANY)
    out_shape = [pltpu.VMEM((quarter, fold), panel.dtype)] * 2
    scratch = [
        pltpu.VMEM((quarter, virtuals), panel.dtype),
        pltpu.SMEM(sizes.shape, jnp.int32),
        pltpu.SMEM((sizes.shape[0] + 1,), jnp.int32),
        pltpu.SemaphoreType.DMA((quarter // chunk + 1,)),
    ]
    extra = []
    if late:
        out_shape.append(pltpu.VMEM((amplitudes.shape[0] - late, virtuals), amplitudes.dtype))
        scratch.append(pltpu.SemaphoreType.DMA((2,)))
        extra.append(amplitudes)
    return pl.pallas_call(
        functools.partial(fold_kernel, chunk, late),
        out_shape=out_shape,
        in_specs=[pl.BlockSpec(memory_space=pltpu.SMEM)] + [anywhere] * (2 + len(extra)),
        out_specs=[vmem] * len(out_shape),
        scratch_shapes=scratch,
        compiler_params=pltpu.CompilerParams(vmem_limit_bytes=8 * MIB),
        cost_estimate=NOTHING,
        name="fold_panel",
    )(pair, sizes, pltpu.with_memory_space_constraint(panel, pltpu.HBM), *extra)


def place_panel(slot, folded, ranges, dense, turned):
    quarter, fold = folded.shape
    virtuals = dense.shape[0]
    width = turned.shape[1]
    columns = slice(slot * width, (slot + 1) * width)
    step = 32
    values = folded[...].astype(jnp.float32)
    if width > quarter:
        values = jnp.concatenate([values, jnp.zeros((width - quarter, fold), jnp.float32)])
    turned[...] = values.T
    low = jnp.concatenate([ranges[0, :, columns]] * (step // 8))
    high = jnp.concatenate([ranges[1, :, columns]] * (step // 8))

    @pl.loop(0, virtuals // step, unroll=4)
    def _(i):
        row = pl.multiple_of(i * step, step)
        source = pl.multiple_of(lax.rem(row, fold), step)
        c = row + lax.broadcasted_iota(jnp.int32, (step, width), 0)
        kept = jnp.where((c >= low) & (c < high), turned[pl.ds(source, step), :], 0.0)
        dense[pl.ds(row, step), columns] = kept.astype(dense.dtype)


def first_spread_kernel(
    groups, sizes, pair, folded, fock, dense, fock_out, ranges, token, bounds, turned, sems
):
    quarter = folded.shape[0]
    virtuals = dense.shape[0]
    width = turned.shape[1]
    group = lax.axis_index("grp")
    copies = []
    for k in range(groups):
        start = pl.multiple_of(jnp.bitwise_xor(group, k) * quarter, SUBLANES)
        copies.append(pltpu.make_async_copy(
            fock.at[pl.ds(start, quarter)], fock_out.at[pl.ds(k * width, quarter)], sems.at[k]
        ))
        copies[-1].start()
        if width > quarter:
            fock_out[k * width + quarter:(k + 1) * width, :] = jnp.zeros(
                (width - quarter, virtuals), fock_out.dtype
            )
    token[...] = jnp.zeros_like(token)
    fill_bounds(sizes, bounds)
    for k in range(groups):
        start = jnp.bitwise_xor(group, k) * quarter
        b = start + lax.broadcasted_iota(jnp.int32, (8, width), 1)
        low, high = wanted_range(b, pair, bounds, sizes.shape[0])
        ranges[0, :, k * width:(k + 1) * width] = low
        ranges[1, :, k * width:(k + 1) * width] = high
    place_panel(0, folded, ranges, dense, turned)
    for copy in copies:
        copy.wait()


def first_spread(groups, folded, fock, sizes, pair):
    quarter, fold = folded.shape
    virtuals = fock.shape[0]
    width = rounded(quarter, LANES)
    smem = pl.BlockSpec(memory_space=pltpu.SMEM)
    vmem = pl.BlockSpec(memory_space=pltpu.VMEM)
    return pl.pallas_call(
        functools.partial(first_spread_kernel, groups),
        out_shape=[
            pltpu.VMEM((virtuals, groups * width), folded.dtype),
            pltpu.VMEM((groups * width, virtuals), fock.dtype),
            pltpu.VMEM((2, 8, groups * width), jnp.int32),
            TOKEN,
        ],
        in_specs=[smem, smem, vmem, pl.BlockSpec(memory_space=pl.ANY)],
        out_specs=[vmem] * 4,
        scratch_shapes=[
            pltpu.SMEM((sizes.shape[0] + 1,), jnp.int32),
            pltpu.VMEM((fold, width), jnp.float32),
            pltpu.SemaphoreType.DMA((groups,)),
        ],
        compiler_params=pltpu.CompilerParams(vmem_limit_bytes=8 * MIB),
        cost_estimate=NOTHING,
        name="first_spread",
    )(sizes, pair, folded, pltpu.with_memory_space_constraint(fock, pltpu.HBM))


def spread_kernel(slot, folded, ranges, before, dense, turned):
    place_panel(slot, folded, ranges, dense, turned)


def spread(slot, folded, ranges, dense):
    fold = folded.shape[1]
    width = rounded(folded.shape[0], LANES)
    vmem = pl.BlockSpec(memory_space=pltpu.VMEM)
    pinned = [pltpu.with_memory_space_constraint(x, pltpu.VMEM) for x in (ranges, dense)]
    return pl.pallas_call(
        functools.partial(spread_kernel, slot),
        out_shape=pltpu.VMEM(dense.shape, dense.dtype),
        in_specs=[vmem, vmem, pl.BlockSpec(memory_space=pl.ANY)],
        out_specs=vmem,
        input_output_aliases={2: 0},
        scratch_shapes=[pltpu.VMEM((fold, width), jnp.float32)],
        compiler_params=pltpu.CompilerParams(vmem_limit_bytes=8 * MIB),
        cost_estimate=NOTHING,
        name="spread_panel",
    )(folded, *pinned)


def after(array, *others):
    anywhere = pl.BlockSpec(memory_space=pl.ANY)
    return pl.pallas_call(
        lambda *refs: None,
        out_shape=jax.ShapeDtypeStruct(array.shape, array.dtype),
        in_specs=[anywhere] * (1 + len(others)),
        out_specs=anywhere,
        input_output_aliases={0: 0},
        compiler_params=pltpu.CompilerParams(vmem_limit_bytes=MIB),
        cost_estimate=NOTHING,
        name="after",
    )(array, *others)


def owned_kernel(members, received, kept, *refs):
    out, sem = refs[-2:]

    @pl.when(lax.div(lax.axis_index("blk"), members) == lax.axis_index("grp"))
    def _():
        copy = pltpu.make_async_copy(kept, out, sem)
        copy.start()
        copy.wait()


def owned(received, kept, members, *others):
    anywhere = pl.BlockSpec(memory_space=pl.ANY)
    return pl.pallas_call(
        functools.partial(owned_kernel, members),
        out_shape=jax.ShapeDtypeStruct(received.shape, received.dtype),
        in_specs=[anywhere] * (2 + len(others)),
        out_specs=anywhere,
        input_output_aliases={0: 0},
        scratch_shapes=[pltpu.SemaphoreType.DMA],
        compiler_params=pltpu.CompilerParams(vmem_limit_bytes=MIB),
        cost_estimate=NOTHING,
        name="owned_rows",
    )(received, kept, *others)


def column_tiles(total, tile):
    return [(first, min(tile, total - first)) for first in range(0, total, tile)]


def dress_kernel(job, amplitudes, dense, fock, *refs):
    columns, spans, rows, members, has_sums, has_base, signed = job
    if has_sums:
        sums, refs = refs[0], refs[1:]
    refs = refs[has_base:]
    result, refs = refs[0], refs[1:]
    if signed:
        refs[0][...] = jnp.zeros_like(refs[0])
        refs = refs[1:]
    virtuals = dense.shape[0]
    begin, end = columns
    coupled = refs[0]
    for first, tile in column_tiles(end - begin, 512):
        coupled[:, first:first + tile] = jnp.dot(
            amplitudes[...], dense[:, begin + first:begin + first + tile],
            preferred_element_type=jnp.float32,
        ).astype(coupled.dtype)
    if spans:
        dressed, sems = refs[1:]
        block = lax.axis_index("blk")
        places = [
            pl.multiple_of(lax.rem(block + by, members) * rows + offset, SUBLANES)
            for by, offset, _ in spans
        ]
    copies = []
    for t, (first, tile) in enumerate(column_tiles(virtuals, 512)):
        here = slice(first, first + tile)
        total = jnp.dot(
            coupled[...], fock[begin:end, here], preferred_element_type=jnp.float32
        )
        if has_sums:
            total = total + sums[:, here]
        if not spans:
            result[:, here] = total
            continue
        dressed[:, here] = total.astype(dressed.dtype)
        top = 0
        for p, (_, _, size) in enumerate(spans):
            copies.append(pltpu.make_async_copy(
                dressed.at[pl.ds(top, size), pl.ds(first, tile)],
                result.at[pl.ds(places[p], size), pl.ds(first, tile)],
                sems.at[p, t],
            ))
            copies[-1].start()
            top += size
    for copy in copies:
        copy.wait()


def dress(amplitudes, dense, fock, *, columns=None, sums=None, spans=(), base=None, rows=0, members=1,
          out_rows=0, signed=False):
    height, virtuals = amplitudes.shape
    begin, end = columns or (0, dense.shape[1])
    vmem = pl.BlockSpec(memory_space=pltpu.VMEM)
    anywhere = pl.BlockSpec(memory_space=pl.ANY)
    pinned = [dense, fock] + ([] if sums is None else [sums])
    pinned = [pltpu.with_memory_space_constraint(x, pltpu.VMEM) for x in pinned]
    bases = [] if base is None else [base]
    scratch = [pltpu.VMEM((height, end - begin), amplitudes.dtype)]
    if spans:
        out_shape = [jax.ShapeDtypeStruct((out_rows, virtuals), amplitudes.dtype)]
        scratch += [
            pltpu.VMEM((height, virtuals), amplitudes.dtype),
            pltpu.SemaphoreType.DMA((len(spans), len(column_tiles(virtuals, 512)))),
        ]
    else:
        out_shape = [pltpu.VMEM((height, virtuals), jnp.float32)]
    job = ((begin, end), spans, rows, members, sums is not None, base is not None, signed)
    return pl.pallas_call(
        functools.partial(dress_kernel, job),
        out_shape=out_shape + [TOKEN] * signed,
        in_specs=[vmem] * (1 + len(pinned)) + [anywhere] * len(bases),
        out_specs=[anywhere if spans else vmem] + [vmem] * signed,
        input_output_aliases={} if base is None else {1 + len(pinned): 0},
        scratch_shapes=scratch,
        compiler_params=pltpu.CompilerParams(vmem_limit_bytes=16 * MIB),
        cost_estimate=NOTHING,
        name="dress_rows",
    )(amplitudes, *pinned, *bases)


def make_local(blocks, groups):
    members = blocks // groups
    axes = ("blk", "grp")

    def device(hi, lo, grp):
        return (hi * members + lo) * groups + grp

    everyone = [(h, l, g) for h in range(groups) for l in range(members) for g in range(groups)]

    if groups == 4:
        copies = ((None, 0, 3, 1), (0, None, 1, 3), (0, 2, None, 3), (2, 0, 3, None))
    else:
        copies = [[None if h == g else h for h in range(groups)] for g in range(groups)]
    to_group = [
        (device(g, l, copies[g][h]), device(h, l, g)) for h, l, g in everyone if h != g
    ]

    def to_member(by):
        return [(device(h, (l + by) % members, g), device(h, l, g)) for h, l, g in everyone]

    def to_slot(slot):
        return [(device(h, l, g ^ slot), device(h, l, g)) for h, l, g in everyone]

    def local(amplitudes, hole_panel, virt_fock, irrep_sizes, pair_irreps):
        rows, virtuals = amplitudes.shape
        out_rows = rows * members
        fold = rounded(virtuals // 4, LANES)
        panel = jnp.swapaxes(hole_panel[:, 0, :], 0, 1)
        irrep_sizes = pltpu.with_memory_space_constraint(irrep_sizes, pltpu.HBM)

        early = rounded(rows * 2 // 3, SUBLANES) if rows % SUBLANES == 0 else 0
        if early:
            amplitudes = pltpu.with_memory_space_constraint(amplitudes, pltpu.HBM)
            top = cut(amplitudes, early)
        else:
            top = amplitudes
        own, own_again, *low = fold_panel(panel, irrep_sizes, pair_irreps, fold, amplitudes, early)
        across = lax.ppermute(own, axes, to_slot(2))
        beside = lax.ppermute(own_again, axes, to_slot(1))
        if early:
            low = low[0]
            swapped = [lax.ppermute(low, axes, to_member(by)) for by in range(1, members)]

        dense, fock, ranges, token = first_spread(groups, own, virt_fock, irrep_sizes, pair_irreps)
        top = owned(lax.ppermute(top, axes, to_group), top, members, token)
        if early:
            lows = jnp.concatenate([after(piece, top) for piece in [low] + swapped])
            late = lax.ppermute(lows, axes, to_group)
        tops = [top] + [lax.ppermute(top, axes, to_member(by)) for by in range(1, members)]
        dense = spread(1, beside, ranges, dense)
        near = 2 * dense.shape[1] // groups
        if early:
            sums, token = dress(top, dense, fock, columns=(0, near), signed=True)
            across = after(across, token)
        both = lax.ppermute(across, axes, to_slot(1))
        dense = spread(2, across, ranges, dense)
        dense = spread(3, both, ranges, dense)

        if early:
            place = dict(rows=rows, members=members, out_rows=out_rows)
            result, = dress(
                top, dense, fock, columns=(near, dense.shape[1]), sums=sums, spans=((0, 0, early),),
                **place,
            )
            for by in range(1, members):
                result, *token = dress(
                    tops[by], dense, fock, spans=((by, 0, early),), base=result,
                    signed=by == members - 1, **place,
                )
            lows = owned(late, lows, members, *token)
            spans = tuple((by, early, rows - early) for by in range(members))
            result, = dress(lows, dense, fock, spans=spans, base=result, **place)
        else:
            member = lax.axis_index("blk") % members
            ordered = jnp.roll(jnp.stack(tops), member, axis=0).reshape(out_rows, virtuals)
            result, = dress(ordered, dense, fock, spans=((0, 0, out_rows),), out_rows=out_rows)
        return result[:, None, :]

    return local


def solution(mesh):
    in_specs = (P("blk", None), P(None, "blk", "grp"), P(), P(), P("blk"))
    out_specs = P("grp", "blk", None)
    local = make_local(mesh.shape["blk"], mesh.shape["grp"])
    return jax.shard_map(local, mesh=mesh, in_specs=in_specs, out_specs=out_specs, check_vma=False)
```

```python
import functools

import jax
import jax.numpy as jnp
from jax import lax
from jax.experimental import pallas as pl
from jax.experimental.pallas import tpu as pltpu
from jax.sharding import PartitionSpec as P

LANES = 128
SUBLANES = 16
MIB = 1 << 20
TOKEN = pltpu.VMEM((8, LANES), jnp.int32)
NOTHING = pl.CostEstimate(flops=0, bytes_accessed=0, transcendentals=0)


def rounded(value, unit):
    return -(-value // unit) * unit


def fill_bounds(sizes, bounds):
    total = jnp.int32(0)
    for r in range(sizes.shape[0]):
        bounds[r] = total
        total = total + sizes[r]
    bounds[sizes.shape[0]] = total


def wanted_range(b, pair, bounds, irreps):
    low, high = jnp.zeros_like(b), jnp.zeros_like(b)
    for r in range(irreps):
        partner = jnp.bitwise_xor(pair[0], r)
        inside = (b >= bounds[r]) & (b < bounds[r + 1])
        low = jnp.where(inside, bounds[partner], low)
        high = jnp.where(inside, bounds[partner + 1], high)
    return low, high


def copies_of(source, first, target, sems):
    count = sems.shape[0]
    step = rounded(-(-target.shape[0] // count), SUBLANES)
    copies = []
    for k, begin in enumerate(range(0, target.shape[0], step)):
        size = min(step, target.shape[0] - begin)
        copies.append(pltpu.make_async_copy(
            source.at[pl.ds(first + begin, size)], target.at[pl.ds(begin, size)], sems.at[k]
        ))
        copies[-1].start()
    return copies


def cut_kernel(whole, top, low, sems, low_sems):
    copies = copies_of(whole, 0, top, sems) + copies_of(whole, top.shape[0], low, low_sems)
    for copy in copies:
        copy.wait()


def cut(whole, size):
    vmem = pl.BlockSpec(memory_space=pltpu.VMEM)
    return pl.pallas_call(
        cut_kernel,
        out_shape=[
            pltpu.VMEM((height, whole.shape[1]), whole.dtype)
            for height in (size, whole.shape[0] - size)
        ],
        in_specs=[pl.BlockSpec(memory_space=pl.ANY)],
        out_specs=[vmem] * 2,
        scratch_shapes=[pltpu.SemaphoreType.DMA((3,)), pltpu.SemaphoreType.DMA((2,))],
        compiler_params=pltpu.CompilerParams(vmem_limit_bytes=4 * MIB),
        cost_estimate=NOTHING,
        name="cut_rows",
    )(whole)


def fold_kernel(chunk, pair, sizes_in, source, folded, again, panel, sizes, bounds, sems):
    quarter, virtuals = panel.shape
    fold = folded.shape[1]
    small = pltpu.make_async_copy(sizes_in, sizes, sems.at[quarter // chunk])
    small.start()
    copies = []
    for k in range(quarter // chunk):
        rows = pl.ds(k * chunk, chunk)
        copies.append(pltpu.make_async_copy(source.at[rows], panel.at[rows], sems.at[k]))
        copies[-1].start()
    small.wait()
    fill_bounds(sizes, bounds)
    start = lax.axis_index("grp") * quarter
    step = 32 if chunk % 32 == 0 else SUBLANES
    for k, copy in enumerate(copies):
        copy.wait()

        @pl.loop(0, chunk // step, unroll=True)
        def _(i):
            first = pl.multiple_of(k * chunk + i * step, SUBLANES)
            here = pl.ds(first, step)
            b = start + first + lax.broadcasted_iota(jnp.int32, (step, LANES), 0)
            low, high = wanted_range(b, pair, bounds, sizes.shape[0])
            lane = lax.broadcasted_iota(jnp.int32, (step, LANES), 1)
            low, high = low - lane, high - lane
            for place in range(0, fold, LANES):
                total = jnp.zeros((step, LANES), jnp.float32)
                for c in range(place, virtuals, fold):
                    value = panel[here, c:c + LANES].astype(jnp.float32)
                    total = jnp.where((low <= c) & (high > c), value, total)
                total = total.astype(folded.dtype)
                folded[here, place:place + LANES] = total
                again[here, place:place + LANES] = total


def fold_panel(panel, sizes, pair, fold):
    quarter, virtuals = panel.shape
    chunk = quarter // 5 if quarter % (5 * SUBLANES) == 0 else quarter
    vmem = pl.BlockSpec(memory_space=pltpu.VMEM)
    anywhere = pl.BlockSpec(memory_space=pl.ANY)
    out_shape = [pltpu.VMEM((quarter, fold), panel.dtype)] * 2
    scratch = [
        pltpu.VMEM((quarter, virtuals), panel.dtype),
        pltpu.SMEM(sizes.shape, jnp.int32),
        pltpu.SMEM((sizes.shape[0] + 1,), jnp.int32),
        pltpu.SemaphoreType.DMA((quarter // chunk + 1,)),
    ]
    return pl.pallas_call(
        functools.partial(fold_kernel, chunk),
        out_shape=out_shape,
        in_specs=[pl.BlockSpec(memory_space=pltpu.SMEM)] + [anywhere] * 2,
        out_specs=[vmem] * 2,
        scratch_shapes=scratch,
        compiler_params=pltpu.CompilerParams(vmem_limit_bytes=8 * MIB),
        cost_estimate=NOTHING,
        name="fold_panel",
    )(pair, sizes, pltpu.with_memory_space_constraint(panel, pltpu.HBM))


def place_panel(slot, folded, ranges, dense, turned):
    quarter, fold = folded.shape
    virtuals = dense.shape[0]
    width = turned.shape[1]
    columns = slice(slot * width, (slot + 1) * width)
    step = 32
    values = folded[...].astype(jnp.float32)
    if width > quarter:
        values = jnp.concatenate([values, jnp.zeros((width - quarter, fold), jnp.float32)])
    turned[...] = values.T
    low = jnp.concatenate([ranges[0, :, columns]] * (step // 8))
    high = jnp.concatenate([ranges[1, :, columns]] * (step // 8))

    @pl.loop(0, virtuals // step, unroll=4)
    def _(i):
        row = pl.multiple_of(i * step, step)
        source = pl.multiple_of(lax.rem(row, fold), step)
        c = row + lax.broadcasted_iota(jnp.int32, (step, width), 0)
        kept = jnp.where((c >= low) & (c < high), turned[pl.ds(source, step), :], 0.0)
        dense[pl.ds(row, step), columns] = kept.astype(dense.dtype)


def first_spread_kernel(
    groups, sizes, pair, folded, fock, dense, fock_out, ranges, token, bounds, turned, sems
):
    quarter = folded.shape[0]
    virtuals = dense.shape[0]
    width = turned.shape[1]
    group = lax.axis_index("grp")
    copies = []
    for k in range(groups):
        start = pl.multiple_of(jnp.bitwise_xor(group, k) * quarter, SUBLANES)
        copies.append(pltpu.make_async_copy(
            fock.at[pl.ds(start, quarter)], fock_out.at[pl.ds(k * width, quarter)], sems.at[k]
        ))
        copies[-1].start()
        if width > quarter:
            fock_out[k * width + quarter:(k + 1) * width, :] = jnp.zeros(
                (width - quarter, virtuals), fock_out.dtype
            )
    token[...] = jnp.zeros_like(token)
    fill_bounds(sizes, bounds)
    for k in range(groups):
        start = jnp.bitwise_xor(group, k) * quarter
        b = start + lax.broadcasted_iota(jnp.int32, (8, width), 1)
        low, high = wanted_range(b, pair, bounds, sizes.shape[0])
        ranges[0, :, k * width:(k + 1) * width] = low
        ranges[1, :, k * width:(k + 1) * width] = high
    place_panel(0, folded, ranges, dense, turned)
    for copy in copies:
        copy.wait()


def first_spread(groups, folded, fock, sizes, pair):
    quarter, fold = folded.shape
    virtuals = fock.shape[0]
    width = rounded(quarter, LANES)
    smem = pl.BlockSpec(memory_space=pltpu.SMEM)
    vmem = pl.BlockSpec(memory_space=pltpu.VMEM)
    return pl.pallas_call(
        functools.partial(first_spread_kernel, groups),
        out_shape=[
            pltpu.VMEM((virtuals, groups * width), folded.dtype),
            pltpu.VMEM((groups * width, virtuals), fock.dtype),
            pltpu.VMEM((2, 8, groups * width), jnp.int32),
            TOKEN,
        ],
        in_specs=[smem, smem, vmem, pl.BlockSpec(memory_space=pl.ANY)],
        out_specs=[vmem] * 4,
        scratch_shapes=[
            pltpu.SMEM((sizes.shape[0] + 1,), jnp.int32),
            pltpu.VMEM((fold, width), jnp.float32),
            pltpu.SemaphoreType.DMA((groups,)),
        ],
        compiler_params=pltpu.CompilerParams(vmem_limit_bytes=8 * MIB),
        cost_estimate=NOTHING,
        name="first_spread",
    )(sizes, pair, folded, pltpu.with_memory_space_constraint(fock, pltpu.HBM))


def spread_kernel(slot, folded, ranges, before, dense, turned):
    place_panel(slot, folded, ranges, dense, turned)


def spread(slot, folded, ranges, dense):
    fold = folded.shape[1]
    width = rounded(folded.shape[0], LANES)
    vmem = pl.BlockSpec(memory_space=pltpu.VMEM)
    pinned = [pltpu.with_memory_space_constraint(x, pltpu.VMEM) for x in (ranges, dense)]
    return pl.pallas_call(
        functools.partial(spread_kernel, slot),
        out_shape=pltpu.VMEM(dense.shape, dense.dtype),
        in_specs=[vmem, vmem, pl.BlockSpec(memory_space=pl.ANY)],
        out_specs=vmem,
        input_output_aliases={2: 0},
        scratch_shapes=[pltpu.VMEM((fold, width), jnp.float32)],
        compiler_params=pltpu.CompilerParams(vmem_limit_bytes=8 * MIB),
        cost_estimate=NOTHING,
        name="spread_panel",
    )(folded, *pinned)


def after(array, *others):
    anywhere = pl.BlockSpec(memory_space=pl.ANY)
    return pl.pallas_call(
        lambda *refs: None,
        out_shape=jax.ShapeDtypeStruct(array.shape, array.dtype),
        in_specs=[anywhere] * (1 + len(others)),
        out_specs=anywhere,
        input_output_aliases={0: 0},
        compiler_params=pltpu.CompilerParams(vmem_limit_bytes=MIB),
        cost_estimate=NOTHING,
        name="after",
    )(array, *others)


def owned_kernel(members, received, kept, *refs):
    out, sem = refs[-2:]

    @pl.when(lax.div(lax.axis_index("blk"), members) == lax.axis_index("grp"))
    def _():
        copy = pltpu.make_async_copy(kept, out, sem)
        copy.start()
        copy.wait()


def owned(received, kept, members, *others):
    anywhere = pl.BlockSpec(memory_space=pl.ANY)
    return pl.pallas_call(
        functools.partial(owned_kernel, members),
        out_shape=jax.ShapeDtypeStruct(received.shape, received.dtype),
        in_specs=[anywhere] * (2 + len(others)),
        out_specs=anywhere,
        input_output_aliases={0: 0},
        scratch_shapes=[pltpu.SemaphoreType.DMA],
        compiler_params=pltpu.CompilerParams(vmem_limit_bytes=MIB),
        cost_estimate=NOTHING,
        name="owned_rows",
    )(received, kept, *others)


def column_tiles(total, tile):
    return [(first, min(tile, total - first)) for first in range(0, total, tile)]


def dress_kernel(job, amplitudes, dense, fock, *refs):
    columns, spans, rows, members, has_sums, has_base, signed = job
    if has_sums:
        sums, refs = refs[0], refs[1:]
    refs = refs[has_base:]
    result, refs = refs[0], refs[1:]
    if signed:
        refs[0][...] = jnp.zeros_like(refs[0])
        refs = refs[1:]
    virtuals = dense.shape[0]
    begin, end = columns
    coupled = refs[0]
    for first, tile in column_tiles(end - begin, 512):
        coupled[:, first:first + tile] = jnp.dot(
            amplitudes[...], dense[:, begin + first:begin + first + tile],
            preferred_element_type=jnp.float32,
        ).astype(coupled.dtype)
    if spans:
        dressed, sems = refs[1:]
        block = lax.axis_index("blk")
        places = [
            pl.multiple_of(lax.rem(block + by, members) * rows + offset, SUBLANES)
            for by, offset, _ in spans
        ]
    copies = []
    for t, (first, tile) in enumerate(column_tiles(virtuals, 512)):
        here = slice(first, first + tile)
        total = jnp.dot(
            coupled[...], fock[begin:end, here], preferred_element_type=jnp.float32
        )
        if has_sums:
            total = total + sums[:, here]
        if not spans:
            result[:, here] = total
            continue
        dressed[:, here] = total.astype(dressed.dtype)
        top = 0
        for p, (_, _, size) in enumerate(spans):
            copies.append(pltpu.make_async_copy(
                dressed.at[pl.ds(top, size), pl.ds(first, tile)],
                result.at[pl.ds(places[p], size), pl.ds(first, tile)],
                sems.at[p, t],
            ))
            copies[-1].start()
            top += size
    for copy in copies:
        copy.wait()


def dress(amplitudes, dense, fock, *, columns=None, sums=None, spans=(), base=None, rows=0, members=1,
          out_rows=0, signed=False):
    height, virtuals = amplitudes.shape
    begin, end = columns or (0, dense.shape[1])
    vmem = pl.BlockSpec(memory_space=pltpu.VMEM)
    anywhere = pl.BlockSpec(memory_space=pl.ANY)
    pinned = [dense, fock] + ([] if sums is None else [sums])
    pinned = [pltpu.with_memory_space_constraint(x, pltpu.VMEM) for x in pinned]
    bases = [] if base is None else [base]
    scratch = [pltpu.VMEM((height, end - begin), amplitudes.dtype)]
    if spans:
        out_shape = [jax.ShapeDtypeStruct((out_rows, virtuals), amplitudes.dtype)]
        scratch += [
            pltpu.VMEM((height, virtuals), amplitudes.dtype),
            pltpu.SemaphoreType.DMA((len(spans), len(column_tiles(virtuals, 512)))),
        ]
    else:
        out_shape = [pltpu.VMEM((height, virtuals), jnp.float32)]
    job = ((begin, end), spans, rows, members, sums is not None, base is not None, signed)
    return pl.pallas_call(
        functools.partial(dress_kernel, job),
        out_shape=out_shape + [TOKEN] * signed,
        in_specs=[vmem] * (1 + len(pinned)) + [anywhere] * len(bases),
        out_specs=[anywhere if spans else vmem] + [vmem] * signed,
        input_output_aliases={} if base is None else {1 + len(pinned): 0},
        scratch_shapes=scratch,
        compiler_params=pltpu.CompilerParams(vmem_limit_bytes=16 * MIB),
        cost_estimate=NOTHING,
        name="dress_rows",
    )(amplitudes, *pinned, *bases)


def make_local(blocks, groups):
    members = blocks // groups
    axes = ("blk", "grp")

    def device(hi, lo, grp):
        return (hi * members + lo) * groups + grp

    everyone = [(h, l, g) for h in range(groups) for l in range(members) for g in range(groups)]

    if groups == 4:
        copies = ((None, 0, 3, 1), (0, None, 1, 3), (0, 2, None, 3), (2, 0, 3, None))
    else:
        copies = [[None if h == g else h for h in range(groups)] for g in range(groups)]
    to_group = [
        (device(g, l, copies[g][h]), device(h, l, g)) for h, l, g in everyone if h != g
    ]

    def to_member(by):
        return [(device(h, (l + by) % members, g), device(h, l, g)) for h, l, g in everyone]

    def to_slot(slot):
        return [(device(h, l, g ^ slot), device(h, l, g)) for h, l, g in everyone]

    def local(amplitudes, hole_panel, virt_fock, irrep_sizes, pair_irreps):
        rows, virtuals = amplitudes.shape
        out_rows = rows * members
        fold = rounded(virtuals // 4, LANES)
        panel = jnp.swapaxes(hole_panel[:, 0, :], 0, 1)
        irrep_sizes = pltpu.with_memory_space_constraint(irrep_sizes, pltpu.HBM)

        early = rounded(rows * 3 // 5, SUBLANES) if rows % SUBLANES == 0 else 0
        if early:
            amplitudes = pltpu.with_memory_space_constraint(amplitudes, pltpu.HBM)
            top, low = cut(amplitudes, early)
        else:
            top = amplitudes
        own, own_again = fold_panel(panel, irrep_sizes, pair_irreps, fold)
        across = lax.ppermute(own, axes, to_slot(2))
        beside = lax.ppermute(own_again, axes, to_slot(1))
        if early:
            swapped = [lax.ppermute(low, axes, to_member(by)) for by in range(1, members)]

        dense, fock, ranges, token = first_spread(groups, own, virt_fock, irrep_sizes, pair_irreps)
        if early:
            lows = jnp.concatenate([after(piece, token) for piece in [low] + swapped])
            late = lax.ppermute(lows, axes, to_group)
        top = owned(lax.ppermute(top, axes, to_group), top, members, token)
        tops = [top] + [lax.ppermute(top, axes, to_member(by)) for by in range(1, members)]
        dense = spread(1, beside, ranges, dense)
        near = 2 * dense.shape[1] // groups
        if early:
            sums, token = dress(top, dense, fock, columns=(0, near), signed=True)
            across = after(across, token)
        both = lax.ppermute(across, axes, to_slot(1))
        dense = spread(2, across, ranges, dense)
        dense = spread(3, both, ranges, dense)

        if early:
            place = dict(rows=rows, members=members, out_rows=out_rows)
            result, = dress(
                top, dense, fock, columns=(near, dense.shape[1]), sums=sums, spans=((0, 0, early),),
                **place,
            )
            for by in range(1, members):
                result, *token = dress(
                    tops[by], dense, fock, spans=((by, 0, early),), base=result,
                    signed=by == members - 1, **place,
                )
            lows = owned(late, lows, members, *token)
            spans = tuple((by, early, rows - early) for by in range(members))
            result, = dress(lows, dense, fock, spans=spans, base=result, **place)
        else:
            member = lax.axis_index("blk") % members
            ordered = jnp.roll(jnp.stack(tops), member, axis=0).reshape(out_rows, virtuals)
            result, = dress(ordered, dense, fock, spans=((0, 0, out_rows),), out_rows=out_rows)
        return result[:, None, :]

    return local


def solution(mesh):
    in_specs = (P("blk", None), P(None, "blk", "grp"), P(), P(), P("blk"))
    out_specs = P("grp", "blk", None)
    local = make_local(mesh.shape["blk"], mesh.shape["grp"])
    return jax.shard_map(local, mesh=mesh, in_specs=in_specs, out_specs=out_specs, check_vma=False)
```

```python
import functools

import jax
import jax.numpy as jnp
from jax import lax
from jax.experimental import pallas as pl
from jax.experimental.pallas import tpu as pltpu
from jax.sharding import PartitionSpec as P

LANES = 128
SUBLANES = 16
MIB = 1 << 20
TOKEN = pltpu.VMEM((8, LANES), jnp.int32)
NOTHING = pl.CostEstimate(flops=0, bytes_accessed=0, transcendentals=0)


def rounded(value, unit):
    return -(-value // unit) * unit


def fill_bounds(sizes, bounds):
    total = jnp.int32(0)
    for r in range(sizes.shape[0]):
        bounds[r] = total
        total = total + sizes[r]
    bounds[sizes.shape[0]] = total


def wanted_range(b, pair, bounds, irreps):
    low, high = jnp.zeros_like(b), jnp.zeros_like(b)
    for r in range(irreps):
        partner = jnp.bitwise_xor(pair[0], r)
        inside = (b >= bounds[r]) & (b < bounds[r + 1])
        low = jnp.where(inside, bounds[partner], low)
        high = jnp.where(inside, bounds[partner + 1], high)
    return low, high


def copies_of(source, first, target, sems):
    count = sems.shape[0]
    step = rounded(-(-target.shape[0] // count), SUBLANES)
    copies = []
    for k, begin in enumerate(range(0, target.shape[0], step)):
        size = min(step, target.shape[0] - begin)
        copies.append(pltpu.make_async_copy(
            source.at[pl.ds(first + begin, size)], target.at[pl.ds(begin, size)], sems.at[k]
        ))
        copies[-1].start()
    return copies


def cut_kernel(whole, piece, sems):
    for copy in copies_of(whole, 0, piece, sems):
        copy.wait()


def cut(whole, size):
    return pl.pallas_call(
        cut_kernel,
        out_shape=pltpu.VMEM((size, whole.shape[1]), whole.dtype),
        in_specs=[pl.BlockSpec(memory_space=pl.ANY)],
        out_specs=pl.BlockSpec(memory_space=pltpu.VMEM),
        scratch_shapes=[pltpu.SemaphoreType.DMA((5,))],
        compiler_params=pltpu.CompilerParams(vmem_limit_bytes=4 * MIB),
        cost_estimate=NOTHING,
        name="cut_rows",
    )(whole)


def fold_kernel(chunk, late, pair, sizes_in, source, *refs):
    if late:
        amplitudes, folded, again, low, panel, sizes, bounds, sems, low_sems = refs
    else:
        folded, again, panel, sizes, bounds, sems = refs
    quarter, virtuals = panel.shape
    fold = folded.shape[1]
    small = pltpu.make_async_copy(sizes_in, sizes, sems.at[quarter // chunk])
    small.start()
    copies = []
    for k in range(quarter // chunk):
        rows = pl.ds(k * chunk, chunk)
        copies.append(pltpu.make_async_copy(source.at[rows], panel.at[rows], sems.at[k]))
        copies[-1].start()
    lows = copies_of(amplitudes, late, low, low_sems) if late else []
    small.wait()
    fill_bounds(sizes, bounds)
    start = lax.axis_index("grp") * quarter
    step = 32 if chunk % 32 == 0 else SUBLANES
    for k, copy in enumerate(copies):
        copy.wait()

        @pl.loop(0, chunk // step, unroll=True)
        def _(i):
            first = pl.multiple_of(k * chunk + i * step, SUBLANES)
            here = pl.ds(first, step)
            b = start + first + lax.broadcasted_iota(jnp.int32, (step, LANES), 0)
            low, high = wanted_range(b, pair, bounds, sizes.shape[0])
            lane = lax.broadcasted_iota(jnp.int32, (step, LANES), 1)
            low, high = low - lane, high - lane
            for place in range(0, fold, LANES):
                total = jnp.zeros((step, LANES), jnp.float32)
                for c in range(place, virtuals, fold):
                    value = panel[here, c:c + LANES].astype(jnp.float32)
                    total = jnp.where((low <= c) & (high > c), value, total)
                total = total.astype(folded.dtype)
                folded[here, place:place + LANES] = total
                again[here, place:place + LANES] = total

    for copy in lows:
        copy.wait()


def fold_panel(panel, sizes, pair, fold, amplitudes, late):
    quarter, virtuals = panel.shape
    chunk = quarter // 5 if quarter % (5 * SUBLANES) == 0 else quarter
    vmem = pl.BlockSpec(memory_space=pltpu.VMEM)
    anywhere = pl.BlockSpec(memory_space=pl.ANY)
    out_shape = [pltpu.VMEM((quarter, fold), panel.dtype)] * 2
    scratch = [
        pltpu.VMEM((quarter, virtuals), panel.dtype),
        pltpu.SMEM(sizes.shape, jnp.int32),
        pltpu.SMEM((sizes.shape[0] + 1,), jnp.int32),
        pltpu.SemaphoreType.DMA((quarter // chunk + 1,)),
    ]
    extra = []
    if late:
        out_shape.append(pltpu.VMEM((amplitudes.shape[0] - late, virtuals), amplitudes.dtype))
        scratch.append(pltpu.SemaphoreType.DMA((2,)))
        extra.append(amplitudes)
    return pl.pallas_call(
        functools.partial(fold_kernel, chunk, late),
        out_shape=out_shape,
        in_specs=[pl.BlockSpec(memory_space=pltpu.SMEM)] + [anywhere] * (2 + len(extra)),
        out_specs=[vmem] * len(out_shape),
        scratch_shapes=scratch,
        compiler_params=pltpu.CompilerParams(vmem_limit_bytes=8 * MIB),
        cost_estimate=NOTHING,
        name="fold_panel",
    )(pair, sizes, pltpu.with_memory_space_constraint(panel, pltpu.HBM), *extra)


def place_panel(slot, folded, ranges, dense, turned):
    quarter, fold = folded.shape
    virtuals = dense.shape[0]
    width = turned.shape[1]
    columns = slice(slot * width, (slot + 1) * width)
    step = 32
    values = folded[...].astype(jnp.float32)
    if width > quarter:
        values = jnp.concatenate([values, jnp.zeros((width - quarter, fold), jnp.float32)])
    turned[...] = values.T
    low = jnp.concatenate([ranges[0, :, columns]] * (step // 8))
    high = jnp.concatenate([ranges[1, :, columns]] * (step // 8))

    @pl.loop(0, virtuals // step, unroll=4)
    def _(i):
        row = pl.multiple_of(i * step, step)
        source = pl.multiple_of(lax.rem(row, fold), step)
        c = row + lax.broadcasted_iota(jnp.int32, (step, width), 0)
        kept = jnp.where((c >= low) & (c < high), turned[pl.ds(source, step), :], 0.0)
        dense[pl.ds(row, step), columns] = kept.astype(dense.dtype)


def first_spread_kernel(
    groups, sizes, pair, folded, fock, dense, fock_out, ranges, token, bounds, turned, sems
):
    quarter = folded.shape[0]
    virtuals = dense.shape[0]
    width = turned.shape[1]
    group = lax.axis_index("grp")
    copies = []
    for k in range(groups):
        start = pl.multiple_of(jnp.bitwise_xor(group, k) * quarter, SUBLANES)
        copies.append(pltpu.make_async_copy(
            fock.at[pl.ds(start, quarter)], fock_out.at[pl.ds(k * width, quarter)], sems.at[k]
        ))
        copies[-1].start()
        if width > quarter:
            fock_out[k * width + quarter:(k + 1) * width, :] = jnp.zeros(
                (width - quarter, virtuals), fock_out.dtype
            )
    token[...] = jnp.zeros_like(token)
    fill_bounds(sizes, bounds)
    for k in range(groups):
        start = jnp.bitwise_xor(group, k) * quarter
        b = start + lax.broadcasted_iota(jnp.int32, (8, width), 1)
        low, high = wanted_range(b, pair, bounds, sizes.shape[0])
        ranges[0, :, k * width:(k + 1) * width] = low
        ranges[1, :, k * width:(k + 1) * width] = high
    place_panel(0, folded, ranges, dense, turned)
    for copy in copies:
        copy.wait()


def first_spread(groups, folded, fock, sizes, pair):
    quarter, fold = folded.shape
    virtuals = fock.shape[0]
    width = rounded(quarter, LANES)
    smem = pl.BlockSpec(memory_space=pltpu.SMEM)
    vmem = pl.BlockSpec(memory_space=pltpu.VMEM)
    return pl.pallas_call(
        functools.partial(first_spread_kernel, groups),
        out_shape=[
            pltpu.VMEM((virtuals, groups * width), folded.dtype),
            pltpu.VMEM((groups * width, virtuals), fock.dtype),
            pltpu.VMEM((2, 8, groups * width), jnp.int32),
            TOKEN,
        ],
        in_specs=[smem, smem, vmem, pl.BlockSpec(memory_space=pl.ANY)],
        out_specs=[vmem] * 4,
        scratch_shapes=[
            pltpu.SMEM((sizes.shape[0] + 1,), jnp.int32),
            pltpu.VMEM((fold, width), jnp.float32),
            pltpu.SemaphoreType.DMA((groups,)),
        ],
        compiler_params=pltpu.CompilerParams(vmem_limit_bytes=8 * MIB),
        cost_estimate=NOTHING,
        name="first_spread",
    )(sizes, pair, folded, pltpu.with_memory_space_constraint(fock, pltpu.HBM))


def spread_kernel(slot, folded, ranges, before, dense, turned):
    place_panel(slot, folded, ranges, dense, turned)


def spread(slot, folded, ranges, dense):
    fold = folded.shape[1]
    width = rounded(folded.shape[0], LANES)
    vmem = pl.BlockSpec(memory_space=pltpu.VMEM)
    pinned = [pltpu.with_memory_space_constraint(x, pltpu.VMEM) for x in (ranges, dense)]
    return pl.pallas_call(
        functools.partial(spread_kernel, slot),
        out_shape=pltpu.VMEM(dense.shape, dense.dtype),
        in_specs=[vmem, vmem, pl.BlockSpec(memory_space=pl.ANY)],
        out_specs=vmem,
        input_output_aliases={2: 0},
        scratch_shapes=[pltpu.VMEM((fold, width), jnp.float32)],
        compiler_params=pltpu.CompilerParams(vmem_limit_bytes=8 * MIB),
        cost_estimate=NOTHING,
        name="spread_panel",
    )(folded, *pinned)


def after(array, *others):
    anywhere = pl.BlockSpec(memory_space=pl.ANY)
    return pl.pallas_call(
        lambda *refs: None,
        out_shape=jax.ShapeDtypeStruct(array.shape, array.dtype),
        in_specs=[anywhere] * (1 + len(others)),
        out_specs=anywhere,
        input_output_aliases={0: 0},
        compiler_params=pltpu.CompilerParams(vmem_limit_bytes=MIB),
        cost_estimate=NOTHING,
        name="after",
    )(array, *others)


def owned_kernel(members, received, kept, *refs):
    out, sem = refs[-2:]

    @pl.when(lax.div(lax.axis_index("blk"), members) == lax.axis_index("grp"))
    def _():
        copy = pltpu.make_async_copy(kept, out, sem)
        copy.start()
        copy.wait()


def owned(received, kept, members, *others):
    anywhere = pl.BlockSpec(memory_space=pl.ANY)
    return pl.pallas_call(
        functools.partial(owned_kernel, members),
        out_shape=jax.ShapeDtypeStruct(received.shape, received.dtype),
        in_specs=[anywhere] * (2 + len(others)),
        out_specs=anywhere,
        input_output_aliases={0: 0},
        scratch_shapes=[pltpu.SemaphoreType.DMA],
        compiler_params=pltpu.CompilerParams(vmem_limit_bytes=MIB),
        cost_estimate=NOTHING,
        name="owned_rows",
    )(received, kept, *others)


def column_tiles(total, tile):
    return [(first, min(tile, total - first)) for first in range(0, total, tile)]


def ending_small(total, tile):
    tiles, first = [], 0
    while first < total:
        left = total - first
        size = tile if left >= 2 * tile or left < 2 * LANES else rounded(left * 2 // 3, LANES)
        size = min(size, tile, left)
        tiles.append((first, size))
        first += size
    return tiles


def dress_kernel(job, amplitudes, dense, fock, *refs):
    columns, spans, rows, members, has_sums, has_base, signed = job
    if has_sums:
        sums, refs = refs[0], refs[1:]
    refs = refs[has_base:]
    result, refs = refs[0], refs[1:]
    if signed:
        refs[0][...] = jnp.zeros_like(refs[0])
        refs = refs[1:]
    virtuals = dense.shape[0]
    begin, end = columns
    coupled = refs[0]
    for first, tile in column_tiles(end - begin, 512):
        coupled[:, first:first + tile] = jnp.dot(
            amplitudes[...], dense[:, begin + first:begin + first + tile],
            preferred_element_type=jnp.float32,
        ).astype(coupled.dtype)
    if spans:
        dressed, sems = refs[1:]
        block = lax.axis_index("blk")
        places = [
            pl.multiple_of(lax.rem(block + by, members) * rows + offset, SUBLANES)
            for by, offset, _ in spans
        ]
    copies = []
    for t, (first, tile) in enumerate(ending_small(virtuals, 512)):
        here = slice(first, first + tile)
        total = jnp.dot(
            coupled[...], fock[begin:end, here], preferred_element_type=jnp.float32
        )
        if has_sums:
            total = total + sums[:, here]
        if not spans:
            result[:, here] = total
            continue
        dressed[:, here] = total.astype(dressed.dtype)
        top = 0
        for p, (_, _, size) in enumerate(spans):
            copies.append(pltpu.make_async_copy(
                dressed.at[pl.ds(top, size), pl.ds(first, tile)],
                result.at[pl.ds(places[p], size), pl.ds(first, tile)],
                sems.at[p, t],
            ))
            copies[-1].start()
            top += size
    for copy in copies:
        copy.wait()


def dress(amplitudes, dense, fock, *, columns=None, sums=None, spans=(), base=None, rows=0, members=1,
          out_rows=0, signed=False):
    height, virtuals = amplitudes.shape
    begin, end = columns or (0, dense.shape[1])
    vmem = pl.BlockSpec(memory_space=pltpu.VMEM)
    anywhere = pl.BlockSpec(memory_space=pl.ANY)
    pinned = [dense, fock] + ([] if sums is None else [sums])
    pinned = [pltpu.with_memory_space_constraint(x, pltpu.VMEM) for x in pinned]
    bases = [] if base is None else [base]
    scratch = [pltpu.VMEM((height, end - begin), amplitudes.dtype)]
    if spans:
        out_shape = [jax.ShapeDtypeStruct((out_rows, virtuals), amplitudes.dtype)]
        scratch += [
            pltpu.VMEM((height, virtuals), amplitudes.dtype),
            pltpu.SemaphoreType.DMA((len(spans), len(ending_small(virtuals, 512)))),
        ]
    else:
        out_shape = [pltpu.VMEM((height, virtuals), jnp.float32)]
    job = ((begin, end), spans, rows, members, sums is not None, base is not None, signed)
    return pl.pallas_call(
        functools.partial(dress_kernel, job),
        out_shape=out_shape + [TOKEN] * signed,
        in_specs=[vmem] * (1 + len(pinned)) + [anywhere] * len(bases),
        out_specs=[anywhere if spans else vmem] + [vmem] * signed,
        input_output_aliases={} if base is None else {1 + len(pinned): 0},
        scratch_shapes=scratch,
        compiler_params=pltpu.CompilerParams(vmem_limit_bytes=16 * MIB),
        cost_estimate=NOTHING,
        name="dress_rows",
    )(amplitudes, *pinned, *bases)


def make_local(blocks, groups):
    members = blocks // groups
    axes = ("blk", "grp")

    def device(hi, lo, grp):
        return (hi * members + lo) * groups + grp

    everyone = [(h, l, g) for h in range(groups) for l in range(members) for g in range(groups)]

    if groups == 4:
        copies = ((None, 0, 3, 1), (2, None, 1, 3), (0, 2, None, 1), (2, 0, 3, None))
    else:
        copies = [[None if h == g else h for h in range(groups)] for g in range(groups)]
    to_group = [
        (device(g, l, copies[g][h]), device(h, l, g)) for h, l, g in everyone if h != g
    ]

    def to_member(by):
        return [(device(h, (l + by) % members, g), device(h, l, g)) for h, l, g in everyone]

    def to_slot(slot):
        return [(device(h, l, g ^ slot), device(h, l, g)) for h, l, g in everyone]

    def local(amplitudes, hole_panel, virt_fock, irrep_sizes, pair_irreps):
        rows, virtuals = amplitudes.shape
        out_rows = rows * members
        fold = rounded(virtuals // 4, LANES)
        panel = jnp.swapaxes(hole_panel[:, 0, :], 0, 1)
        irrep_sizes = pltpu.with_memory_space_constraint(irrep_sizes, pltpu.HBM)

        early = rounded(rows * 2 // 3, SUBLANES) if rows % SUBLANES == 0 else 0
        if early:
            amplitudes = pltpu.with_memory_space_constraint(amplitudes, pltpu.HBM)
            top = cut(amplitudes, early)
        else:
            top = amplitudes
        own, own_again, *low = fold_panel(panel, irrep_sizes, pair_irreps, fold, amplitudes, early)
        across = lax.ppermute(own, axes, to_slot(2))
        beside = lax.ppermute(own_again, axes, to_slot(1))
        if early:
            low = low[0]
            swapped = [lax.ppermute(low, axes, to_member(by)) for by in range(1, members)]

        dense, fock, ranges, token = first_spread(groups, own, virt_fock, irrep_sizes, pair_irreps)
        top = owned(lax.ppermute(top, axes, to_group), top, members, token)
        if early:
            lows = jnp.concatenate([after(piece, top) for piece in [low] + swapped])
            late = lax.ppermute(lows, axes, to_group)
        tops = [top] + [lax.ppermute(top, axes, to_member(by)) for by in range(1, members)]
        dense = spread(1, beside, ranges, dense)
        near = 2 * dense.shape[1] // groups
        if early:
            sums, token = dress(top, dense, fock, columns=(0, near), signed=True)
            across = after(across, token)
        both = lax.ppermute(across, axes, to_slot(1))
        dense = spread(2, across, ranges, dense)
        dense = spread(3, both, ranges, dense)

        if early:
            place = dict(rows=rows, members=members, out_rows=out_rows)
            result, = dress(
                top, dense, fock, columns=(near, dense.shape[1]), sums=sums, spans=((0, 0, early),),
                **place,
            )
            for by in range(1, members):
                result, *token = dress(
                    tops[by], dense, fock, spans=((by, 0, early),), base=result,
                    signed=by == members - 1, **place,
                )
            lows = owned(late, lows, members, *token)
            spans = tuple((by, early, rows - early) for by in range(members))
            result, = dress(lows, dense, fock, spans=spans, base=result, **place)
        else:
            member = lax.axis_index("blk") % members
            ordered = jnp.roll(jnp.stack(tops), member, axis=0).reshape(out_rows, virtuals)
            result, = dress(ordered, dense, fock, spans=((0, 0, out_rows),), out_rows=out_rows)
        return result[:, None, :]

    return local


def solution(mesh):
    in_specs = (P("blk", None), P(None, "blk", "grp"), P(), P(), P("blk"))
    out_specs = P("grp", "blk", None)
    local = make_local(mesh.shape["blk"], mesh.shape["grp"])
    return jax.shard_map(local, mesh=mesh, in_specs=in_specs, out_specs=out_specs, check_vma=False)
```

```python
import functools

import jax
import jax.numpy as jnp
from jax import lax
from jax.experimental import pallas as pl
from jax.experimental.pallas import tpu as pltpu
from jax.sharding import PartitionSpec as P

LANES = 128
SUBLANES = 16
MIB = 1 << 20
TOKEN = pltpu.VMEM((8, LANES), jnp.int32)
NOTHING = pl.CostEstimate(flops=0, bytes_accessed=0, transcendentals=0)


def rounded(value, unit):
    return -(-value // unit) * unit


def fill_bounds(sizes, bounds):
    total = jnp.int32(0)
    for r in range(sizes.shape[0]):
        bounds[r] = total
        total = total + sizes[r]
    bounds[sizes.shape[0]] = total


def wanted_range(b, pair, bounds, irreps):
    low, high = jnp.zeros_like(b), jnp.zeros_like(b)
    for r in range(irreps):
        partner = jnp.bitwise_xor(pair[0], r)
        inside = (b >= bounds[r]) & (b < bounds[r + 1])
        low = jnp.where(inside, bounds[partner], low)
        high = jnp.where(inside, bounds[partner + 1], high)
    return low, high


def copies_of(source, first, target, sems):
    count = sems.shape[0]
    step = rounded(-(-target.shape[0] // count), SUBLANES)
    copies = []
    for k, begin in enumerate(range(0, target.shape[0], step)):
        size = min(step, target.shape[0] - begin)
        copies.append(pltpu.make_async_copy(
            source.at[pl.ds(first + begin, size)], target.at[pl.ds(begin, size)], sems.at[k]
        ))
        copies[-1].start()
    return copies


def cut_kernel(whole, piece, sems):
    for copy in copies_of(whole, 0, piece, sems):
        copy.wait()


def cut(whole, size):
    return pl.pallas_call(
        cut_kernel,
        out_shape=pltpu.VMEM((size, whole.shape[1]), whole.dtype),
        in_specs=[pl.BlockSpec(memory_space=pl.ANY)],
        out_specs=pl.BlockSpec(memory_space=pltpu.VMEM),
        scratch_shapes=[pltpu.SemaphoreType.DMA((5,))],
        compiler_params=pltpu.CompilerParams(vmem_limit_bytes=4 * MIB),
        cost_estimate=NOTHING,
        name="cut_rows",
    )(whole)


def fold_kernel(chunk, late, pair, sizes_in, source, *refs):
    if late:
        amplitudes, folded, again, low, panel, sizes, bounds, sems, low_sems = refs
    else:
        folded, again, panel, sizes, bounds, sems = refs
    quarter, virtuals = panel.shape
    fold = folded.shape[1]
    small = pltpu.make_async_copy(sizes_in, sizes, sems.at[quarter // chunk])
    small.start()
    copies = []
    for k in range(quarter // chunk):
        rows = pl.ds(k * chunk, chunk)
        copies.append(pltpu.make_async_copy(source.at[rows], panel.at[rows], sems.at[k]))
        copies[-1].start()
    lows = copies_of(amplitudes, late, low, low_sems) if late else []
    small.wait()
    fill_bounds(sizes, bounds)
    start = lax.axis_index("grp") * quarter
    step = 32 if chunk % 32 == 0 else SUBLANES
    for k, copy in enumerate(copies):
        copy.wait()

        @pl.loop(0, chunk // step, unroll=True)
        def _(i):
            first = pl.multiple_of(k * chunk + i * step, SUBLANES)
            here = pl.ds(first, step)
            b = start + first + lax.broadcasted_iota(jnp.int32, (step, LANES), 0)
            low, high = wanted_range(b, pair, bounds, sizes.shape[0])
            lane = lax.broadcasted_iota(jnp.int32, (step, LANES), 1)
            low, high = low - lane, high - lane
            for place in range(0, fold, LANES):
                total = jnp.zeros((step, LANES), jnp.float32)
                for c in range(place, virtuals, fold):
                    value = panel[here, c:c + LANES].astype(jnp.float32)
                    total = jnp.where((low <= c) & (high > c), value, total)
                total = total.astype(folded.dtype)
                folded[here, place:place + LANES] = total
                again[here, place:place + LANES] = total

    for copy in lows:
        copy.wait()


def fold_panel(panel, sizes, pair, fold, amplitudes, late):
    quarter, virtuals = panel.shape
    chunk = quarter // 5 if quarter % (5 * SUBLANES) == 0 else quarter
    vmem = pl.BlockSpec(memory_space=pltpu.VMEM)
    anywhere = pl.BlockSpec(memory_space=pl.ANY)
    out_shape = [pltpu.VMEM((quarter, fold), panel.dtype)] * 2
    scratch = [
        pltpu.VMEM((quarter, virtuals), panel.dtype),
        pltpu.SMEM(sizes.shape, jnp.int32),
        pltpu.SMEM((sizes.shape[0] + 1,), jnp.int32),
        pltpu.SemaphoreType.DMA((quarter // chunk + 1,)),
    ]
    extra = []
    if late:
        out_shape.append(pltpu.VMEM((amplitudes.shape[0] - late, virtuals), amplitudes.dtype))
        scratch.append(pltpu.SemaphoreType.DMA((2,)))
        extra.append(amplitudes)
    return pl.pallas_call(
        functools.partial(fold_kernel, chunk, late),
        out_shape=out_shape,
        in_specs=[pl.BlockSpec(memory_space=pltpu.SMEM)] + [anywhere] * (2 + len(extra)),
        out_specs=[vmem] * len(out_shape),
        scratch_shapes=scratch,
        compiler_params=pltpu.CompilerParams(vmem_limit_bytes=8 * MIB),
        cost_estimate=NOTHING,
        name="fold_panel",
    )(pair, sizes, pltpu.with_memory_space_constraint(panel, pltpu.HBM), *extra)


def place_panel(slot, folded, ranges, dense, turned):
    quarter, fold = folded.shape
    virtuals = dense.shape[0]
    width = turned.shape[1]
    columns = slice(slot * width, (slot + 1) * width)
    step = 32
    values = folded[...].astype(jnp.float32)
    if width > quarter:
        values = jnp.concatenate([values, jnp.zeros((width - quarter, fold), jnp.float32)])
    turned[...] = values.T
    low = jnp.concatenate([ranges[0, :, columns]] * (step // 8))
    high = jnp.concatenate([ranges[1, :, columns]] * (step // 8))

    @pl.loop(0, virtuals // step, unroll=4)
    def _(i):
        row = pl.multiple_of(i * step, step)
        source = pl.multiple_of(lax.rem(row, fold), step)
        c = row + lax.broadcasted_iota(jnp.int32, (step, width), 0)
        kept = jnp.where((c >= low) & (c < high), turned[pl.ds(source, step), :], 0.0)
        dense[pl.ds(row, step), columns] = kept.astype(dense.dtype)


def first_spread_kernel(
    groups, sizes, pair, folded, fock, dense, fock_out, ranges, token, bounds, turned, sems
):
    quarter = folded.shape[0]
    virtuals = dense.shape[0]
    width = turned.shape[1]
    group = lax.axis_index("grp")
    copies = []
    for k in range(groups):
        start = pl.multiple_of(jnp.bitwise_xor(group, k) * quarter, SUBLANES)
        copies.append(pltpu.make_async_copy(
            fock.at[pl.ds(start, quarter)], fock_out.at[pl.ds(k * width, quarter)], sems.at[k]
        ))
        copies[-1].start()
        if width > quarter:
            fock_out[k * width + quarter:(k + 1) * width, :] = jnp.zeros(
                (width - quarter, virtuals), fock_out.dtype
            )
    token[...] = jnp.zeros_like(token)
    fill_bounds(sizes, bounds)
    for k in range(groups):
        start = jnp.bitwise_xor(group, k) * quarter
        b = start + lax.broadcasted_iota(jnp.int32, (8, width), 1)
        low, high = wanted_range(b, pair, bounds, sizes.shape[0])
        ranges[0, :, k * width:(k + 1) * width] = low
        ranges[1, :, k * width:(k + 1) * width] = high
    place_panel(0, folded, ranges, dense, turned)
    for copy in copies:
        copy.wait()


def first_spread(groups, folded, fock, sizes, pair):
    quarter, fold = folded.shape
    virtuals = fock.shape[0]
    width = rounded(quarter, LANES)
    smem = pl.BlockSpec(memory_space=pltpu.SMEM)
    vmem = pl.BlockSpec(memory_space=pltpu.VMEM)
    return pl.pallas_call(
        functools.partial(first_spread_kernel, groups),
        out_shape=[
            pltpu.VMEM((virtuals, groups * width), folded.dtype),
            pltpu.VMEM((groups * width, virtuals), fock.dtype),
            pltpu.VMEM((2, 8, groups * width), jnp.int32),
            TOKEN,
        ],
        in_specs=[smem, smem, vmem, pl.BlockSpec(memory_space=pl.ANY)],
        out_specs=[vmem] * 4,
        scratch_shapes=[
            pltpu.SMEM((sizes.shape[0] + 1,), jnp.int32),
            pltpu.VMEM((fold, width), jnp.float32),
            pltpu.SemaphoreType.DMA((groups,)),
        ],
        compiler_params=pltpu.CompilerParams(vmem_limit_bytes=8 * MIB),
        cost_estimate=NOTHING,
        name="first_spread",
    )(sizes, pair, folded, pltpu.with_memory_space_constraint(fock, pltpu.HBM))


def spread_kernel(slot, folded, ranges, before, dense, turned):
    place_panel(slot, folded, ranges, dense, turned)


def spread(slot, folded, ranges, dense):
    fold = folded.shape[1]
    width = rounded(folded.shape[0], LANES)
    vmem = pl.BlockSpec(memory_space=pltpu.VMEM)
    pinned = [pltpu.with_memory_space_constraint(x, pltpu.VMEM) for x in (ranges, dense)]
    return pl.pallas_call(
        functools.partial(spread_kernel, slot),
        out_shape=pltpu.VMEM(dense.shape, dense.dtype),
        in_specs=[vmem, vmem, pl.BlockSpec(memory_space=pl.ANY)],
        out_specs=vmem,
        input_output_aliases={2: 0},
        scratch_shapes=[pltpu.VMEM((fold, width), jnp.float32)],
        compiler_params=pltpu.CompilerParams(vmem_limit_bytes=8 * MIB),
        cost_estimate=NOTHING,
        name="spread_panel",
    )(folded, *pinned)


def after(array, *others):
    anywhere = pl.BlockSpec(memory_space=pl.ANY)
    return pl.pallas_call(
        lambda *refs: None,
        out_shape=jax.ShapeDtypeStruct(array.shape, array.dtype),
        in_specs=[anywhere] * (1 + len(others)),
        out_specs=anywhere,
        input_output_aliases={0: 0},
        compiler_params=pltpu.CompilerParams(vmem_limit_bytes=MIB),
        cost_estimate=NOTHING,
        name="after",
    )(array, *others)


def owned_kernel(members, received, kept, *refs):
    out, sem = refs[-2:]

    @pl.when(lax.div(lax.axis_index("blk"), members) == lax.axis_index("grp"))
    def _():
        copy = pltpu.make_async_copy(kept, out, sem)
        copy.start()
        copy.wait()


def owned(received, kept, members, *others):
    anywhere = pl.BlockSpec(memory_space=pl.ANY)
    return pl.pallas_call(
        functools.partial(owned_kernel, members),
        out_shape=jax.ShapeDtypeStruct(received.shape, received.dtype),
        in_specs=[anywhere] * (2 + len(others)),
        out_specs=anywhere,
        input_output_aliases={0: 0},
        scratch_shapes=[pltpu.SemaphoreType.DMA],
        compiler_params=pltpu.CompilerParams(vmem_limit_bytes=MIB),
        cost_estimate=NOTHING,
        name="owned_rows",
    )(received, kept, *others)


def column_tiles(total, tile):
    return [(first, min(tile, total - first)) for first in range(0, total, tile)]


def dress_kernel(job, amplitudes, dense, fock, *refs):
    columns, spans, rows, members, has_sums, has_base, signed = job
    if has_sums:
        sums, refs = refs[0], refs[1:]
    refs = refs[has_base:]
    result, refs = refs[0], refs[1:]
    if signed:
        refs[0][...] = jnp.zeros_like(refs[0])
        refs = refs[1:]
    virtuals = dense.shape[0]
    begin, end = columns
    coupled = refs[0]
    for first, tile in column_tiles(end - begin, 512):
        coupled[:, first:first + tile] = jnp.dot(
            amplitudes[...], dense[:, begin + first:begin + first + tile],
            preferred_element_type=jnp.float32,
        ).astype(coupled.dtype)
    if spans:
        dressed, sems = refs[1:]
        block = lax.axis_index("blk")
        places = [
            pl.multiple_of(lax.rem(block + by, members) * rows + offset, SUBLANES)
            for by, offset, _ in spans
        ]
    copies = []
    for t, (first, tile) in enumerate(column_tiles(virtuals, 512)):
        here = slice(first, first + tile)
        total = jnp.dot(
            coupled[...], fock[begin:end, here], preferred_element_type=jnp.float32
        )
        if has_sums:
            total = total + sums[:, here]
        if not spans:
            result[:, here] = total
            continue
        dressed[:, here] = total.astype(dressed.dtype)
        top = 0
        for p, (_, _, size) in enumerate(spans):
            copies.append(pltpu.make_async_copy(
                dressed.at[pl.ds(top, size), pl.ds(first, tile)],
                result.at[pl.ds(places[p], size), pl.ds(first, tile)],
                sems.at[p, t],
            ))
            copies[-1].start()
            top += size
    for copy in copies:
        copy.wait()


def dress(amplitudes, dense, fock, *, columns=None, sums=None, spans=(), base=None, rows=0, members=1,
          out_rows=0, signed=False):
    height, virtuals = amplitudes.shape
    begin, end = columns or (0, dense.shape[1])
    vmem = pl.BlockSpec(memory_space=pltpu.VMEM)
    anywhere = pl.BlockSpec(memory_space=pl.ANY)
    pinned = [dense, fock] + ([] if sums is None else [sums])
    pinned = [pltpu.with_memory_space_constraint(x, pltpu.VMEM) for x in pinned]
    bases = [] if base is None else [base]
    scratch = [pltpu.VMEM((height, end - begin), amplitudes.dtype)]
    if spans:
        out_shape = [jax.ShapeDtypeStruct((out_rows, virtuals), amplitudes.dtype)]
        scratch += [
            pltpu.VMEM((height, virtuals), amplitudes.dtype),
            pltpu.SemaphoreType.DMA((len(spans), len(column_tiles(virtuals, 512)))),
        ]
    else:
        out_shape = [pltpu.VMEM((height, virtuals), jnp.float32)]
    job = ((begin, end), spans, rows, members, sums is not None, base is not None, signed)
    return pl.pallas_call(
        functools.partial(dress_kernel, job),
        out_shape=out_shape + [TOKEN] * signed,
        in_specs=[vmem] * (1 + len(pinned)) + [anywhere] * len(bases),
        out_specs=[anywhere if spans else vmem] + [vmem] * signed,
        input_output_aliases={} if base is None else {1 + len(pinned): 0},
        scratch_shapes=scratch,
        compiler_params=pltpu.CompilerParams(vmem_limit_bytes=16 * MIB),
        cost_estimate=NOTHING,
        name="dress_rows",
    )(amplitudes, *pinned, *bases)


def make_local(blocks, groups):
    members = blocks // groups
    axes = ("blk", "grp")

    def device(hi, lo, grp):
        return (hi * members + lo) * groups + grp

    everyone = [(h, l, g) for h in range(groups) for l in range(members) for g in range(groups)]

    if groups == 4:
        early_copies = ((None, 0, 3, 1), (0, None, 1, 3), (0, 2, None, 3), (2, 0, 3, None))
        late_copies = ((None, 0, 1, 3), (0, None, 3, 1), (2, 0, None, 3), (0, 2, 3, None))
    else:
        early_copies = [[None if h == g else h for h in range(groups)] for g in range(groups)]
        late_copies = early_copies

    def to_group(copies):
        return [(device(g, l, copies[g][h]), device(h, l, g)) for h, l, g in everyone if h != g]

    def to_member(by):
        return [(device(h, (l + by) % members, g), device(h, l, g)) for h, l, g in everyone]

    def to_slot(slot):
        return [(device(h, l, g ^ slot), device(h, l, g)) for h, l, g in everyone]

    def local(amplitudes, hole_panel, virt_fock, irrep_sizes, pair_irreps):
        rows, virtuals = amplitudes.shape
        out_rows = rows * members
        fold = rounded(virtuals // 4, LANES)
        panel = jnp.swapaxes(hole_panel[:, 0, :], 0, 1)
        irrep_sizes = pltpu.with_memory_space_constraint(irrep_sizes, pltpu.HBM)

        early = rounded(rows * 2 // 3, SUBLANES) if rows % SUBLANES == 0 else 0
        if early:
            amplitudes = pltpu.with_memory_space_constraint(amplitudes, pltpu.HBM)
            top = cut(amplitudes, early)
        else:
            top = amplitudes
        own, own_again, *low = fold_panel(panel, irrep_sizes, pair_irreps, fold, amplitudes, early)
        across = lax.ppermute(own, axes, to_slot(2))
        beside = lax.ppermute(own_again, axes, to_slot(1))
        if early:
            low = low[0]
            swapped = [lax.ppermute(low, axes, to_member(by)) for by in range(1, members)]

        dense, fock, ranges, token = first_spread(groups, own, virt_fock, irrep_sizes, pair_irreps)
        top = owned(lax.ppermute(top, axes, to_group(early_copies)), top, members, token)
        if early:
            lows = jnp.concatenate([after(piece, top) for piece in [low] + swapped])
            late = lax.ppermute(lows, axes, to_group(late_copies))
        tops = [top] + [lax.ppermute(top, axes, to_member(by)) for by in range(1, members)]
        dense = spread(1, beside, ranges, dense)
        near = 2 * dense.shape[1] // groups
        if early:
            sums, token = dress(top, dense, fock, columns=(0, near), signed=True)
            across = after(across, token)
        both = lax.ppermute(across, axes, to_slot(1))
        dense = spread(2, across, ranges, dense)
        dense = spread(3, both, ranges, dense)

        if early:
            place = dict(rows=rows, members=members, out_rows=out_rows)
            result, = dress(
                top, dense, fock, columns=(near, dense.shape[1]), sums=sums, spans=((0, 0, early),),
                **place,
            )
            for by in range(1, members):
                result, *token = dress(
                    tops[by], dense, fock, spans=((by, 0, early),), base=result,
                    signed=by == members - 1, **place,
                )
            lows = owned(late, lows, members, *token)
            spans = tuple((by, early, rows - early) for by in range(members))
            result, = dress(lows, dense, fock, spans=spans, base=result, **place)
        else:
            member = lax.axis_index("blk") % members
            ordered = jnp.roll(jnp.stack(tops), member, axis=0).reshape(out_rows, virtuals)
            result, = dress(ordered, dense, fock, spans=((0, 0, out_rows),), out_rows=out_rows)
        return result[:, None, :]

    return local


def solution(mesh):
    in_specs = (P("blk", None), P(None, "blk", "grp"), P(), P(), P("blk"))
    out_specs = P("grp", "blk", None)
    local = make_local(mesh.shape["blk"], mesh.shape["grp"])
    return jax.shard_map(local, mesh=mesh, in_specs=in_specs, out_specs=out_specs, check_vma=False)
```

```python
import functools

import jax
import jax.numpy as jnp
from jax import lax
from jax.experimental import pallas as pl
from jax.experimental.pallas import tpu as pltpu
from jax.sharding import PartitionSpec as P

LANES = 128
SUBLANES = 16
MIB = 1 << 20
TOKEN = pltpu.VMEM((8, LANES), jnp.int32)
NOTHING = pl.CostEstimate(flops=0, bytes_accessed=0, transcendentals=0)


def rounded(value, unit):
    return -(-value // unit) * unit


def fill_bounds(sizes, bounds):
    total = jnp.int32(0)
    for r in range(sizes.shape[0]):
        bounds[r] = total
        total = total + sizes[r]
    bounds[sizes.shape[0]] = total


def wanted_range(b, pair, bounds, irreps):
    low, high = jnp.zeros_like(b), jnp.zeros_like(b)
    for r in range(irreps):
        partner = jnp.bitwise_xor(pair[0], r)
        inside = (b >= bounds[r]) & (b < bounds[r + 1])
        low = jnp.where(inside, bounds[partner], low)
        high = jnp.where(inside, bounds[partner + 1], high)
    return low, high


def copies_of(source, first, target, sems):
    count = sems.shape[0]
    step = rounded(-(-target.shape[0] // count), SUBLANES)
    copies = []
    for k, begin in enumerate(range(0, target.shape[0], step)):
        size = min(step, target.shape[0] - begin)
        copies.append(pltpu.make_async_copy(
            source.at[pl.ds(first + begin, size)], target.at[pl.ds(begin, size)], sems.at[k]
        ))
        copies[-1].start()
    return copies


def cut_kernel(whole, piece, sems):
    for copy in copies_of(whole, 0, piece, sems):
        copy.wait()


def cut(whole, size):
    return pl.pallas_call(
        cut_kernel,
        out_shape=pltpu.VMEM((size, whole.shape[1]), whole.dtype),
        in_specs=[pl.BlockSpec(memory_space=pl.ANY)],
        out_specs=pl.BlockSpec(memory_space=pltpu.VMEM),
        scratch_shapes=[pltpu.SemaphoreType.DMA((5,))],
        compiler_params=pltpu.CompilerParams(vmem_limit_bytes=4 * MIB),
        cost_estimate=NOTHING,
        name="cut_rows",
    )(whole)


def fold_kernel(chunk, starts, pair, sizes_in, source, *refs):
    if starts:
        amplitudes, refs, piece_sems = refs[0], refs[1:-1], refs[-1]
    folded, again, *pieces, panel, sizes, bounds, sems = refs
    quarter, virtuals = panel.shape
    fold = folded.shape[1]
    small = pltpu.make_async_copy(sizes_in, sizes, sems.at[quarter // chunk])
    small.start()
    copies = []
    for k in range(quarter // chunk):
        rows = pl.ds(k * chunk, chunk)
        copies.append(pltpu.make_async_copy(source.at[rows], panel.at[rows], sems.at[k]))
        copies[-1].start()
    piece_copies = []
    for k, (first, piece) in enumerate(zip(starts, pieces)):
        piece_copies += copies_of(amplitudes, first, piece, piece_sems.at[pl.ds(2 * k, 2)])
    small.wait()
    fill_bounds(sizes, bounds)
    start = lax.axis_index("grp") * quarter
    step = 32 if chunk % 32 == 0 else SUBLANES
    for k, copy in enumerate(copies):
        copy.wait()

        @pl.loop(0, chunk // step, unroll=True)
        def _(i):
            first = pl.multiple_of(k * chunk + i * step, SUBLANES)
            here = pl.ds(first, step)
            b = start + first + lax.broadcasted_iota(jnp.int32, (step, LANES), 0)
            low, high = wanted_range(b, pair, bounds, sizes.shape[0])
            lane = lax.broadcasted_iota(jnp.int32, (step, LANES), 1)
            low, high = low - lane, high - lane
            for place in range(0, fold, LANES):
                total = jnp.zeros((step, LANES), jnp.float32)
                for c in range(place, virtuals, fold):
                    value = panel[here, c:c + LANES].astype(jnp.float32)
                    total = jnp.where((low <= c) & (high > c), value, total)
                total = total.astype(folded.dtype)
                folded[here, place:place + LANES] = total
                again[here, place:place + LANES] = total

    for copy in piece_copies:
        copy.wait()


def fold_panel(panel, sizes, pair, fold, amplitudes, starts):
    quarter, virtuals = panel.shape
    chunk = quarter // 5 if quarter % (5 * SUBLANES) == 0 else quarter
    vmem = pl.BlockSpec(memory_space=pltpu.VMEM)
    anywhere = pl.BlockSpec(memory_space=pl.ANY)
    out_shape = [pltpu.VMEM((quarter, fold), panel.dtype)] * 2
    scratch = [
        pltpu.VMEM((quarter, virtuals), panel.dtype),
        pltpu.SMEM(sizes.shape, jnp.int32),
        pltpu.SMEM((sizes.shape[0] + 1,), jnp.int32),
        pltpu.SemaphoreType.DMA((quarter // chunk + 1,)),
    ]
    extra = []
    if starts:
        for first, end in zip(starts, (*starts[1:], amplitudes.shape[0])):
            out_shape.append(pltpu.VMEM((end - first, virtuals), amplitudes.dtype))
        scratch.append(pltpu.SemaphoreType.DMA((2 * len(starts),)))
        extra.append(amplitudes)
    return pl.pallas_call(
        functools.partial(fold_kernel, chunk, starts),
        out_shape=out_shape,
        in_specs=[pl.BlockSpec(memory_space=pltpu.SMEM)] + [anywhere] * (2 + len(extra)),
        out_specs=[vmem] * len(out_shape),
        scratch_shapes=scratch,
        compiler_params=pltpu.CompilerParams(vmem_limit_bytes=8 * MIB),
        cost_estimate=NOTHING,
        name="fold_panel",
    )(pair, sizes, pltpu.with_memory_space_constraint(panel, pltpu.HBM), *extra)


def place_panel(slot, parts, ranges, dense, turned):
    quarter, fold = sum(part.shape[0] for part in parts), parts[0].shape[1]
    virtuals = dense.shape[0]
    width = turned.shape[1]
    columns = slice(slot * width, (slot + 1) * width)
    step = 32
    values = [part[...].astype(jnp.float32) for part in parts]
    if width > quarter:
        values.append(jnp.zeros((width - quarter, fold), jnp.float32))
    turned[...] = jnp.concatenate(values).T
    low = jnp.concatenate([ranges[0, :, columns]] * (step // 8))
    high = jnp.concatenate([ranges[1, :, columns]] * (step // 8))

    @pl.loop(0, virtuals // step, unroll=4)
    def _(i):
        row = pl.multiple_of(i * step, step)
        source = pl.multiple_of(lax.rem(row, fold), step)
        c = row + lax.broadcasted_iota(jnp.int32, (step, width), 0)
        kept = jnp.where((c >= low) & (c < high), turned[pl.ds(source, step), :], 0.0)
        dense[pl.ds(row, step), columns] = kept.astype(dense.dtype)


def first_spread_kernel(
    groups, sizes, pair, folded, fock, dense, fock_out, ranges, token, bounds, turned, sems
):
    quarter = folded.shape[0]
    virtuals = dense.shape[0]
    width = turned.shape[1]
    group = lax.axis_index("grp")
    copies = []
    for k in range(groups):
        start = pl.multiple_of(jnp.bitwise_xor(group, k) * quarter, SUBLANES)
        copies.append(pltpu.make_async_copy(
            fock.at[pl.ds(start, quarter)], fock_out.at[pl.ds(k * width, quarter)], sems.at[k]
        ))
        copies[-1].start()
        if width > quarter:
            fock_out[k * width + quarter:(k + 1) * width, :] = jnp.zeros(
                (width - quarter, virtuals), fock_out.dtype
            )
    token[...] = jnp.zeros_like(token)
    fill_bounds(sizes, bounds)
    for k in range(groups):
        start = jnp.bitwise_xor(group, k) * quarter
        b = start + lax.broadcasted_iota(jnp.int32, (8, width), 1)
        low, high = wanted_range(b, pair, bounds, sizes.shape[0])
        ranges[0, :, k * width:(k + 1) * width] = low
        ranges[1, :, k * width:(k + 1) * width] = high
    place_panel(0, [folded], ranges, dense, turned)
    for copy in copies:
        copy.wait()


def first_spread(groups, folded, fock, sizes, pair):
    quarter, fold = folded.shape
    virtuals = fock.shape[0]
    width = rounded(quarter, LANES)
    smem = pl.BlockSpec(memory_space=pltpu.SMEM)
    vmem = pl.BlockSpec(memory_space=pltpu.VMEM)
    return pl.pallas_call(
        functools.partial(first_spread_kernel, groups),
        out_shape=[
            pltpu.VMEM((virtuals, groups * width), folded.dtype),
            pltpu.VMEM((groups * width, virtuals), fock.dtype),
            pltpu.VMEM((2, 8, groups * width), jnp.int32),
            TOKEN,
        ],
        in_specs=[smem, smem, vmem, pl.BlockSpec(memory_space=pl.ANY)],
        out_specs=[vmem] * 4,
        scratch_shapes=[
            pltpu.SMEM((sizes.shape[0] + 1,), jnp.int32),
            pltpu.VMEM((fold, width), jnp.float32),
            pltpu.SemaphoreType.DMA((groups,)),
        ],
        compiler_params=pltpu.CompilerParams(vmem_limit_bytes=8 * MIB),
        cost_estimate=NOTHING,
        name="first_spread",
    )(sizes, pair, folded, pltpu.with_memory_space_constraint(fock, pltpu.HBM))


def spread_kernel(slot, count, *refs):
    parts, (ranges, _, dense, turned) = refs[:count], refs[count:]
    place_panel(slot, parts, ranges, dense, turned)


def spread(slot, parts, ranges, dense):
    fold = parts[0].shape[1]
    width = rounded(sum(part.shape[0] for part in parts), LANES)
    vmem = pl.BlockSpec(memory_space=pltpu.VMEM)
    pinned = [pltpu.with_memory_space_constraint(x, pltpu.VMEM) for x in (ranges, dense)]
    return pl.pallas_call(
        functools.partial(spread_kernel, slot, len(parts)),
        out_shape=pltpu.VMEM(dense.shape, dense.dtype),
        in_specs=[vmem] * (len(parts) + 1) + [pl.BlockSpec(memory_space=pl.ANY)],
        out_specs=vmem,
        input_output_aliases={len(parts) + 1: 0},
        scratch_shapes=[pltpu.VMEM((fold, width), jnp.float32)],
        compiler_params=pltpu.CompilerParams(vmem_limit_bytes=8 * MIB),
        cost_estimate=NOTHING,
        name="spread_panel",
    )(*parts, *pinned)


def after(array, *others):
    anywhere = pl.BlockSpec(memory_space=pl.ANY)
    return pl.pallas_call(
        lambda *refs: None,
        out_shape=jax.ShapeDtypeStruct(array.shape, array.dtype),
        in_specs=[anywhere] * (1 + len(others)),
        out_specs=anywhere,
        input_output_aliases={0: 0},
        compiler_params=pltpu.CompilerParams(vmem_limit_bytes=MIB),
        cost_estimate=NOTHING,
        name="after",
    )(array, *others)


def owned_kernel(members, received, kept, *refs):
    out, sem = refs[-2:]

    @pl.when(lax.div(lax.axis_index("blk"), members) == lax.axis_index("grp"))
    def _():
        copy = pltpu.make_async_copy(kept, out, sem)
        copy.start()
        copy.wait()


def owned(received, kept, members, *others):
    anywhere = pl.BlockSpec(memory_space=pl.ANY)
    return pl.pallas_call(
        functools.partial(owned_kernel, members),
        out_shape=jax.ShapeDtypeStruct(received.shape, received.dtype),
        in_specs=[anywhere] * (2 + len(others)),
        out_specs=anywhere,
        input_output_aliases={0: 0},
        scratch_shapes=[pltpu.SemaphoreType.DMA],
        compiler_params=pltpu.CompilerParams(vmem_limit_bytes=MIB),
        cost_estimate=NOTHING,
        name="owned_rows",
    )(received, kept, *others)


def column_tiles(total, tile):
    return [(first, min(tile, total - first)) for first in range(0, total, tile)]


def dress_kernel(job, amplitudes, dense, fock, *refs):
    columns, spans, rows, members, has_sums, has_base, signed = job
    if has_sums:
        sums, refs = refs[0], refs[1:]
    refs = refs[has_base:]
    result, refs = refs[0], refs[1:]
    if signed:
        refs[0][...] = jnp.zeros_like(refs[0])
        refs = refs[1:]
    virtuals = dense.shape[0]
    begin, end = columns
    coupled = refs[0]
    for first, tile in column_tiles(end - begin, 512):
        coupled[:, first:first + tile] = jnp.dot(
            amplitudes[...], dense[:, begin + first:begin + first + tile],
            preferred_element_type=jnp.float32,
        ).astype(coupled.dtype)
    if spans:
        dressed, sems = refs[1:]
        block = lax.axis_index("blk")
        places = [
            pl.multiple_of(lax.rem(block + by, members) * rows + offset, SUBLANES)
            for by, offset, _ in spans
        ]
    copies = []
    for t, (first, tile) in enumerate(column_tiles(virtuals, 512)):
        here = slice(first, first + tile)
        total = jnp.dot(
            coupled[...], fock[begin:end, here], preferred_element_type=jnp.float32
        )
        if has_sums:
            total = total + sums[:, here]
        if not spans:
            result[:, here] = total
            continue
        dressed[:, here] = total.astype(dressed.dtype)
        top = 0
        for p, (_, _, size) in enumerate(spans):
            copies.append(pltpu.make_async_copy(
                dressed.at[pl.ds(top, size), pl.ds(first, tile)],
                result.at[pl.ds(places[p], size), pl.ds(first, tile)],
                sems.at[p, t],
            ))
            copies[-1].start()
            top += size
    for copy in copies:
        copy.wait()


def dress(amplitudes, dense, fock, *, columns=None, sums=None, spans=(), base=None, rows=0, members=1,
          out_rows=0, signed=False):
    height, virtuals = amplitudes.shape
    begin, end = columns or (0, dense.shape[1])
    vmem = pl.BlockSpec(memory_space=pltpu.VMEM)
    anywhere = pl.BlockSpec(memory_space=pl.ANY)
    pinned = [dense, fock] + ([] if sums is None else [sums])
    pinned = [pltpu.with_memory_space_constraint(x, pltpu.VMEM) for x in pinned]
    bases = [] if base is None else [base]
    scratch = [pltpu.VMEM((height, end - begin), amplitudes.dtype)]
    if spans:
        out_shape = [jax.ShapeDtypeStruct((out_rows, virtuals), amplitudes.dtype)]
        scratch += [
            pltpu.VMEM((height, virtuals), amplitudes.dtype),
            pltpu.SemaphoreType.DMA((len(spans), len(column_tiles(virtuals, 512)))),
        ]
    else:
        out_shape = [pltpu.VMEM((height, virtuals), jnp.float32)]
    job = ((begin, end), spans, rows, members, sums is not None, base is not None, signed)
    return pl.pallas_call(
        functools.partial(dress_kernel, job),
        out_shape=out_shape + [TOKEN] * signed,
        in_specs=[vmem] * (1 + len(pinned)) + [anywhere] * len(bases),
        out_specs=[anywhere if spans else vmem] + [vmem] * signed,
        input_output_aliases={} if base is None else {1 + len(pinned): 0},
        scratch_shapes=scratch,
        compiler_params=pltpu.CompilerParams(vmem_limit_bytes=16 * MIB),
        cost_estimate=NOTHING,
        name="dress_rows",
    )(amplitudes, *pinned, *bases)


def make_local(blocks, groups):
    members = blocks // groups
    axes = ("blk", "grp")

    def device(hi, lo, grp):
        return (hi * members + lo) * groups + grp

    everyone = [(h, l, g) for h in range(groups) for l in range(members) for g in range(groups)]

    if groups == 4:
        copies = ((None, 0, 3, 1), (0, None, 1, 3), (0, 2, None, 3), (2, 0, 3, None))
    else:
        copies = [[None if h == g else h for h in range(groups)] for g in range(groups)]
    to_group = [
        (device(g, l, copies[g][h]), device(h, l, g)) for h, l, g in everyone if h != g
    ]

    def to_member(by):
        return [(device(h, (l + by) % members, g), device(h, l, g)) for h, l, g in everyone]

    def to_slot(slot):
        return [(device(h, l, g ^ slot), device(h, l, g)) for h, l, g in everyone]

    def local(amplitudes, hole_panel, virt_fock, irrep_sizes, pair_irreps):
        rows, virtuals = amplitudes.shape
        out_rows = rows * members
        fold = rounded(virtuals // 4, LANES)
        panel = jnp.swapaxes(hole_panel[:, 0, :], 0, 1)
        irrep_sizes = pltpu.with_memory_space_constraint(irrep_sizes, pltpu.HBM)

        piece = rounded(rows * 2 // 5, SUBLANES) if rows % SUBLANES == 0 else 0
        early = rounded(rows * 7 // 10, SUBLANES)
        if piece:
            amplitudes = pltpu.with_memory_space_constraint(amplitudes, pltpu.HBM)
            first = cut(amplitudes, piece)
            starts = (piece, early)
        else:
            first, starts = amplitudes, ()
        own, own_again, *pieces = fold_panel(
            panel, irrep_sizes, pair_irreps, fold, amplitudes, starts
        )
        across = lax.ppermute(own, axes, to_slot(2))
        beside = lax.ppermute(own_again, axes, to_slot(1))
        if piece:
            second, late = pieces
            lates = [late] + [lax.ppermute(late, axes, to_member(by)) for by in range(1, members)]

        dense, fock, ranges, token = first_spread(groups, own, virt_fock, irrep_sizes, pair_irreps)
        first = owned(lax.ppermute(first, axes, to_group), first, members, token)
        firsts = [lax.ppermute(first, axes, to_member(by)) for by in range(1, members)]
        if piece:
            second = owned(lax.ppermute(second, axes, to_group), second, members, first)
            seconds = [lax.ppermute(second, axes, to_member(by)) for by in range(1, members)]
            lates = jnp.concatenate([after(rows_of, second) for rows_of in lates])
            sent = lax.ppermute(lates, axes, to_group)
        dense = spread(1, [beside], ranges, dense)
        near = 2 * dense.shape[1] // groups
        if piece:
            mine = jnp.concatenate([first, second])
            sums, token = dress(mine, dense, fock, columns=(0, near), signed=True)
            across = after(across, token)
        cuts = [rounded(across.shape[0] // 2, SUBLANES)] if piece else []
        both = [lax.ppermute(part, axes, to_slot(1)) for part in jnp.split(across, cuts)]
        dense = spread(2, [across], ranges, dense)
        dense = spread(3, both, ranges, dense)

        if piece:
            place = dict(rows=rows, members=members, out_rows=out_rows)
            result, token = dress(
                mine, dense, fock, columns=(near, dense.shape[1]), sums=sums,
                spans=((0, 0, early),), signed=True, **place,
            )
            for by in range(1, members):
                other = [after(part, token) for part in (firsts[by - 1], seconds[by - 1])]
                result, token = dress(
                    jnp.concatenate(other), dense, fock,
                    spans=((by, 0, early),), base=result, signed=True, **place,
                )
            lates = owned(sent, lates, members, token)
            spans = tuple((by, early, rows - early) for by in range(members))
            result, = dress(lates, dense, fock, spans=spans, base=result, **place)
        else:
            member = lax.axis_index("blk") % members
            ordered = jnp.roll(jnp.stack([first, *firsts]), member, axis=0).reshape(out_rows, virtuals)
            result, = dress(ordered, dense, fock, spans=((0, 0, out_rows),), out_rows=out_rows)
        return result[:, None, :]

    return local


def solution(mesh):
    in_specs = (P("blk", None), P(None, "blk", "grp"), P(), P(), P("blk"))
    out_specs = P("grp", "blk", None)
    local = make_local(mesh.shape["blk"], mesh.shape["grp"])
    return jax.shard_map(local, mesh=mesh, in_specs=in_specs, out_specs=out_specs, check_vma=False)
```

```python
import functools

import jax
import jax.numpy as jnp
from jax import lax
from jax.experimental import pallas as pl
from jax.experimental.pallas import tpu as pltpu
from jax.sharding import PartitionSpec as P

LANES = 128
SUBLANES = 16
MIB = 1 << 20
TOKEN = pltpu.VMEM((8, LANES), jnp.int32)
NOTHING = pl.CostEstimate(flops=0, bytes_accessed=0, transcendentals=0)


def rounded(value, unit):
    return -(-value // unit) * unit


def fill_bounds(sizes, bounds):
    total = jnp.int32(0)
    for r in range(sizes.shape[0]):
        bounds[r] = total
        total = total + sizes[r]
    bounds[sizes.shape[0]] = total


def wanted_range(b, pair, bounds, irreps):
    low, high = jnp.zeros_like(b), jnp.zeros_like(b)
    for r in range(irreps):
        partner = jnp.bitwise_xor(pair[0], r)
        inside = (b >= bounds[r]) & (b < bounds[r + 1])
        low = jnp.where(inside, bounds[partner], low)
        high = jnp.where(inside, bounds[partner + 1], high)
    return low, high


def copies_of(source, first, target, sems):
    count = sems.shape[0]
    step = rounded(-(-target.shape[0] // count), SUBLANES)
    copies = []
    for k, begin in enumerate(range(0, target.shape[0], step)):
        size = min(step, target.shape[0] - begin)
        copies.append(pltpu.make_async_copy(
            source.at[pl.ds(first + begin, size)], target.at[pl.ds(begin, size)], sems.at[k]
        ))
        copies[-1].start()
    return copies


def cut_kernel(whole, piece, sems):
    for copy in copies_of(whole, 0, piece, sems):
        copy.wait()


def cut(whole, size):
    return pl.pallas_call(
        cut_kernel,
        out_shape=pltpu.VMEM((size, whole.shape[1]), whole.dtype),
        in_specs=[pl.BlockSpec(memory_space=pl.ANY)],
        out_specs=pl.BlockSpec(memory_space=pltpu.VMEM),
        scratch_shapes=[pltpu.SemaphoreType.DMA((5,))],
        compiler_params=pltpu.CompilerParams(vmem_limit_bytes=4 * MIB),
        cost_estimate=NOTHING,
        name="cut_rows",
    )(whole)


def fold_kernel(chunk, starts, pair, sizes_in, source, *refs):
    if starts:
        amplitudes, refs, piece_sems = refs[0], refs[1:-1], refs[-1]
    folded, again, *pieces, panel, sizes, bounds, sems = refs
    quarter, virtuals = panel.shape
    fold = folded.shape[1]
    small = pltpu.make_async_copy(sizes_in, sizes, sems.at[quarter // chunk])
    small.start()
    copies = []
    for k in range(quarter // chunk):
        rows = pl.ds(k * chunk, chunk)
        copies.append(pltpu.make_async_copy(source.at[rows], panel.at[rows], sems.at[k]))
        copies[-1].start()
    piece_copies = []
    for k, (first, piece) in enumerate(zip(starts, pieces)):
        piece_copies += copies_of(amplitudes, first, piece, piece_sems.at[pl.ds(2 * k, 2)])
    small.wait()
    fill_bounds(sizes, bounds)
    start = lax.axis_index("grp") * quarter
    step = 32 if chunk % 32 == 0 else SUBLANES
    for k, copy in enumerate(copies):
        copy.wait()

        @pl.loop(0, chunk // step, unroll=True)
        def _(i):
            first = pl.multiple_of(k * chunk + i * step, SUBLANES)
            here = pl.ds(first, step)
            b = start + first + lax.broadcasted_iota(jnp.int32, (step, LANES), 0)
            low, high = wanted_range(b, pair, bounds, sizes.shape[0])
            lane = lax.broadcasted_iota(jnp.int32, (step, LANES), 1)
            low, high = low - lane, high - lane
            for place in range(0, fold, LANES):
                total = jnp.zeros((step, LANES), jnp.float32)
                for c in range(place, virtuals, fold):
                    value = panel[here, c:c + LANES].astype(jnp.float32)
                    total = jnp.where((low <= c) & (high > c), value, total)
                total = total.astype(folded.dtype)
                folded[here, place:place + LANES] = total
                again[here, place:place + LANES] = total

    for copy in piece_copies:
        copy.wait()


def fold_panel(panel, sizes, pair, fold, amplitudes, starts):
    quarter, virtuals = panel.shape
    chunk = quarter // 5 if quarter % (5 * SUBLANES) == 0 else quarter
    vmem = pl.BlockSpec(memory_space=pltpu.VMEM)
    anywhere = pl.BlockSpec(memory_space=pl.ANY)
    out_shape = [pltpu.VMEM((quarter, fold), panel.dtype)] * 2
    scratch = [
        pltpu.VMEM((quarter, virtuals), panel.dtype),
        pltpu.SMEM(sizes.shape, jnp.int32),
        pltpu.SMEM((sizes.shape[0] + 1,), jnp.int32),
        pltpu.SemaphoreType.DMA((quarter // chunk + 1,)),
    ]
    extra = []
    if starts:
        for first, end in zip(starts, (*starts[1:], amplitudes.shape[0])):
            out_shape.append(pltpu.VMEM((end - first, virtuals), amplitudes.dtype))
        scratch.append(pltpu.SemaphoreType.DMA((2 * len(starts),)))
        extra.append(amplitudes)
    return pl.pallas_call(
        functools.partial(fold_kernel, chunk, starts),
        out_shape=out_shape,
        in_specs=[pl.BlockSpec(memory_space=pltpu.SMEM)] + [anywhere] * (2 + len(extra)),
        out_specs=[vmem] * len(out_shape),
        scratch_shapes=scratch,
        compiler_params=pltpu.CompilerParams(vmem_limit_bytes=8 * MIB),
        cost_estimate=NOTHING,
        name="fold_panel",
    )(pair, sizes, pltpu.with_memory_space_constraint(panel, pltpu.HBM), *extra)


def place_panel(slot, parts, ranges, dense, turned):
    quarter, fold = sum(part.shape[0] for part in parts), parts[0].shape[1]
    virtuals = dense.shape[0]
    width = turned.shape[1]
    columns = slice(slot * width, (slot + 1) * width)
    step = 32
    values = [part[...].astype(jnp.float32) for part in parts]
    if width > quarter:
        values.append(jnp.zeros((width - quarter, fold), jnp.float32))
    turned[...] = jnp.concatenate(values).T
    low = jnp.concatenate([ranges[0, :, columns]] * (step // 8))
    high = jnp.concatenate([ranges[1, :, columns]] * (step // 8))

    @pl.loop(0, virtuals // step, unroll=4)
    def _(i):
        row = pl.multiple_of(i * step, step)
        source = pl.multiple_of(lax.rem(row, fold), step)
        c = row + lax.broadcasted_iota(jnp.int32, (step, width), 0)
        kept = jnp.where((c >= low) & (c < high), turned[pl.ds(source, step), :], 0.0)
        dense[pl.ds(row, step), columns] = kept.astype(dense.dtype)


def first_spread_kernel(
    groups, sizes, pair, folded, fock, dense, fock_out, ranges, token, bounds, turned, sems
):
    quarter = folded.shape[0]
    virtuals = dense.shape[0]
    width = turned.shape[1]
    group = lax.axis_index("grp")
    copies = []
    for k in range(groups):
        start = pl.multiple_of(jnp.bitwise_xor(group, k) * quarter, SUBLANES)
        copies.append(pltpu.make_async_copy(
            fock.at[pl.ds(start, quarter)], fock_out.at[pl.ds(k * width, quarter)], sems.at[k]
        ))
        copies[-1].start()
        if width > quarter:
            fock_out[k * width + quarter:(k + 1) * width, :] = jnp.zeros(
                (width - quarter, virtuals), fock_out.dtype
            )
    token[...] = jnp.zeros_like(token)
    fill_bounds(sizes, bounds)
    for k in range(groups):
        start = jnp.bitwise_xor(group, k) * quarter
        b = start + lax.broadcasted_iota(jnp.int32, (8, width), 1)
        low, high = wanted_range(b, pair, bounds, sizes.shape[0])
        ranges[0, :, k * width:(k + 1) * width] = low
        ranges[1, :, k * width:(k + 1) * width] = high
    place_panel(0, [folded], ranges, dense, turned)
    for copy in copies:
        copy.wait()


def first_spread(groups, folded, fock, sizes, pair):
    quarter, fold = folded.shape
    virtuals = fock.shape[0]
    width = rounded(quarter, LANES)
    smem = pl.BlockSpec(memory_space=pltpu.SMEM)
    vmem = pl.BlockSpec(memory_space=pltpu.VMEM)
    return pl.pallas_call(
        functools.partial(first_spread_kernel, groups),
        out_shape=[
            pltpu.VMEM((virtuals, groups * width), folded.dtype),
            pltpu.VMEM((groups * width, virtuals), fock.dtype),
            pltpu.VMEM((2, 8, groups * width), jnp.int32),
            TOKEN,
        ],
        in_specs=[smem, smem, vmem, pl.BlockSpec(memory_space=pl.ANY)],
        out_specs=[vmem] * 4,
        scratch_shapes=[
            pltpu.SMEM((sizes.shape[0] + 1,), jnp.int32),
            pltpu.VMEM((fold, width), jnp.float32),
            pltpu.SemaphoreType.DMA((groups,)),
        ],
        compiler_params=pltpu.CompilerParams(vmem_limit_bytes=8 * MIB),
        cost_estimate=NOTHING,
        name="first_spread",
    )(sizes, pair, folded, pltpu.with_memory_space_constraint(fock, pltpu.HBM))


def spread_kernel(slot, count, *refs):
    parts, (ranges, _, dense, turned) = refs[:count], refs[count:]
    place_panel(slot, parts, ranges, dense, turned)


def spread(slot, parts, ranges, dense):
    fold = parts[0].shape[1]
    width = rounded(sum(part.shape[0] for part in parts), LANES)
    vmem = pl.BlockSpec(memory_space=pltpu.VMEM)
    pinned = [pltpu.with_memory_space_constraint(x, pltpu.VMEM) for x in (ranges, dense)]
    return pl.pallas_call(
        functools.partial(spread_kernel, slot, len(parts)),
        out_shape=pltpu.VMEM(dense.shape, dense.dtype),
        in_specs=[vmem] * (len(parts) + 1) + [pl.BlockSpec(memory_space=pl.ANY)],
        out_specs=vmem,
        input_output_aliases={len(parts) + 1: 0},
        scratch_shapes=[pltpu.VMEM((fold, width), jnp.float32)],
        compiler_params=pltpu.CompilerParams(vmem_limit_bytes=8 * MIB),
        cost_estimate=NOTHING,
        name="spread_panel",
    )(*parts, *pinned)


def after(array, *others):
    anywhere = pl.BlockSpec(memory_space=pl.ANY)
    return pl.pallas_call(
        lambda *refs: None,
        out_shape=jax.ShapeDtypeStruct(array.shape, array.dtype),
        in_specs=[anywhere] * (1 + len(others)),
        out_specs=anywhere,
        input_output_aliases={0: 0},
        compiler_params=pltpu.CompilerParams(vmem_limit_bytes=MIB),
        cost_estimate=NOTHING,
        name="after",
    )(array, *others)


def owned_kernel(members, received, kept, *refs):
    out, sem = refs[-2:]

    @pl.when(lax.div(lax.axis_index("blk"), members) == lax.axis_index("grp"))
    def _():
        copy = pltpu.make_async_copy(kept, out, sem)
        copy.start()
        copy.wait()


def owned(received, kept, members, *others):
    anywhere = pl.BlockSpec(memory_space=pl.ANY)
    return pl.pallas_call(
        functools.partial(owned_kernel, members),
        out_shape=jax.ShapeDtypeStruct(received.shape, received.dtype),
        in_specs=[anywhere] * (2 + len(others)),
        out_specs=anywhere,
        input_output_aliases={0: 0},
        scratch_shapes=[pltpu.SemaphoreType.DMA],
        compiler_params=pltpu.CompilerParams(vmem_limit_bytes=MIB),
        cost_estimate=NOTHING,
        name="owned_rows",
    )(received, kept, *others)


def column_tiles(total, tile):
    return [(first, min(tile, total - first)) for first in range(0, total, tile)]


def dress_kernel(job, amplitudes, dense, fock, *refs):
    columns, spans, rows, members, has_sums, has_base, signed = job
    if has_sums:
        sums, refs = refs[0], refs[1:]
    refs = refs[has_base:]
    result, refs = refs[0], refs[1:]
    if signed:
        refs[0][...] = jnp.zeros_like(refs[0])
        refs = refs[1:]
    virtuals = dense.shape[0]
    begin, end = columns
    coupled = refs[0]
    for first, tile in column_tiles(end - begin, 512):
        coupled[:, first:first + tile] = jnp.dot(
            amplitudes[...], dense[:, begin + first:begin + first + tile],
            preferred_element_type=jnp.float32,
        ).astype(coupled.dtype)
    if spans:
        dressed, sems = refs[1:]
        block = lax.axis_index("blk")
        places = [
            pl.multiple_of(lax.rem(block + by, members) * rows + offset, SUBLANES)
            for by, offset, _ in spans
        ]
    copies = []
    for t, (first, tile) in enumerate(column_tiles(virtuals, 512)):
        here = slice(first, first + tile)
        total = jnp.dot(
            coupled[...], fock[begin:end, here], preferred_element_type=jnp.float32
        )
        if has_sums:
            total = total + sums[:, here]
        if not spans:
            result[:, here] = total
            continue
        dressed[:, here] = total.astype(dressed.dtype)
        top = 0
        for p, (_, _, size) in enumerate(spans):
            copies.append(pltpu.make_async_copy(
                dressed.at[pl.ds(top, size), pl.ds(first, tile)],
                result.at[pl.ds(places[p], size), pl.ds(first, tile)],
                sems.at[p, t],
            ))
            copies[-1].start()
            top += size
    for copy in copies:
        copy.wait()


def dress(amplitudes, dense, fock, *, columns=None, sums=None, spans=(), base=None, rows=0, members=1,
          out_rows=0, signed=False):
    height, virtuals = amplitudes.shape
    begin, end = columns or (0, dense.shape[1])
    vmem = pl.BlockSpec(memory_space=pltpu.VMEM)
    anywhere = pl.BlockSpec(memory_space=pl.ANY)
    pinned = [dense, fock] + ([] if sums is None else [sums])
    pinned = [pltpu.with_memory_space_constraint(x, pltpu.VMEM) for x in pinned]
    bases = [] if base is None else [base]
    scratch = [pltpu.VMEM((height, end - begin), amplitudes.dtype)]
    if spans:
        out_shape = [jax.ShapeDtypeStruct((out_rows, virtuals), amplitudes.dtype)]
        scratch += [
            pltpu.VMEM((height, virtuals), amplitudes.dtype),
            pltpu.SemaphoreType.DMA((len(spans), len(column_tiles(virtuals, 512)))),
        ]
    else:
        out_shape = [pltpu.VMEM((height, virtuals), jnp.float32)]
    job = ((begin, end), spans, rows, members, sums is not None, base is not None, signed)
    return pl.pallas_call(
        functools.partial(dress_kernel, job),
        out_shape=out_shape + [TOKEN] * signed,
        in_specs=[vmem] * (1 + len(pinned)) + [anywhere] * len(bases),
        out_specs=[anywhere if spans else vmem] + [vmem] * signed,
        input_output_aliases={} if base is None else {1 + len(pinned): 0},
        scratch_shapes=scratch,
        compiler_params=pltpu.CompilerParams(vmem_limit_bytes=16 * MIB),
        cost_estimate=NOTHING,
        name="dress_rows",
    )(amplitudes, *pinned, *bases)


def make_local(blocks, groups):
    members = blocks // groups
    axes = ("blk", "grp")

    def device(hi, lo, grp):
        return (hi * members + lo) * groups + grp

    everyone = [(h, l, g) for h in range(groups) for l in range(members) for g in range(groups)]

    if groups == 4:
        copies = ((None, 0, 3, 1), (0, None, 1, 3), (0, 2, None, 3), (2, 0, 3, None))
    else:
        copies = [[None if h == g else h for h in range(groups)] for g in range(groups)]
    to_group = [
        (device(g, l, copies[g][h]), device(h, l, g)) for h, l, g in everyone if h != g
    ]

    def to_member(by):
        return [(device(h, (l + by) % members, g), device(h, l, g)) for h, l, g in everyone]

    def to_slot(slot):
        return [(device(h, l, g ^ slot), device(h, l, g)) for h, l, g in everyone]

    def local(amplitudes, hole_panel, virt_fock, irrep_sizes, pair_irreps):
        rows, virtuals = amplitudes.shape
        out_rows = rows * members
        fold = rounded(virtuals // 4, LANES)
        panel = jnp.swapaxes(hole_panel[:, 0, :], 0, 1)
        irrep_sizes = pltpu.with_memory_space_constraint(irrep_sizes, pltpu.HBM)

        piece = rounded(rows * 7 // 15, SUBLANES) if rows % SUBLANES == 0 else 0
        early = rounded(rows * 4 // 5, SUBLANES)
        if piece:
            amplitudes = pltpu.with_memory_space_constraint(amplitudes, pltpu.HBM)
            first = cut(amplitudes, piece)
            starts = (piece, early)
        else:
            first, starts = amplitudes, ()
        own, own_again, *pieces = fold_panel(
            panel, irrep_sizes, pair_irreps, fold, amplitudes, starts
        )
        across = lax.ppermute(own, axes, to_slot(2))
        beside = lax.ppermute(own_again, axes, to_slot(1))
        if piece:
            second, late = pieces
            lates = [late] + [lax.ppermute(late, axes, to_member(by)) for by in range(1, members)]

        dense, fock, ranges, token = first_spread(groups, own, virt_fock, irrep_sizes, pair_irreps)
        first = owned(lax.ppermute(first, axes, to_group), first, members, token)
        firsts = [lax.ppermute(first, axes, to_member(by)) for by in range(1, members)]
        if piece:
            second = owned(lax.ppermute(second, axes, to_group), second, members, first)
            seconds = [lax.ppermute(second, axes, to_member(by)) for by in range(1, members)]
            lates = jnp.concatenate([after(rows_of, second) for rows_of in lates])
            sent = lax.ppermute(lates, axes, to_group)
        dense = spread(1, [beside], ranges, dense)
        near = 2 * dense.shape[1] // groups
        if piece:
            mine = jnp.concatenate([first, second])
            sums, token = dress(mine, dense, fock, columns=(0, near), signed=True)
            across = after(across, token)
        cuts = [rounded(across.shape[0] // 2, SUBLANES)] if piece else []
        both = [lax.ppermute(part, axes, to_slot(1)) for part in jnp.split(across, cuts)]
        dense = spread(2, [across], ranges, dense)
        dense = spread(3, both, ranges, dense)

        if piece:
            place = dict(rows=rows, members=members, out_rows=out_rows)
            result, token = dress(
                mine, dense, fock, columns=(near, dense.shape[1]), sums=sums,
                spans=((0, 0, early),), signed=True, **place,
            )
            for by in range(1, members):
                result, token = dress(
                    after(firsts[by - 1], token), dense, fock, spans=((by, 0, piece),), base=result,
                    signed=True, **place,
                )
            last = [after(part, token) for part in seconds] + [owned(sent, lates, members, token)]
            spans = [(by, piece, early - piece) for by in range(1, members)]
            spans += [(by, early, rows - early) for by in range(members)]
            result, = dress(
                jnp.concatenate(last), dense, fock, spans=tuple(spans), base=result, **place
            )
        else:
            member = lax.axis_index("blk") % members
            ordered = jnp.roll(jnp.stack([first, *firsts]), member, axis=0).reshape(out_rows, virtuals)
            result, = dress(ordered, dense, fock, spans=((0, 0, out_rows),), out_rows=out_rows)
        return result[:, None, :]

    return local


def solution(mesh):
    in_specs = (P("blk", None), P(None, "blk", "grp"), P(), P(), P("blk"))
    out_specs = P("grp", "blk", None)
    local = make_local(mesh.shape["blk"], mesh.shape["grp"])
    return jax.shard_map(local, mesh=mesh, in_specs=in_specs, out_specs=out_specs, check_vma=False)
```

```python
import functools

import jax
import jax.numpy as jnp
from jax import lax
from jax.experimental import pallas as pl
from jax.experimental.pallas import tpu as pltpu
from jax.sharding import PartitionSpec as P

LANES = 128
SUBLANES = 16
MIB = 1 << 20
TOKEN = pltpu.VMEM((8, LANES), jnp.int32)
NOTHING = pl.CostEstimate(flops=0, bytes_accessed=0, transcendentals=0)


def rounded(value, unit):
    return -(-value // unit) * unit


def fill_bounds(sizes, bounds):
    total = jnp.int32(0)
    for r in range(sizes.shape[0]):
        bounds[r] = total
        total = total + sizes[r]
    bounds[sizes.shape[0]] = total


def wanted_range(b, pair, bounds, irreps):
    low, high = jnp.zeros_like(b), jnp.zeros_like(b)
    for r in range(irreps):
        partner = jnp.bitwise_xor(pair[0], r)
        inside = (b >= bounds[r]) & (b < bounds[r + 1])
        low = jnp.where(inside, bounds[partner], low)
        high = jnp.where(inside, bounds[partner + 1], high)
    return low, high


def copies_of(source, first, target, sems):
    count = sems.shape[0]
    step = rounded(-(-target.shape[0] // count), SUBLANES)
    copies = []
    for k, begin in enumerate(range(0, target.shape[0], step)):
        size = min(step, target.shape[0] - begin)
        copies.append(pltpu.make_async_copy(
            source.at[pl.ds(first + begin, size)], target.at[pl.ds(begin, size)], sems.at[k]
        ))
        copies[-1].start()
    return copies


def cut_kernel(whole, piece, sems):
    for copy in copies_of(whole, 0, piece, sems):
        copy.wait()


def cut(whole, size):
    return pl.pallas_call(
        cut_kernel,
        out_shape=pltpu.VMEM((size, whole.shape[1]), whole.dtype),
        in_specs=[pl.BlockSpec(memory_space=pl.ANY)],
        out_specs=pl.BlockSpec(memory_space=pltpu.VMEM),
        scratch_shapes=[pltpu.SemaphoreType.DMA((5,))],
        compiler_params=pltpu.CompilerParams(vmem_limit_bytes=4 * MIB),
        cost_estimate=NOTHING,
        name="cut_rows",
    )(whole)


def fold_kernel(chunk, starts, pair, sizes_in, source, *refs):
    if starts:
        amplitudes, refs, piece_sems = refs[0], refs[1:-1], refs[-1]
    folded, again, *pieces, panel, sizes, bounds, sems = refs
    quarter, virtuals = panel.shape
    fold = folded.shape[1]
    small = pltpu.make_async_copy(sizes_in, sizes, sems.at[quarter // chunk])
    small.start()
    copies = []
    for k in range(quarter // chunk):
        rows = pl.ds(k * chunk, chunk)
        copies.append(pltpu.make_async_copy(source.at[rows], panel.at[rows], sems.at[k]))
        copies[-1].start()
    piece_copies = []
    for k, (first, piece) in enumerate(zip(starts, pieces)):
        piece_copies += copies_of(amplitudes, first, piece, piece_sems.at[pl.ds(2 * k, 2)])
    small.wait()
    fill_bounds(sizes, bounds)
    start = lax.axis_index("grp") * quarter
    step = 32 if chunk % 32 == 0 else SUBLANES
    for k, copy in enumerate(copies):
        copy.wait()

        @pl.loop(0, chunk // step, unroll=True)
        def _(i):
            first = pl.multiple_of(k * chunk + i * step, SUBLANES)
            here = pl.ds(first, step)
            b = start + first + lax.broadcasted_iota(jnp.int32, (step, LANES), 0)
            low, high = wanted_range(b, pair, bounds, sizes.shape[0])
            lane = lax.broadcasted_iota(jnp.int32, (step, LANES), 1)
            low, high = low - lane, high - lane
            for place in range(0, fold, LANES):
                total = jnp.zeros((step, LANES), jnp.float32)
                for c in range(place, virtuals, fold):
                    value = panel[here, c:c + LANES].astype(jnp.float32)
                    total = jnp.where((low <= c) & (high > c), value, total)
                total = total.astype(folded.dtype)
                folded[here, place:place + LANES] = total
                again[here, place:place + LANES] = total

    for copy in piece_copies:
        copy.wait()


def fold_panel(panel, sizes, pair, fold, amplitudes, starts):
    quarter, virtuals = panel.shape
    chunk = quarter // 5 if quarter % (5 * SUBLANES) == 0 else quarter
    vmem = pl.BlockSpec(memory_space=pltpu.VMEM)
    anywhere = pl.BlockSpec(memory_space=pl.ANY)
    out_shape = [pltpu.VMEM((quarter, fold), panel.dtype)] * 2
    scratch = [
        pltpu.VMEM((quarter, virtuals), panel.dtype),
        pltpu.SMEM(sizes.shape, jnp.int32),
        pltpu.SMEM((sizes.shape[0] + 1,), jnp.int32),
        pltpu.SemaphoreType.DMA((quarter // chunk + 1,)),
    ]
    extra = []
    if starts:
        for first, end in zip(starts, (*starts[1:], amplitudes.shape[0])):
            out_shape.append(pltpu.VMEM((end - first, virtuals), amplitudes.dtype))
        scratch.append(pltpu.SemaphoreType.DMA((2 * len(starts),)))
        extra.append(amplitudes)
    return pl.pallas_call(
        functools.partial(fold_kernel, chunk, starts),
        out_shape=out_shape,
        in_specs=[pl.BlockSpec(memory_space=pltpu.SMEM)] + [anywhere] * (2 + len(extra)),
        out_specs=[vmem] * len(out_shape),
        scratch_shapes=scratch,
        compiler_params=pltpu.CompilerParams(vmem_limit_bytes=8 * MIB),
        cost_estimate=NOTHING,
        name="fold_panel",
    )(pair, sizes, pltpu.with_memory_space_constraint(panel, pltpu.HBM), *extra)


def place_panel(slot, parts, ranges, dense, turned):
    quarter, fold = sum(part.shape[0] for part in parts), parts[0].shape[1]
    virtuals = dense.shape[0]
    width = turned.shape[1]
    columns = slice(slot * width, (slot + 1) * width)
    step = 32
    values = [part[...].astype(jnp.float32) for part in parts]
    if width > quarter:
        values.append(jnp.zeros((width - quarter, fold), jnp.float32))
    turned[...] = jnp.concatenate(values).T
    low = jnp.concatenate([ranges[0, :, columns]] * (step // 8))
    high = jnp.concatenate([ranges[1, :, columns]] * (step // 8))

    @pl.loop(0, virtuals // step, unroll=4)
    def _(i):
        row = pl.multiple_of(i * step, step)
        source = pl.multiple_of(lax.rem(row, fold), step)
        c = row + lax.broadcasted_iota(jnp.int32, (step, width), 0)
        kept = jnp.where((c >= low) & (c < high), turned[pl.ds(source, step), :], 0.0)
        dense[pl.ds(row, step), columns] = kept.astype(dense.dtype)


def first_spread_kernel(
    groups, sizes, pair, folded, fock, dense, fock_out, ranges, token, bounds, turned, sems
):
    quarter = folded.shape[0]
    virtuals = dense.shape[0]
    width = turned.shape[1]
    group = lax.axis_index("grp")
    copies = []
    for k in range(groups):
        start = pl.multiple_of(jnp.bitwise_xor(group, k) * quarter, SUBLANES)
        copies.append(pltpu.make_async_copy(
            fock.at[pl.ds(start, quarter)], fock_out.at[pl.ds(k * width, quarter)], sems.at[k]
        ))
        copies[-1].start()
        if width > quarter:
            fock_out[k * width + quarter:(k + 1) * width, :] = jnp.zeros(
                (width - quarter, virtuals), fock_out.dtype
            )
    token[...] = jnp.zeros_like(token)
    fill_bounds(sizes, bounds)
    for k in range(groups):
        start = jnp.bitwise_xor(group, k) * quarter
        b = start + lax.broadcasted_iota(jnp.int32, (8, width), 1)
        low, high = wanted_range(b, pair, bounds, sizes.shape[0])
        ranges[0, :, k * width:(k + 1) * width] = low
        ranges[1, :, k * width:(k + 1) * width] = high
    place_panel(0, [folded], ranges, dense, turned)
    for copy in copies:
        copy.wait()


def first_spread(groups, folded, fock, sizes, pair):
    quarter, fold = folded.shape
    virtuals = fock.shape[0]
    width = rounded(quarter, LANES)
    smem = pl.BlockSpec(memory_space=pltpu.SMEM)
    vmem = pl.BlockSpec(memory_space=pltpu.VMEM)
    return pl.pallas_call(
        functools.partial(first_spread_kernel, groups),
        out_shape=[
            pltpu.VMEM((virtuals, groups * width), folded.dtype),
            pltpu.VMEM((groups * width, virtuals), fock.dtype),
            pltpu.VMEM((2, 8, groups * width), jnp.int32),
            TOKEN,
        ],
        in_specs=[smem, smem, vmem, pl.BlockSpec(memory_space=pl.ANY)],
        out_specs=[vmem] * 4,
        scratch_shapes=[
            pltpu.SMEM((sizes.shape[0] + 1,), jnp.int32),
            pltpu.VMEM((fold, width), jnp.float32),
            pltpu.SemaphoreType.DMA((groups,)),
        ],
        compiler_params=pltpu.CompilerParams(vmem_limit_bytes=8 * MIB),
        cost_estimate=NOTHING,
        name="first_spread",
    )(sizes, pair, folded, pltpu.with_memory_space_constraint(fock, pltpu.HBM))


def spread_kernel(slot, count, *refs):
    parts, (ranges, _, dense, turned) = refs[:count], refs[count:]
    place_panel(slot, parts, ranges, dense, turned)


def spread(slot, parts, ranges, dense):
    fold = parts[0].shape[1]
    width = rounded(sum(part.shape[0] for part in parts), LANES)
    vmem = pl.BlockSpec(memory_space=pltpu.VMEM)
    pinned = [pltpu.with_memory_space_constraint(x, pltpu.VMEM) for x in (ranges, dense)]
    return pl.pallas_call(
        functools.partial(spread_kernel, slot, len(parts)),
        out_shape=pltpu.VMEM(dense.shape, dense.dtype),
        in_specs=[vmem] * (len(parts) + 1) + [pl.BlockSpec(memory_space=pl.ANY)],
        out_specs=vmem,
        input_output_aliases={len(parts) + 1: 0},
        scratch_shapes=[pltpu.VMEM((fold, width), jnp.float32)],
        compiler_params=pltpu.CompilerParams(vmem_limit_bytes=8 * MIB),
        cost_estimate=NOTHING,
        name="spread_panel",
    )(*parts, *pinned)


def after(array, *others):
    anywhere = pl.BlockSpec(memory_space=pl.ANY)
    return pl.pallas_call(
        lambda *refs: None,
        out_shape=jax.ShapeDtypeStruct(array.shape, array.dtype),
        in_specs=[anywhere] * (1 + len(others)),
        out_specs=anywhere,
        input_output_aliases={0: 0},
        compiler_params=pltpu.CompilerParams(vmem_limit_bytes=MIB),
        cost_estimate=NOTHING,
        name="after",
    )(array, *others)


def owned_kernel(members, received, kept, *refs):
    out, sem = refs[-2:]

    @pl.when(lax.div(lax.axis_index("blk"), members) == lax.axis_index("grp"))
    def _():
        copy = pltpu.make_async_copy(kept, out, sem)
        copy.start()
        copy.wait()


def owned(received, kept, members, *others):
    anywhere = pl.BlockSpec(memory_space=pl.ANY)
    return pl.pallas_call(
        functools.partial(owned_kernel, members),
        out_shape=jax.ShapeDtypeStruct(received.shape, received.dtype),
        in_specs=[anywhere] * (2 + len(others)),
        out_specs=anywhere,
        input_output_aliases={0: 0},
        scratch_shapes=[pltpu.SemaphoreType.DMA],
        compiler_params=pltpu.CompilerParams(vmem_limit_bytes=MIB),
        cost_estimate=NOTHING,
        name="owned_rows",
    )(received, kept, *others)


def column_tiles(total, tile):
    return [(first, min(tile, total - first)) for first in range(0, total, tile)]


def dress_kernel(job, amplitudes, dense, fock, *refs):
    columns, spans, rows, members, has_sums, has_base, signed = job
    if has_sums:
        sums, refs = refs[0], refs[1:]
    refs = refs[has_base:]
    result, refs = refs[0], refs[1:]
    if signed:
        refs[0][...] = jnp.zeros_like(refs[0])
        refs = refs[1:]
    virtuals = dense.shape[0]
    begin, end = columns
    coupled = refs[0]
    for first, tile in column_tiles(end - begin, 512):
        coupled[:, first:first + tile] = jnp.dot(
            amplitudes[...], dense[:, begin + first:begin + first + tile],
            preferred_element_type=jnp.float32,
        ).astype(coupled.dtype)
    if spans:
        dressed, sems = refs[1:]
        block = lax.axis_index("blk")
        places = [
            pl.multiple_of(lax.rem(block + by, members) * rows + offset, SUBLANES)
            for by, offset, _ in spans
        ]
    copies = []
    for t, (first, tile) in enumerate(column_tiles(virtuals, 512)):
        here = slice(first, first + tile)
        total = jnp.dot(
            coupled[...], fock[begin:end, here], preferred_element_type=jnp.float32
        )
        if has_sums:
            total = total + sums[:, here]
        if not spans:
            result[:, here] = total
            continue
        dressed[:, here] = total.astype(dressed.dtype)
        top = 0
        for p, (_, _, size) in enumerate(spans):
            copies.append(pltpu.make_async_copy(
                dressed.at[pl.ds(top, size), pl.ds(first, tile)],
                result.at[pl.ds(places[p], size), pl.ds(first, tile)],
                sems.at[p, t],
            ))
            copies[-1].start()
            top += size
    for copy in copies:
        copy.wait()


def dress(amplitudes, dense, fock, *, columns=None, sums=None, spans=(), base=None, rows=0, members=1,
          out_rows=0, signed=False):
    height, virtuals = amplitudes.shape
    begin, end = columns or (0, dense.shape[1])
    vmem = pl.BlockSpec(memory_space=pltpu.VMEM)
    anywhere = pl.BlockSpec(memory_space=pl.ANY)
    pinned = [dense, fock] + ([] if sums is None else [sums])
    pinned = [pltpu.with_memory_space_constraint(x, pltpu.VMEM) for x in pinned]
    bases = [] if base is None else [base]
    scratch = [pltpu.VMEM((height, end - begin), amplitudes.dtype)]
    if spans:
        out_shape = [jax.ShapeDtypeStruct((out_rows, virtuals), amplitudes.dtype)]
        scratch += [
            pltpu.VMEM((height, virtuals), amplitudes.dtype),
            pltpu.SemaphoreType.DMA((len(spans), len(column_tiles(virtuals, 512)))),
        ]
    else:
        out_shape = [pltpu.VMEM((height, virtuals), jnp.float32)]
    job = ((begin, end), spans, rows, members, sums is not None, base is not None, signed)
    return pl.pallas_call(
        functools.partial(dress_kernel, job),
        out_shape=out_shape + [TOKEN] * signed,
        in_specs=[vmem] * (1 + len(pinned)) + [anywhere] * len(bases),
        out_specs=[anywhere if spans else vmem] + [vmem] * signed,
        input_output_aliases={} if base is None else {1 + len(pinned): 0},
        scratch_shapes=scratch,
        compiler_params=pltpu.CompilerParams(vmem_limit_bytes=16 * MIB),
        cost_estimate=NOTHING,
        name="dress_rows",
    )(amplitudes, *pinned, *bases)


def make_local(blocks, groups):
    members = blocks // groups
    axes = ("blk", "grp")

    def device(hi, lo, grp):
        return (hi * members + lo) * groups + grp

    everyone = [(h, l, g) for h in range(groups) for l in range(members) for g in range(groups)]

    if groups == 4:
        copies = ((None, 0, 3, 1), (0, None, 1, 3), (0, 2, None, 3), (2, 0, 3, None))
    else:
        copies = [[None if h == g else h for h in range(groups)] for g in range(groups)]
    to_group = [
        (device(g, l, copies[g][h]), device(h, l, g)) for h, l, g in everyone if h != g
    ]

    def to_member(by):
        return [(device(h, (l + by) % members, g), device(h, l, g)) for h, l, g in everyone]

    def to_slot(slot):
        return [(device(h, l, g ^ slot), device(h, l, g)) for h, l, g in everyone]

    def local(amplitudes, hole_panel, virt_fock, irrep_sizes, pair_irreps):
        rows, virtuals = amplitudes.shape
        out_rows = rows * members
        fold = rounded(virtuals // 4, LANES)
        panel = jnp.swapaxes(hole_panel[:, 0, :], 0, 1)
        irrep_sizes = pltpu.with_memory_space_constraint(irrep_sizes, pltpu.HBM)

        piece = rounded(rows * 7 // 15, SUBLANES) if rows % SUBLANES == 0 else 0
        early = rounded(rows * 4 // 5, SUBLANES)
        if piece:
            amplitudes = pltpu.with_memory_space_constraint(amplitudes, pltpu.HBM)
            first = cut(amplitudes, piece)
            starts = (piece, early)
        else:
            first, starts = amplitudes, ()
        own, own_again, *pieces = fold_panel(
            panel, irrep_sizes, pair_irreps, fold, amplitudes, starts
        )
        across = lax.ppermute(own, axes, to_slot(2))
        beside = lax.ppermute(own_again, axes, to_slot(1))
        if piece:
            second, late = pieces
            lates = [late] + [lax.ppermute(late, axes, to_member(by)) for by in range(1, members)]

        dense, fock, ranges, token = first_spread(groups, own, virt_fock, irrep_sizes, pair_irreps)
        first = owned(lax.ppermute(first, axes, to_group), first, members, token)
        firsts = [lax.ppermute(first, axes, to_member(by)) for by in range(1, members)]
        if piece:
            second = owned(lax.ppermute(second, axes, to_group), second, members, first)
            seconds = [lax.ppermute(second, axes, to_member(by)) for by in range(1, members)]
            lates = jnp.concatenate([after(rows_of, second) for rows_of in lates])
            sent = lax.ppermute(lates, axes, to_group)
        dense = spread(1, [beside], ranges, dense)
        near = 2 * dense.shape[1] // groups
        if piece:
            mine = jnp.concatenate([first, second])
            sums, token = dress(mine, dense, fock, columns=(0, near), signed=True)
            across = after(across, token)
        cuts = [rounded(across.shape[0] // 2, SUBLANES)] if piece else []
        both = [lax.ppermute(part, axes, to_slot(1)) for part in jnp.split(across, cuts)]
        dense = spread(2, [across], ranges, dense)
        dense = spread(3, both, ranges, dense)

        if piece:
            place = dict(rows=rows, members=members, out_rows=out_rows)
            result, token = dress(
                mine, dense, fock, columns=(near, dense.shape[1]), sums=sums,
                spans=((0, 0, early),), signed=True, **place,
            )
            last = []
            for parts in zip(firsts, seconds):
                last += [after(part, token) for part in parts]
            last.append(owned(sent, lates, members, token))
            spans = [(by, 0, early) for by in range(1, members)]
            spans += [(by, early, rows - early) for by in range(members)]
            result, = dress(
                jnp.concatenate(last), dense, fock, spans=tuple(spans), base=result, **place
            )
        else:
            member = lax.axis_index("blk") % members
            ordered = jnp.roll(jnp.stack([first, *firsts]), member, axis=0).reshape(out_rows, virtuals)
            result, = dress(ordered, dense, fock, spans=((0, 0, out_rows),), out_rows=out_rows)
        return result[:, None, :]

    return local


def solution(mesh):
    in_specs = (P("blk", None), P(None, "blk", "grp"), P(), P(), P("blk"))
    out_specs = P("grp", "blk", None)
    local = make_local(mesh.shape["blk"], mesh.shape["grp"])
    return jax.shard_map(local, mesh=mesh, in_specs=in_specs, out_specs=out_specs, check_vma=False)
```

```python
import functools

import jax
import jax.numpy as jnp
from jax import lax
from jax.experimental import pallas as pl
from jax.experimental.pallas import tpu as pltpu
from jax.sharding import PartitionSpec as P

LANES = 128
SUBLANES = 16
MIB = 1 << 20
TOKEN = pltpu.VMEM((8, LANES), jnp.int32)
NOTHING = pl.CostEstimate(flops=0, bytes_accessed=0, transcendentals=0)


def rounded(value, unit):
    return -(-value // unit) * unit


def fill_bounds(sizes, bounds):
    total = jnp.int32(0)
    for r in range(sizes.shape[0]):
        bounds[r] = total
        total = total + sizes[r]
    bounds[sizes.shape[0]] = total


def wanted_range(b, pair, bounds, irreps):
    low, high = jnp.zeros_like(b), jnp.zeros_like(b)
    for r in range(irreps):
        partner = jnp.bitwise_xor(pair[0], r)
        inside = (b >= bounds[r]) & (b < bounds[r + 1])
        low = jnp.where(inside, bounds[partner], low)
        high = jnp.where(inside, bounds[partner + 1], high)
    return low, high


def copies_of(source, first, target, sems):
    count = sems.shape[0]
    step = rounded(-(-target.shape[0] // count), SUBLANES)
    copies = []
    for k, begin in enumerate(range(0, target.shape[0], step)):
        size = min(step, target.shape[0] - begin)
        copies.append(pltpu.make_async_copy(
            source.at[pl.ds(first + begin, size)], target.at[pl.ds(begin, size)], sems.at[k]
        ))
        copies[-1].start()
    return copies


def cut_kernel(whole, piece, sems):
    for copy in copies_of(whole, 0, piece, sems):
        copy.wait()


def cut(whole, size):
    return pl.pallas_call(
        cut_kernel,
        out_shape=pltpu.VMEM((size, whole.shape[1]), whole.dtype),
        in_specs=[pl.BlockSpec(memory_space=pl.ANY)],
        out_specs=pl.BlockSpec(memory_space=pltpu.VMEM),
        scratch_shapes=[pltpu.SemaphoreType.DMA((5,))],
        compiler_params=pltpu.CompilerParams(vmem_limit_bytes=4 * MIB),
        cost_estimate=NOTHING,
        name="cut_rows",
    )(whole)


def fold_kernel(chunk, starts, pair, sizes_in, source, *refs):
    if starts:
        amplitudes, refs, piece_sems = refs[0], refs[1:-1], refs[-1]
    folded, again, *pieces, panel, sizes, bounds, sems = refs
    quarter, virtuals = panel.shape
    fold = folded.shape[1]
    small = pltpu.make_async_copy(sizes_in, sizes, sems.at[quarter // chunk])
    small.start()
    copies = []
    for k in range(quarter // chunk):
        rows = pl.ds(k * chunk, chunk)
        copies.append(pltpu.make_async_copy(source.at[rows], panel.at[rows], sems.at[k]))
        copies[-1].start()
    piece_copies = []
    for k, (first, piece) in enumerate(zip(starts, pieces)):
        piece_copies += copies_of(amplitudes, first, piece, piece_sems.at[pl.ds(2 * k, 2)])
    small.wait()
    fill_bounds(sizes, bounds)
    start = lax.axis_index("grp") * quarter
    step = 32 if chunk % 32 == 0 else SUBLANES
    for k, copy in enumerate(copies):
        copy.wait()

        @pl.loop(0, chunk // step, unroll=True)
        def _(i):
            first = pl.multiple_of(k * chunk + i * step, SUBLANES)
            here = pl.ds(first, step)
            b = start + first + lax.broadcasted_iota(jnp.int32, (step, LANES), 0)
            low, high = wanted_range(b, pair, bounds, sizes.shape[0])
            lane = lax.broadcasted_iota(jnp.int32, (step, LANES), 1)
            low, high = low - lane, high - lane
            for place in range(0, fold, LANES):
                total = jnp.zeros((step, LANES), jnp.float32)
                for c in range(place, virtuals, fold):
                    value = panel[here, c:c + LANES].astype(jnp.float32)
                    total = jnp.where((low <= c) & (high > c), value, total)
                total = total.astype(folded.dtype)
                folded[here, place:place + LANES] = total
                again[here, place:place + LANES] = total

    for copy in piece_copies:
        copy.wait()


def fold_panel(panel, sizes, pair, fold, amplitudes, starts):
    quarter, virtuals = panel.shape
    chunk = quarter // 5 if quarter % (5 * SUBLANES) == 0 else quarter
    vmem = pl.BlockSpec(memory_space=pltpu.VMEM)
    anywhere = pl.BlockSpec(memory_space=pl.ANY)
    out_shape = [pltpu.VMEM((quarter, fold), panel.dtype)] * 2
    scratch = [
        pltpu.VMEM((quarter, virtuals), panel.dtype),
        pltpu.SMEM(sizes.shape, jnp.int32),
        pltpu.SMEM((sizes.shape[0] + 1,), jnp.int32),
        pltpu.SemaphoreType.DMA((quarter // chunk + 1,)),
    ]
    extra = []
    if starts:
        for first, end in zip(starts, (*starts[1:], amplitudes.shape[0])):
            out_shape.append(pltpu.VMEM((end - first, virtuals), amplitudes.dtype))
        scratch.append(pltpu.SemaphoreType.DMA((2 * len(starts),)))
        extra.append(amplitudes)
    return pl.pallas_call(
        functools.partial(fold_kernel, chunk, starts),
        out_shape=out_shape,
        in_specs=[pl.BlockSpec(memory_space=pltpu.SMEM)] + [anywhere] * (2 + len(extra)),
        out_specs=[vmem] * len(out_shape),
        scratch_shapes=scratch,
        compiler_params=pltpu.CompilerParams(vmem_limit_bytes=8 * MIB),
        cost_estimate=NOTHING,
        name="fold_panel",
    )(pair, sizes, pltpu.with_memory_space_constraint(panel, pltpu.HBM), *extra)


def place_panel(slot, parts, ranges, dense, turned):
    quarter, fold = sum(part.shape[0] for part in parts), parts[0].shape[1]
    virtuals = dense.shape[0]
    width = turned.shape[1]
    columns = slice(slot * width, (slot + 1) * width)
    step = 32
    values = [part[...].astype(jnp.float32) for part in parts]
    if width > quarter:
        values.append(jnp.zeros((width - quarter, fold), jnp.float32))
    turned[...] = jnp.concatenate(values).T
    low = jnp.concatenate([ranges[0, :, columns]] * (step // 8))
    high = jnp.concatenate([ranges[1, :, columns]] * (step // 8))

    @pl.loop(0, virtuals // step, unroll=4)
    def _(i):
        row = pl.multiple_of(i * step, step)
        source = pl.multiple_of(lax.rem(row, fold), step)
        c = row + lax.broadcasted_iota(jnp.int32, (step, width), 0)
        kept = jnp.where((c >= low) & (c < high), turned[pl.ds(source, step), :], 0.0)
        dense[pl.ds(row, step), columns] = kept.astype(dense.dtype)


def first_spread_kernel(
    groups, sizes, pair, folded, fock, dense, fock_out, ranges, token, bounds, turned, sems
):
    quarter = folded.shape[0]
    virtuals = dense.shape[0]
    width = turned.shape[1]
    group = lax.axis_index("grp")
    copies = []
    for k in range(groups):
        start = pl.multiple_of(jnp.bitwise_xor(group, k) * quarter, SUBLANES)
        copies.append(pltpu.make_async_copy(
            fock.at[pl.ds(start, quarter)], fock_out.at[pl.ds(k * width, quarter)], sems.at[k]
        ))
        copies[-1].start()
        if width > quarter:
            fock_out[k * width + quarter:(k + 1) * width, :] = jnp.zeros(
                (width - quarter, virtuals), fock_out.dtype
            )
    token[...] = jnp.zeros_like(token)
    fill_bounds(sizes, bounds)
    for k in range(groups):
        start = jnp.bitwise_xor(group, k) * quarter
        b = start + lax.broadcasted_iota(jnp.int32, (8, width), 1)
        low, high = wanted_range(b, pair, bounds, sizes.shape[0])
        ranges[0, :, k * width:(k + 1) * width] = low
        ranges[1, :, k * width:(k + 1) * width] = high
    place_panel(0, [folded], ranges, dense, turned)
    for copy in copies:
        copy.wait()


def first_spread(groups, folded, fock, sizes, pair):
    quarter, fold = folded.shape
    virtuals = fock.shape[0]
    width = rounded(quarter, LANES)
    smem = pl.BlockSpec(memory_space=pltpu.SMEM)
    vmem = pl.BlockSpec(memory_space=pltpu.VMEM)
    return pl.pallas_call(
        functools.partial(first_spread_kernel, groups),
        out_shape=[
            pltpu.VMEM((virtuals, groups * width), folded.dtype),
            pltpu.VMEM((groups * width, virtuals), fock.dtype),
            pltpu.VMEM((2, 8, groups * width), jnp.int32),
            TOKEN,
        ],
        in_specs=[smem, smem, vmem, pl.BlockSpec(memory_space=pl.ANY)],
        out_specs=[vmem] * 4,
        scratch_shapes=[
            pltpu.SMEM((sizes.shape[0] + 1,), jnp.int32),
            pltpu.VMEM((fold, width), jnp.float32),
            pltpu.SemaphoreType.DMA((groups,)),
        ],
        compiler_params=pltpu.CompilerParams(vmem_limit_bytes=8 * MIB),
        cost_estimate=NOTHING,
        name="first_spread",
    )(sizes, pair, folded, pltpu.with_memory_space_constraint(fock, pltpu.HBM))


def spread_kernel(slot, count, *refs):
    parts, (ranges, _, dense, turned) = refs[:count], refs[count:]
    place_panel(slot, parts, ranges, dense, turned)


def spread(slot, parts, ranges, dense):
    fold = parts[0].shape[1]
    width = rounded(sum(part.shape[0] for part in parts), LANES)
    vmem = pl.BlockSpec(memory_space=pltpu.VMEM)
    pinned = [pltpu.with_memory_space_constraint(x, pltpu.VMEM) for x in (ranges, dense)]
    return pl.pallas_call(
        functools.partial(spread_kernel, slot, len(parts)),
        out_shape=pltpu.VMEM(dense.shape, dense.dtype),
        in_specs=[vmem] * (len(parts) + 1) + [pl.BlockSpec(memory_space=pl.ANY)],
        out_specs=vmem,
        input_output_aliases={len(parts) + 1: 0},
        scratch_shapes=[pltpu.VMEM((fold, width), jnp.float32)],
        compiler_params=pltpu.CompilerParams(vmem_limit_bytes=8 * MIB),
        cost_estimate=NOTHING,
        name="spread_panel",
    )(*parts, *pinned)


def after(array, *others):
    anywhere = pl.BlockSpec(memory_space=pl.ANY)
    return pl.pallas_call(
        lambda *refs: None,
        out_shape=jax.ShapeDtypeStruct(array.shape, array.dtype),
        in_specs=[anywhere] * (1 + len(others)),
        out_specs=anywhere,
        input_output_aliases={0: 0},
        compiler_params=pltpu.CompilerParams(vmem_limit_bytes=MIB),
        cost_estimate=NOTHING,
        name="after",
    )(array, *others)


def owned_kernel(members, received, kept, *refs):
    out, sem = refs[-2:]

    @pl.when(lax.div(lax.axis_index("blk"), members) == lax.axis_index("grp"))
    def _():
        copy = pltpu.make_async_copy(kept, out, sem)
        copy.start()
        copy.wait()


def owned(received, kept, members, *others):
    anywhere = pl.BlockSpec(memory_space=pl.ANY)
    return pl.pallas_call(
        functools.partial(owned_kernel, members),
        out_shape=jax.ShapeDtypeStruct(received.shape, received.dtype),
        in_specs=[anywhere] * (2 + len(others)),
        out_specs=anywhere,
        input_output_aliases={0: 0},
        scratch_shapes=[pltpu.SemaphoreType.DMA],
        compiler_params=pltpu.CompilerParams(vmem_limit_bytes=MIB),
        cost_estimate=NOTHING,
        name="owned_rows",
    )(received, kept, *others)


def column_tiles(total, tile):
    return [(first, min(tile, total - first)) for first in range(0, total, tile)]


def dress_kernel(job, amplitudes, dense, fock, *refs):
    columns, spans, rows, members, has_sums, has_base, signed = job
    if has_sums:
        sums, refs = refs[0], refs[1:]
    refs = refs[has_base:]
    result, refs = refs[0], refs[1:]
    if signed:
        refs[0][...] = jnp.zeros_like(refs[0])
        refs = refs[1:]
    virtuals = dense.shape[0]
    begin, end = columns
    coupled = refs[0]
    for first, tile in column_tiles(end - begin, 512):
        coupled[:, first:first + tile] = jnp.dot(
            amplitudes[...], dense[:, begin + first:begin + first + tile],
            preferred_element_type=jnp.float32,
        ).astype(coupled.dtype)
    if spans:
        dressed, sems = refs[1:]
        block = lax.axis_index("blk")
        places = [
            pl.multiple_of(lax.rem(block + by, members) * rows + offset, SUBLANES)
            for by, offset, _ in spans
        ]
    copies = []
    for t, (first, tile) in enumerate(column_tiles(virtuals, 512)):
        here = slice(first, first + tile)
        total = jnp.dot(
            coupled[...], fock[begin:end, here], preferred_element_type=jnp.float32
        )
        if has_sums:
            total = total + sums[:, here]
        if not spans:
            result[:, here] = total
            continue
        dressed[:, here] = total.astype(dressed.dtype)
        top = 0
        for p, (_, _, size) in enumerate(spans):
            copies.append(pltpu.make_async_copy(
                dressed.at[pl.ds(top, size), pl.ds(first, tile)],
                result.at[pl.ds(places[p], size), pl.ds(first, tile)],
                sems.at[p, t],
            ))
            copies[-1].start()
            top += size
    for copy in copies:
        copy.wait()


def dress(amplitudes, dense, fock, *, columns=None, sums=None, spans=(), base=None, rows=0, members=1,
          out_rows=0, signed=False):
    height, virtuals = amplitudes.shape
    begin, end = columns or (0, dense.shape[1])
    vmem = pl.BlockSpec(memory_space=pltpu.VMEM)
    anywhere = pl.BlockSpec(memory_space=pl.ANY)
    pinned = [dense, fock] + ([] if sums is None else [sums])
    pinned = [pltpu.with_memory_space_constraint(x, pltpu.VMEM) for x in pinned]
    bases = [] if base is None else [base]
    scratch = [pltpu.VMEM((height, end - begin), amplitudes.dtype)]
    if spans:
        out_shape = [jax.ShapeDtypeStruct((out_rows, virtuals), amplitudes.dtype)]
        scratch += [
            pltpu.VMEM((height, virtuals), amplitudes.dtype),
            pltpu.SemaphoreType.DMA((len(spans), len(column_tiles(virtuals, 512)))),
        ]
    else:
        out_shape = [pltpu.VMEM((height, virtuals), jnp.float32)]
    job = ((begin, end), spans, rows, members, sums is not None, base is not None, signed)
    return pl.pallas_call(
        functools.partial(dress_kernel, job),
        out_shape=out_shape + [TOKEN] * signed,
        in_specs=[vmem] * (1 + len(pinned)) + [anywhere] * len(bases),
        out_specs=[anywhere if spans else vmem] + [vmem] * signed,
        input_output_aliases={} if base is None else {1 + len(pinned): 0},
        scratch_shapes=scratch,
        compiler_params=pltpu.CompilerParams(vmem_limit_bytes=16 * MIB),
        cost_estimate=NOTHING,
        name="dress_rows",
    )(amplitudes, *pinned, *bases)


def make_local(blocks, groups):
    members = blocks // groups
    axes = ("blk", "grp")

    def device(hi, lo, grp):
        return (hi * members + lo) * groups + grp

    everyone = [(h, l, g) for h in range(groups) for l in range(members) for g in range(groups)]

    if groups == 4:
        copies = ((None, 0, 3, 1), (0, None, 1, 3), (0, 2, None, 3), (2, 0, 3, None))
    else:
        copies = [[None if h == g else h for h in range(groups)] for g in range(groups)]
    to_group = [
        (device(g, l, copies[g][h]), device(h, l, g)) for h, l, g in everyone if h != g
    ]

    def to_member(by):
        return [(device(h, (l + by) % members, g), device(h, l, g)) for h, l, g in everyone]

    def to_slot(slot):
        return [(device(h, l, g ^ slot), device(h, l, g)) for h, l, g in everyone]

    def local(amplitudes, hole_panel, virt_fock, irrep_sizes, pair_irreps):
        rows, virtuals = amplitudes.shape
        out_rows = rows * members
        fold = rounded(virtuals // 4, LANES)
        panel = jnp.swapaxes(hole_panel[:, 0, :], 0, 1)
        irrep_sizes = pltpu.with_memory_space_constraint(irrep_sizes, pltpu.HBM)

        piece = rounded(rows * 2 // 5, SUBLANES) if rows % SUBLANES == 0 else 0
        early = rounded(rows * 7 // 10, SUBLANES)
        if piece:
            amplitudes = pltpu.with_memory_space_constraint(amplitudes, pltpu.HBM)
            first = cut(amplitudes, piece)
            starts = (piece, early)
        else:
            first, starts = amplitudes, ()
        own, own_again, *pieces = fold_panel(
            panel, irrep_sizes, pair_irreps, fold, amplitudes, starts
        )
        across = lax.ppermute(own, axes, to_slot(2))
        beside = lax.ppermute(own_again, axes, to_slot(1))
        if piece:
            second, late = pieces
            lates = [late] + [lax.ppermute(late, axes, to_member(by)) for by in range(1, members)]

        dense, fock, ranges, token = first_spread(groups, own, virt_fock, irrep_sizes, pair_irreps)
        first = owned(lax.ppermute(first, axes, to_group), first, members, token)
        firsts = [lax.ppermute(first, axes, to_member(by)) for by in range(1, members)]
        if piece:
            lates = jnp.concatenate([after(rows_of, first) for rows_of in lates])
            sent = lax.ppermute(lates, axes, to_group)
        dense = spread(1, [beside], ranges, dense)
        near = 2 * dense.shape[1] // groups
        if piece:
            sums, token = dress(first, dense, fock, columns=(0, near), signed=True)
            across = after(across, token)
        cuts = [rounded(across.shape[0] // 2, SUBLANES)] if piece else []
        both = [lax.ppermute(part, axes, to_slot(1)) for part in jnp.split(across, cuts)]
        if piece:
            second = owned(lax.ppermute(second, axes, to_group), second, members, across)
            seconds = [lax.ppermute(second, axes, to_member(by)) for by in range(1, members)]
        dense = spread(2, [across], ranges, dense)
        dense = spread(3, both, ranges, dense)

        if piece:
            place = dict(rows=rows, members=members, out_rows=out_rows)
            result, token = dress(
                first, dense, fock, columns=(near, dense.shape[1]), sums=sums,
                spans=((0, 0, piece),), signed=True, **place,
            )
            parts = [second] + [after(part, token) for part in firsts]
            spans = [(0, piece, early - piece)] + [(by, 0, piece) for by in range(1, members)]
            result, token = dress(
                jnp.concatenate(parts), dense, fock, spans=tuple(spans), base=result, signed=True, **place
            )
            last = [after(part, token) for part in seconds] + [owned(sent, lates, members, token)]
            spans = [(by, piece, early - piece) for by in range(1, members)]
            spans += [(by, early, rows - early) for by in range(members)]
            result, = dress(
                jnp.concatenate(last), dense, fock, spans=tuple(spans), base=result, **place
            )
        else:
            member = lax.axis_index("blk") % members
            ordered = jnp.roll(jnp.stack([first, *firsts]), member, axis=0).reshape(out_rows, virtuals)
            result, = dress(ordered, dense, fock, spans=((0, 0, out_rows),), out_rows=out_rows)
        return result[:, None, :]

    return local


def solution(mesh):
    in_specs = (P("blk", None), P(None, "blk", "grp"), P(), P(), P("blk"))
    out_specs = P("grp", "blk", None)
    local = make_local(mesh.shape["blk"], mesh.shape["grp"])
    return jax.shard_map(local, mesh=mesh, in_specs=in_specs, out_specs=out_specs, check_vma=False)
```

```python
import functools

import jax
import jax.numpy as jnp
from jax import lax
from jax.experimental import pallas as pl
from jax.experimental.pallas import tpu as pltpu
from jax.sharding import PartitionSpec as P

LANES = 128
SUBLANES = 16
MIB = 1 << 20
TOKEN = pltpu.VMEM((8, LANES), jnp.int32)
NOTHING = pl.CostEstimate(flops=0, bytes_accessed=0, transcendentals=0)


def rounded(value, unit):
    return -(-value // unit) * unit


def fill_bounds(sizes, bounds):
    total = jnp.int32(0)
    for r in range(sizes.shape[0]):
        bounds[r] = total
        total = total + sizes[r]
    bounds[sizes.shape[0]] = total


def wanted_range(b, pair, bounds, irreps):
    low, high = jnp.zeros_like(b), jnp.zeros_like(b)
    for r in range(irreps):
        partner = jnp.bitwise_xor(pair[0], r)
        inside = (b >= bounds[r]) & (b < bounds[r + 1])
        low = jnp.where(inside, bounds[partner], low)
        high = jnp.where(inside, bounds[partner + 1], high)
    return low, high


def copies_of(source, first, target, sems):
    count = sems.shape[0]
    step = rounded(-(-target.shape[0] // count), SUBLANES)
    copies = []
    for k, begin in enumerate(range(0, target.shape[0], step)):
        size = min(step, target.shape[0] - begin)
        copies.append(pltpu.make_async_copy(
            source.at[pl.ds(first + begin, size)], target.at[pl.ds(begin, size)], sems.at[k]
        ))
        copies[-1].start()
    return copies


def cut_kernel(whole, piece, sems):
    for copy in copies_of(whole, 0, piece, sems):
        copy.wait()


def cut(whole, size):
    return pl.pallas_call(
        cut_kernel,
        out_shape=pltpu.VMEM((size, whole.shape[1]), whole.dtype),
        in_specs=[pl.BlockSpec(memory_space=pl.ANY)],
        out_specs=pl.BlockSpec(memory_space=pltpu.VMEM),
        scratch_shapes=[pltpu.SemaphoreType.DMA((5,))],
        compiler_params=pltpu.CompilerParams(vmem_limit_bytes=4 * MIB),
        cost_estimate=NOTHING,
        name="cut_rows",
    )(whole)


def fold_kernel(chunk, late, pair, sizes_in, source, *refs):
    if late:
        amplitudes, folded, again, low, panel, sizes, bounds, sems, low_sems = refs
    else:
        folded, again, panel, sizes, bounds, sems = refs
    quarter, virtuals = panel.shape
    fold = folded.shape[1]
    small = pltpu.make_async_copy(sizes_in, sizes, sems.at[quarter // chunk])
    small.start()
    copies = []
    for k in range(quarter // chunk):
        rows = pl.ds(k * chunk, chunk)
        copies.append(pltpu.make_async_copy(source.at[rows], panel.at[rows], sems.at[k]))
        copies[-1].start()
    lows = copies_of(amplitudes, late, low, low_sems) if late else []
    small.wait()
    fill_bounds(sizes, bounds)
    start = lax.axis_index("grp") * quarter
    step = 32 if chunk % 32 == 0 else SUBLANES
    for k, copy in enumerate(copies):
        copy.wait()

        @pl.loop(0, chunk // step, unroll=True)
        def _(i):
            first = pl.multiple_of(k * chunk + i * step, SUBLANES)
            here = pl.ds(first, step)
            b = start + first + lax.broadcasted_iota(jnp.int32, (step, LANES), 0)
            low, high = wanted_range(b, pair, bounds, sizes.shape[0])
            lane = lax.broadcasted_iota(jnp.int32, (step, LANES), 1)
            low, high = low - lane, high - lane
            for place in range(0, fold, LANES):
                total = jnp.zeros((step, LANES), jnp.float32)
                for c in range(place, virtuals, fold):
                    value = panel[here, c:c + LANES].astype(jnp.float32)
                    total = jnp.where((low <= c) & (high > c), value, total)
                total = total.astype(folded.dtype)
                folded[here, place:place + LANES] = total
                again[here, place:place + LANES] = total

    for copy in lows:
        copy.wait()


def fold_panel(panel, sizes, pair, fold, amplitudes, late):
    quarter, virtuals = panel.shape
    chunk = quarter // 5 if quarter % (5 * SUBLANES) == 0 else quarter
    vmem = pl.BlockSpec(memory_space=pltpu.VMEM)
    anywhere = pl.BlockSpec(memory_space=pl.ANY)
    out_shape = [pltpu.VMEM((quarter, fold), panel.dtype)] * 2
    scratch = [
        pltpu.VMEM((quarter, virtuals), panel.dtype),
        pltpu.SMEM(sizes.shape, jnp.int32),
        pltpu.SMEM((sizes.shape[0] + 1,), jnp.int32),
        pltpu.SemaphoreType.DMA((quarter // chunk + 1,)),
    ]
    extra = []
    if late:
        out_shape.append(pltpu.VMEM((amplitudes.shape[0] - late, virtuals), amplitudes.dtype))
        scratch.append(pltpu.SemaphoreType.DMA((2,)))
        extra.append(amplitudes)
    return pl.pallas_call(
        functools.partial(fold_kernel, chunk, late),
        out_shape=out_shape,
        in_specs=[pl.BlockSpec(memory_space=pltpu.SMEM)] + [anywhere] * (2 + len(extra)),
        out_specs=[vmem] * len(out_shape),
        scratch_shapes=scratch,
        compiler_params=pltpu.CompilerParams(vmem_limit_bytes=8 * MIB),
        cost_estimate=NOTHING,
        name="fold_panel",
    )(pair, sizes, pltpu.with_memory_space_constraint(panel, pltpu.HBM), *extra)


def place_panel(slot, folded, ranges, dense, turned):
    quarter, fold = folded.shape
    virtuals = dense.shape[0]
    width = turned.shape[1]
    columns = slice(slot * width, (slot + 1) * width)
    step = 32
    values = folded[...].astype(jnp.float32)
    if width > quarter:
        values = jnp.concatenate([values, jnp.zeros((width - quarter, fold), jnp.float32)])
    turned[...] = values.T
    low = jnp.concatenate([ranges[0, :, columns]] * (step // 8))
    high = jnp.concatenate([ranges[1, :, columns]] * (step // 8))

    @pl.loop(0, virtuals // step, unroll=4)
    def _(i):
        row = pl.multiple_of(i * step, step)
        source = pl.multiple_of(lax.rem(row, fold), step)
        c = row + lax.broadcasted_iota(jnp.int32, (step, width), 0)
        kept = jnp.where((c >= low) & (c < high), turned[pl.ds(source, step), :], 0.0)
        dense[pl.ds(row, step), columns] = kept.astype(dense.dtype)


def first_spread_kernel(
    groups, sizes, pair, folded, fock, dense, fock_out, ranges, token, bounds, turned, sems
):
    quarter = folded.shape[0]
    virtuals = dense.shape[0]
    width = turned.shape[1]
    group = lax.axis_index("grp")
    copies = []
    for k in range(groups):
        start = pl.multiple_of(jnp.bitwise_xor(group, k) * quarter, SUBLANES)
        copies.append(pltpu.make_async_copy(
            fock.at[pl.ds(start, quarter)], fock_out.at[pl.ds(k * width, quarter)], sems.at[k]
        ))
        copies[-1].start()
        if width > quarter:
            fock_out[k * width + quarter:(k + 1) * width, :] = jnp.zeros(
                (width - quarter, virtuals), fock_out.dtype
            )
    token[...] = jnp.zeros_like(token)
    fill_bounds(sizes, bounds)
    for k in range(groups):
        start = jnp.bitwise_xor(group, k) * quarter
        b = start + lax.broadcasted_iota(jnp.int32, (8, width), 1)
        low, high = wanted_range(b, pair, bounds, sizes.shape[0])
        ranges[0, :, k * width:(k + 1) * width] = low
        ranges[1, :, k * width:(k + 1) * width] = high
    place_panel(0, folded, ranges, dense, turned)
    for copy in copies:
        copy.wait()


def first_spread(groups, folded, fock, sizes, pair):
    quarter, fold = folded.shape
    virtuals = fock.shape[0]
    width = rounded(quarter, LANES)
    smem = pl.BlockSpec(memory_space=pltpu.SMEM)
    vmem = pl.BlockSpec(memory_space=pltpu.VMEM)
    return pl.pallas_call(
        functools.partial(first_spread_kernel, groups),
        out_shape=[
            pltpu.VMEM((virtuals, groups * width), folded.dtype),
            pltpu.VMEM((groups * width, virtuals), fock.dtype),
            pltpu.VMEM((2, 8, groups * width), jnp.int32),
            TOKEN,
        ],
        in_specs=[smem, smem, vmem, pl.BlockSpec(memory_space=pl.ANY)],
        out_specs=[vmem] * 4,
        scratch_shapes=[
            pltpu.SMEM((sizes.shape[0] + 1,), jnp.int32),
            pltpu.VMEM((fold, width), jnp.float32),
            pltpu.SemaphoreType.DMA((groups,)),
        ],
        compiler_params=pltpu.CompilerParams(vmem_limit_bytes=8 * MIB),
        cost_estimate=NOTHING,
        name="first_spread",
    )(sizes, pair, folded, pltpu.with_memory_space_constraint(fock, pltpu.HBM))


def spread_kernel(slot, folded, ranges, before, dense, turned):
    place_panel(slot, folded, ranges, dense, turned)


def spread(slot, folded, ranges, dense):
    fold = folded.shape[1]
    width = rounded(folded.shape[0], LANES)
    vmem = pl.BlockSpec(memory_space=pltpu.VMEM)
    pinned = [pltpu.with_memory_space_constraint(x, pltpu.VMEM) for x in (ranges, dense)]
    return pl.pallas_call(
        functools.partial(spread_kernel, slot),
        out_shape=pltpu.VMEM(dense.shape, dense.dtype),
        in_specs=[vmem, vmem, pl.BlockSpec(memory_space=pl.ANY)],
        out_specs=vmem,
        input_output_aliases={2: 0},
        scratch_shapes=[pltpu.VMEM((fold, width), jnp.float32)],
        compiler_params=pltpu.CompilerParams(vmem_limit_bytes=8 * MIB),
        cost_estimate=NOTHING,
        name="spread_panel",
    )(folded, *pinned)


def after(array, *others):
    anywhere = pl.BlockSpec(memory_space=pl.ANY)
    return pl.pallas_call(
        lambda *refs: None,
        out_shape=jax.ShapeDtypeStruct(array.shape, array.dtype),
        in_specs=[anywhere] * (1 + len(others)),
        out_specs=anywhere,
        input_output_aliases={0: 0},
        compiler_params=pltpu.CompilerParams(vmem_limit_bytes=MIB),
        cost_estimate=NOTHING,
        name="after",
    )(array, *others)


def owned_kernel(members, received, kept, *refs):
    out, sem = refs[-2:]

    @pl.when(lax.div(lax.axis_index("blk"), members) == lax.axis_index("grp"))
    def _():
        copy = pltpu.make_async_copy(kept, out, sem)
        copy.start()
        copy.wait()


def owned(received, kept, members, *others):
    anywhere = pl.BlockSpec(memory_space=pl.ANY)
    return pl.pallas_call(
        functools.partial(owned_kernel, members),
        out_shape=jax.ShapeDtypeStruct(received.shape, received.dtype),
        in_specs=[anywhere] * (2 + len(others)),
        out_specs=anywhere,
        input_output_aliases={0: 0},
        scratch_shapes=[pltpu.SemaphoreType.DMA],
        compiler_params=pltpu.CompilerParams(vmem_limit_bytes=MIB),
        cost_estimate=NOTHING,
        name="owned_rows",
    )(received, kept, *others)


def column_tiles(total, tile):
    return [(first, min(tile, total - first)) for first in range(0, total, tile)]


def dress_kernel(job, amplitudes, dense, fock, *refs):
    columns, spans, rows, members, has_sums, has_base, signed = job
    if has_sums:
        sums, refs = refs[0], refs[1:]
    refs = refs[has_base:]
    result, refs = refs[0], refs[1:]
    if signed:
        refs[0][...] = jnp.zeros_like(refs[0])
        refs = refs[1:]
    virtuals = dense.shape[0]
    begin, end = columns
    coupled = refs[0]
    for first, tile in column_tiles(end - begin, 1024):
        coupled[:, first:first + tile] = jnp.dot(
            amplitudes[...], dense[:, begin + first:begin + first + tile],
            preferred_element_type=jnp.float32,
        ).astype(coupled.dtype)
    if spans:
        dressed, sems = refs[1:]
        block = lax.axis_index("blk")
        places = [
            pl.multiple_of(lax.rem(block + by, members) * rows + offset, SUBLANES)
            for by, offset, _ in spans
        ]
    copies = []
    for t, (first, tile) in enumerate(column_tiles(virtuals, 640)):
        here = slice(first, first + tile)
        total = jnp.dot(
            coupled[...], fock[begin:end, here], preferred_element_type=jnp.float32
        )
        if has_sums:
            total = total + sums[:, here]
        if not spans:
            result[:, here] = total
            continue
        dressed[:, here] = total.astype(dressed.dtype)
        top = 0
        for p, (_, _, size) in enumerate(spans):
            copies.append(pltpu.make_async_copy(
                dressed.at[pl.ds(top, size), pl.ds(first, tile)],
                result.at[pl.ds(places[p], size), pl.ds(first, tile)],
                sems.at[p, t],
            ))
            copies[-1].start()
            top += size
    for copy in copies:
        copy.wait()


def dress(amplitudes, dense, fock, *, columns=None, sums=None, spans=(), base=None, rows=0, members=1,
          out_rows=0, signed=False):
    height, virtuals = amplitudes.shape
    begin, end = columns or (0, dense.shape[1])
    vmem = pl.BlockSpec(memory_space=pltpu.VMEM)
    anywhere = pl.BlockSpec(memory_space=pl.ANY)
    pinned = [dense, fock] + ([] if sums is None else [sums])
    pinned = [pltpu.with_memory_space_constraint(x, pltpu.VMEM) for x in pinned]
    bases = [] if base is None else [base]
    scratch = [pltpu.VMEM((height, end - begin), amplitudes.dtype)]
    if spans:
        out_shape = [jax.ShapeDtypeStruct((out_rows, virtuals), amplitudes.dtype)]
        scratch += [
            pltpu.VMEM((height, virtuals), amplitudes.dtype),
            pltpu.SemaphoreType.DMA((len(spans), len(column_tiles(virtuals, 640)))),
        ]
    else:
        out_shape = [pltpu.VMEM((height, virtuals), jnp.float32)]
    job = ((begin, end), spans, rows, members, sums is not None, base is not None, signed)
    return pl.pallas_call(
        functools.partial(dress_kernel, job),
        out_shape=out_shape + [TOKEN] * signed,
        in_specs=[vmem] * (1 + len(pinned)) + [anywhere] * len(bases),
        out_specs=[anywhere if spans else vmem] + [vmem] * signed,
        input_output_aliases={} if base is None else {1 + len(pinned): 0},
        scratch_shapes=scratch,
        compiler_params=pltpu.CompilerParams(vmem_limit_bytes=16 * MIB),
        cost_estimate=NOTHING,
        name="dress_rows",
    )(amplitudes, *pinned, *bases)


def make_local(blocks, groups):
    members = blocks // groups
    axes = ("blk", "grp")

    def device(hi, lo, grp):
        return (hi * members + lo) * groups + grp

    everyone = [(h, l, g) for h in range(groups) for l in range(members) for g in range(groups)]

    if groups == 4:
        copies = ((None, 0, 3, 1), (0, None, 1, 3), (0, 2, None, 3), (2, 0, 3, None))
    else:
        copies = [[None if h == g else h for h in range(groups)] for g in range(groups)]
    to_group = [
        (device(g, l, copies[g][h]), device(h, l, g)) for h, l, g in everyone if h != g
    ]

    def to_member(by):
        return [(device(h, (l + by) % members, g), device(h, l, g)) for h, l, g in everyone]

    def to_slot(slot):
        return [(device(h, l, g ^ slot), device(h, l, g)) for h, l, g in everyone]

    def local(amplitudes, hole_panel, virt_fock, irrep_sizes, pair_irreps):
        rows, virtuals = amplitudes.shape
        out_rows = rows * members
        fold = rounded(virtuals // 4, LANES)
        panel = jnp.swapaxes(hole_panel[:, 0, :], 0, 1)
        irrep_sizes = pltpu.with_memory_space_constraint(irrep_sizes, pltpu.HBM)

        early = rounded(rows * 2 // 3, SUBLANES) if rows % SUBLANES == 0 else 0
        if early:
            amplitudes = pltpu.with_memory_space_constraint(amplitudes, pltpu.HBM)
            top = cut(amplitudes, early)
        else:
            top = amplitudes
        own, own_again, *low = fold_panel(panel, irrep_sizes, pair_irreps, fold, amplitudes, early)
        across = lax.ppermute(own, axes, to_slot(2))
        beside = lax.ppermute(own_again, axes, to_slot(1))
        if early:
            low = low[0]
            swapped = [lax.ppermute(low, axes, to_member(by)) for by in range(1, members)]

        dense, fock, ranges, token = first_spread(groups, own, virt_fock, irrep_sizes, pair_irreps)
        top = owned(lax.ppermute(top, axes, to_group), top, members, token)
        if early:
            lows = jnp.concatenate([after(piece, top) for piece in [low] + swapped])
            late = lax.ppermute(lows, axes, to_group)
        tops = [top] + [lax.ppermute(top, axes, to_member(by)) for by in range(1, members)]
        dense = spread(1, beside, ranges, dense)
        near = 2 * dense.shape[1] // groups
        if early:
            sums, token = dress(top, dense, fock, columns=(0, near), signed=True)
            across = after(across, token)
        both = lax.ppermute(across, axes, to_slot(1))
        dense = spread(2, across, ranges, dense)
        dense = spread(3, both, ranges, dense)

        if early:
            place = dict(rows=rows, members=members, out_rows=out_rows)
            result, = dress(
                top, dense, fock, columns=(near, dense.shape[1]), sums=sums, spans=((0, 0, early),),
                **place,
            )
            for by in range(1, members):
                result, *token = dress(
                    tops[by], dense, fock, spans=((by, 0, early),), base=result,
                    signed=by == members - 1, **place,
                )
            lows = owned(late, lows, members, *token)
            spans = tuple((by, early, rows - early) for by in range(members))
            result, = dress(lows, dense, fock, spans=spans, base=result, **place)
        else:
            member = lax.axis_index("blk") % members
            ordered = jnp.roll(jnp.stack(tops), member, axis=0).reshape(out_rows, virtuals)
            result, = dress(ordered, dense, fock, spans=((0, 0, out_rows),), out_rows=out_rows)
        return result[:, None, :]

    return local


def solution(mesh):
    in_specs = (P("blk", None), P(None, "blk", "grp"), P(), P(), P("blk"))
    out_specs = P("grp", "blk", None)
    local = make_local(mesh.shape["blk"], mesh.shape["grp"])
    return jax.shard_map(local, mesh=mesh, in_specs=in_specs, out_specs=out_specs, check_vma=False)
```
